32 devices in a mesh: dom: 8 (over y, x, core), edge: 4 (over z).
Axes of the slice: x: 2, y: 2, z: 4, core: 2. Of those that a mesh axis runs over, the one named last changes fastest.
Arguments:
- edges: bfloat16 [32768, 512], P(('dom', 'edge')), may hold values from -6 to 6
- atoms: bfloat16 [1024, 256], P(('dom', 'edge')), may hold values from -6 to 6
- reverse: int32 [32768], P(('dom', 'edge')), may hold values from 0 to 32767, as said below
- atom_index: int32 [2, 32768], P(None, ('dom', 'edge')), may hold values from 0 to 127
- tile_source: int32 [512, 2], P(('dom', 'edge')), may hold values from 0 to 63
- tiles: bfloat16 [512, 64, 128], P(('dom', 'edge')), may hold values from -1 to 1
- weight_edge: bfloat16 [512, 512], replicated, may hold values from -0.25 to 0.25
- weight_down: bfloat16 [64, 512], replicated, may hold values from -0.25 to 0.25
- weight_up: bfloat16 [2, 64, 512], replicated, may hold values from -0.75 to 0.75
- weight_residual: bfloat16 [1, 2, 512, 512], replicated, may hold values from -0.25 to 0.25
- weight_message: bfloat16 [512, 256], replicated, may hold values from -0.25 to 0.25
- weight_atom: bfloat16 [2, 256, 256], replicated, may hold values from -0.375 to 0.375
- weight_join: bfloat16 [1024, 512], replicated, may hold values from -0.1875 to 0.1875
Outputs:
- new_edges: bfloat16 [32768, 512], P(('dom', 'edge'))
- new_atoms: bfloat16 [1024, 256], P(('dom', 'edge'))
The draws below stay inside these ranges and needn't reach their ends.
Inputs may be any that keep to these rules, and one draw needn't show every extreme that they name: reverse is an involution without fixed points. The reverse of a row lies on a device of the same edge index. Besides its own partition, the rows of each partition have their reverses in exactly 4 other partitions; at most 128 rows of one device have their reverses in any one other partition, and some device reaches 128.
All inputs are finite; a program needn't handle non-finite values.
Results may differ from the reference program's by a relative error of at most 0.015.
Values may be sent and summed in bfloat16 or wider, within the bound.
No kernel may reach another device: no remote copies, remote signals or barrier semaphores. Data moves between devices by JAX's collectives and lax.ppermute only.
A program may use at most 64 MiB of HBM per device.

```python
import jax
import jax.numpy as jnp

D = 512
DA = 256
TR = 64
BLK = 64
K = 2
EPA = 32
NRES = 1
E_DEV = 1024
NNB = 4
CAP = 128
A_PART = 128
ATOMS = 1024
TOTAL_E = 32768
NB_PART = 64
NB_TOTAL = 512
N_DOM = 8
N_EDGE = 4


def draw_reverse(key, part):
    key_list = jax.random.split(jax.random.fold_in(key, 11), 4)
    relabel = jax.random.permutation(key_list[0], N_DOM).astype(jnp.int32)
    inverse = jnp.argsort(relabel).astype(jnp.int32)
    totals = 2 * jax.random.permutation(key_list[1], N_DOM // 2)[:NNB].astype(jnp.int32) + 1
    partner = inverse[(totals[None, :] - relabel[:, None]) % N_DOM]
    lesser = jnp.minimum(jnp.arange(N_DOM, dtype=jnp.int32)[:, None], partner)
    count_table = 2 * jax.random.randint(key_list[2], (NNB, N_DOM, N_EDGE), 3 * CAP // 8, CAP // 2 + 1, dtype=jnp.int32)
    count_table = count_table.at[0, 0, 0].set(CAP)
    counts = count_table[jnp.arange(NNB, dtype=jnp.int32)[None, :], lesser, :]
    canonical = jnp.arange(E_DEV, dtype=jnp.int32)
    region = canonical // CAP
    within = canonical % CAP
    region_cap = jnp.minimum(region, NNB - 1)
    domain_ids = jnp.arange(N_DOM, dtype=jnp.int32)[:, None, None]
    edge_ids = jnp.arange(N_EDGE, dtype=jnp.int32)[None, :, None]
    limits = counts[domain_ids, region_cap[None, None, :], edge_ids]
    is_cross = (region[None, None, :] < NNB) & (within[None, None, :] < limits)
    far_domain = partner[domain_ids, region_cap[None, None, :]]
    target_dom = jnp.where(is_cross, far_domain, domain_ids)
    target_canon = jnp.where(is_cross, canonical[None, None, :], jnp.bitwise_xor(canonical, 1)[None, None, :])
    device_keys = jax.random.split(key_list[3], N_DOM * N_EDGE)
    shuffle = jax.vmap(lambda single: jax.random.permutation(single, E_DEV))(device_keys).astype(jnp.int32)
    shuffle = shuffle.reshape(N_DOM, N_EDGE, E_DEV)
    unshuffle = jnp.argsort(shuffle, axis=-1).astype(jnp.int32)
    target_edge = jnp.broadcast_to(edge_ids, target_dom.shape)
    target_pos = shuffle[target_dom, target_edge, target_canon]
    target_global = (target_dom * N_EDGE + target_edge) * E_DEV + target_pos
    result = jnp.take_along_axis(target_global, unshuffle, axis=-1)
    return result.reshape(-1).astype(jnp.int32)


def with_ends(array, key, low, largest):
    longest = array.shape.index(max(array.shape))
    spots = []
    for shift in (0, 1):
        where = [jax.random.randint(jax.random.fold_in(key, axis), (), 0, length) for axis, length in enumerate(array.shape)]
        where[longest] = (where[longest] + shift) % array.shape[longest]
        spots.append(tuple(where))
    return array.at[spots[0]].set(low).at[spots[1]].set(largest)


def block_levels(key, dims, pieces, least, high):
    level, own = 1.0, jax.random.fold_in(key, 6)
    for axis_at, blocks in pieces:
        steps = jnp.exp(jax.random.uniform(jax.random.fold_in(own, axis_at), (blocks,), jnp.float32, least / len(pieces), high / len(pieces)))
        level = level * jnp.repeat(steps, dims[axis_at] // blocks).reshape([-1 if axis == axis_at else 1 for axis in range(len(dims))])
    return level


def noise(stream_key, extent, deviation, most, cuts=(), kind=jnp.bfloat16):
    drawn = jax.random.normal(stream_key, extent, jnp.float32) * deviation
    if len(cuts) > 0:
        drawn = block_levels(stream_key, extent, cuts, -0.22, 0.18) * drawn
    return jnp.clip(drawn, min=-most, max=most).astype(kind)


def setup_inputs(seed: int = 0) -> dict:
    streams_of = jax.random.split(jax.random.key(seed), 14)
    return {
        "edges": noise(streams_of[0], (TOTAL_E, D), 1.0, 6.0, ((0, 32),)),
        "atoms": noise(streams_of[1], (ATOMS, DA), 1.0, 6.0, ((0, 32),)),
        "reverse": draw_reverse(jax.random.fold_in(streams_of[13], 71), 0),
        "atom_index": with_ends(jax.random.randint(streams_of[3], (2, TOTAL_E), 0, A_PART), jax.random.fold_in(streams_of[3], 1), 0, A_PART - 1).astype(jnp.int32),
        "tile_source": with_ends(jax.random.randint(streams_of[4], (NB_TOTAL, K), 0, NB_PART), jax.random.fold_in(streams_of[4], 1), 0, NB_PART - 1).astype(jnp.int32),
        "tiles": noise(streams_of[5], (NB_TOTAL, BLK, K * BLK), (K * BLK // 4) ** -0.5, 1.0, ((0, 32),)),
        "weight_edge": noise(streams_of[6], (D, D), D ** -0.5, 0.25),
        "weight_down": noise(streams_of[7], (TR, D), D ** -0.5, 0.25),
        "weight_up": noise(streams_of[8], (2, TR, D), TR ** -0.5, 0.75),
        "weight_residual": noise(streams_of[9], (NRES, 2, D, D), D ** -0.5, 0.25),
        "weight_message": noise(streams_of[10], (D, DA), D ** -0.5, 0.25),
        "weight_atom": noise(streams_of[11], (2, DA, DA), DA ** -0.5, 0.375),
        "weight_join": noise(streams_of[12], (2 * DA + D, D), (2 * DA + D) ** -0.5, 0.1875),
    }


root_half = 0.7071067811865476


def reference(edges, atoms, reverse, atom_index, tile_source, tiles, weight_edge, weight_down, weight_up, weight_residual, weight_message, weight_atom, weight_join):
    hidden = jax.nn.silu(jnp.dot(edges, weight_edge, preferred_element_type=jnp.float32)).astype(jnp.bfloat16)
    narrow = jax.nn.silu(jnp.dot(hidden, weight_down.T, preferred_element_type=jnp.float32)).astype(jnp.bfloat16)
    blocks = narrow.reshape(NB_TOTAL, BLK, TR)
    owners = (jnp.arange(NB_TOTAL, dtype=jnp.int32) // NB_PART) * NB_PART
    source = owners[:, None] + tile_source
    picked = blocks[source].astype(jnp.float32)
    shaped = tiles.reshape(NB_TOTAL, BLK, K, BLK).astype(jnp.float32)
    mixed = jnp.einsum("bekj,bkjt->bet", shaped, picked)
    trip_out = mixed.reshape(TOTAL_E, TR).astype(jnp.bfloat16)
    swapped = jnp.dot(trip_out, weight_up[1], preferred_element_type=jnp.float32).astype(jnp.bfloat16)
    direct = jnp.dot(trip_out, weight_up[0], preferred_element_type=jnp.float32)
    joined = (direct + swapped[reverse].astype(jnp.float32)) * root_half
    edge_state = (edges.astype(jnp.float32) + joined).astype(jnp.bfloat16)
    for layer_index in range(NRES):
        middle = jax.nn.silu(jnp.dot(edge_state, weight_residual[layer_index, 0], preferred_element_type=jnp.float32)).astype(jnp.bfloat16)
        branch = jax.nn.silu(jnp.dot(middle, weight_residual[layer_index, 1], preferred_element_type=jnp.float32))
        edge_state = ((edge_state.astype(jnp.float32) + branch) * root_half).astype(jnp.bfloat16)
    message = jnp.dot(edge_state, weight_message, preferred_element_type=jnp.float32).astype(jnp.bfloat16)
    partition = jnp.arange(TOTAL_E, dtype=jnp.int32) // (E_DEV * N_EDGE)
    target = partition * A_PART + atom_index[1]
    source_atom = partition * A_PART + atom_index[0]
    atom_sums = jax.ops.segment_sum(message.astype(jnp.float32), target, num_segments=ATOMS)
    scaled = (atom_sums * (EPA ** -0.5)).astype(jnp.bfloat16)
    atom_middle = jax.nn.silu(jnp.dot(scaled, weight_atom[0], preferred_element_type=jnp.float32)).astype(jnp.bfloat16)
    new_atoms = (atoms.astype(jnp.float32) + jnp.dot(atom_middle, weight_atom[1], preferred_element_type=jnp.float32)).astype(jnp.bfloat16)
    gathered = jnp.concatenate([new_atoms[source_atom], new_atoms[target], edge_state], axis=1)
    update = jax.nn.silu(jnp.dot(gathered, weight_join, preferred_element_type=jnp.float32))
    new_edges = ((edge_state.astype(jnp.float32) + update) * root_half).astype(jnp.bfloat16)
    return new_edges, new_atoms
```

```python
import functools

import jax
import jax.numpy as jnp
from jax import lax
from jax.experimental import pallas as pl
from jax.experimental.pallas import tpu as pltpu
from jax.sharding import PartitionSpec as P

root_half = 0.7071067811865476
MIB = 1 << 20
CHUNK = 256


def product(operand, weights):
    return jnp.dot(operand, weights, preferred_element_type=jnp.float32)


def silu(value):
    halved = 0.5 * value
    return halved + halved * jnp.tanh(halved)


def as_column(row):
    wide = jnp.broadcast_to(row.astype(jnp.float32), (8, row.shape[1]))
    return jnp.transpose(wide)[:, :1].astype(jnp.int32)


def row_chunks(rows):
    step = min(CHUNK, rows)
    return [slice(at, at + step) for at in range(0, rows, step)]


def call(kernel, outs, args, *, smem=(), scratch=(), flops=0, nbytes=0, limit=24):
    in_specs = [
        pl.BlockSpec(memory_space=pltpu.SMEM if at in smem else pltpu.VMEM)
        for at in range(len(args))
    ]
    return pl.pallas_call(
        kernel,
        out_shape=outs,
        in_specs=in_specs,
        out_specs=jax.tree.map(lambda _: pl.BlockSpec(memory_space=pltpu.VMEM), outs),
        scratch_shapes=list(scratch),
        compiler_params=pltpu.CompilerParams(vmem_limit_bytes=limit * MIB),
        cost_estimate=pl.CostEstimate(flops=flops, bytes_accessed=nbytes, transcendentals=0),
    )(*args)


def shaped(shape, dtype=jnp.bfloat16):
    return jax.ShapeDtypeStruct(shape, dtype)


def narrow_kernel(edges_ref, weight_ref, down_ref, out_ref):
    half = edges_ref.shape[0] // 2
    for rows in row_chunks(half):
        pieces = []
        for base in (0, half):
            piece = edges_ref[base + rows.start : base + rows.stop, :]
            hidden = silu(product(piece, weight_ref[...])).astype(jnp.bfloat16)
            pieces.append(
                silu(
                    lax.dot_general(
                        hidden,
                        down_ref[...],
                        (((1,), (1,)), ((), ())),
                        preferred_element_type=jnp.float32,
                    )
                )
            )
        out_ref[rows, :] = jnp.concatenate(pieces, axis=1).astype(jnp.bfloat16)


def index_kernel(domains, shards, reverse_ref, send_ref, fetch_ref, local_ref):
    rows = reverse_ref.shape[1]
    capacity = rows // domains
    half = capacity // 2
    slots = (domains - 1) * capacity
    own = lax.axis_index("dom")
    reverse = reverse_ref[...]
    holder = reverse // (rows * shards)
    source_row = lax.rem(reverse, rows)
    partner = holder ^ own
    source_column = as_column(source_row)
    member = (lax.broadcasted_iota(jnp.int32, (domains, rows), 0) == partner).astype(jnp.bfloat16)
    before = (
        lax.broadcasted_iota(jnp.int32, (rows, rows), 0)
        < lax.broadcasted_iota(jnp.int32, (rows, rows), 1)
    ).astype(jnp.bfloat16)
    place = jnp.sum(
        product(member, before) * member.astype(jnp.float32), axis=0, keepdims=True
    ).astype(jnp.int32)
    earlier = (source_column < source_row).astype(jnp.bfloat16)
    far_place = jnp.sum(
        product(member, earlier) * member.astype(jnp.float32), axis=0, keepdims=True
    ).astype(jnp.int32)

    def slot_of(at):
        part = (at >= half).astype(jnp.int32)
        slot = part * (slots // 2) + (partner - 1) * half + at - part * half
        return jnp.where(partner == 0, -1, slot)

    send_slot = slot_of(place)
    send_ref[...] = (
        lax.broadcasted_iota(jnp.int32, (slots, rows), 0) == send_slot
    ).astype(jnp.bfloat16)
    fetch_column = as_column(slot_of(far_place))
    fetch_ref[...] = (
        lax.broadcasted_iota(jnp.int32, (rows, slots), 1) == fetch_column
    ).astype(jnp.bfloat16)
    local_column = as_column(jnp.where(partner == 0, source_row, -1))
    local_ref[...] = (
        lax.broadcasted_iota(jnp.int32, (rows, rows), 1) == local_column
    ).astype(jnp.bfloat16)


def mix_kernel(shards, *refs):
    source_ref, tiles_ref = refs[:2]
    parts = refs[2 : 2 + shards]
    send_ref, trip_ref = refs[2 + shards : 4 + shards]
    out_refs = refs[4 + shards : -1]
    held_ref = refs[-1]
    blocks, block_len, width = tiles_ref.shape
    count = width // block_len
    lines = parts[0].shape[0]
    me = lax.axis_index("edge")
    for at in range(shards):
        held_ref[at * lines : (at + 1) * lines, :] = parts[at][...]
    half_blocks = blocks // 2
    channels = trip_ref.shape[1]
    for block in range(blocks):
        picks = []
        for tile in range(count):
            source = source_ref[block, tile]
            shard = source // blocks
            within = source - shard * blocks
            upper = within // half_blocks
            near = lax.rem(shard - me + shards, shards)
            start = near * lines + (within - upper * half_blocks) * block_len
            rows = held_ref[pl.ds(pl.multiple_of(start, block_len), block_len), :]
            picks.append(jnp.where(upper == 1, rows[:, channels:], rows[:, :channels]))
        mixed = product(tiles_ref[block], jnp.concatenate(picks, axis=0))
        trip_ref[block * block_len : (block + 1) * block_len, :] = mixed.astype(jnp.bfloat16)
    half_slots = send_ref.shape[0] // 2
    low = product(send_ref[:half_slots, :], trip_ref[...])
    high = product(send_ref[half_slots:, :], trip_ref[...])
    packed = jnp.concatenate([low, high], axis=1).astype(jnp.bfloat16)
    each = half_slots // len(out_refs)
    for at, out_ref in enumerate(out_refs):
        out_ref[...] = packed[at * each : (at + 1) * each, :]


def base_kernel(edges_ref, trip_ref, local_ref, up_ref, out_ref):
    channels = trip_ref.shape[1]
    for rows in row_chunks(edges_ref.shape[0]):
        picked = product(local_ref[rows, :], trip_ref[...]).astype(jnp.bfloat16)
        joined = product(trip_ref[rows, :], up_ref[0]) + product(picked, up_ref[1])
        out_ref[rows, :] = edges_ref[rows, :].astype(jnp.float32) + joined * root_half


def state_kernel(partners, *refs):
    base_ref, fetch_ref, up_ref, residual_ref, message_ref, index_ref = refs[:6]
    arrived = refs[6 : 6 + partners]
    state_ref, sums_ref, slots_ref = refs[6 + partners :]
    channels = up_ref.shape[1]
    each = arrived[0].shape[0]
    for at in range(partners):
        piece = arrived[at][...]
        slots_ref[at * each : (at + 1) * each, :] = piece[:, :channels]
        slots_ref[(partners + at) * each : (partners + at + 1) * each, :] = piece[:, channels:]
    for rows in row_chunks(base_ref.shape[0]):
        picked = product(fetch_ref[rows, :], slots_ref[...]).astype(jnp.bfloat16)
        state = (base_ref[rows, :] + product(picked, up_ref[1]) * root_half).astype(jnp.bfloat16)
        for layer in range(residual_ref.shape[0]):
            middle = silu(product(state, residual_ref[layer, 0])).astype(jnp.bfloat16)
            branch = silu(product(middle, residual_ref[layer, 1]))
            state = ((state.astype(jnp.float32) + branch) * root_half).astype(jnp.bfloat16)
        state_ref[rows, :] = state
    part_atoms = sums_ref.shape[0]
    shards = lax.axis_size("edge")
    near = near_atoms(index_ref[1:2, :], part_atoms, shards)
    chosen = (
        lax.broadcasted_iota(jnp.int32, (part_atoms, near.shape[1]), 0) == near
    ).astype(jnp.bfloat16)
    gathered = product(chosen, state_ref[...]).astype(jnp.bfloat16)
    sums_ref[...] = product(gathered, message_ref[...]).astype(jnp.bfloat16)


def near_atoms(index, part_atoms, shards):
    first = lax.axis_index("edge") * (part_atoms // shards)
    shifted = index - first
    return jnp.where(shifted < 0, shifted + part_atoms, shifted)


def side_kernel(shards, part_atoms, state_ref, join_ref, index_ref, out_ref, chosen_ref):
    width = join_ref.shape[0] - state_ref.shape[1]
    for rows in row_chunks(state_ref.shape[0]):
        out_ref[rows, :] = product(state_ref[rows, :], join_ref[width:, :])
    index = near_atoms(index_ref[...], part_atoms, shards)
    for end in range(2):
        column = as_column(index[end : end + 1, :])
        chosen_ref[:, end * part_atoms : (end + 1) * part_atoms] = (
            lax.broadcasted_iota(jnp.int32, (column.shape[0], part_atoms), 1) == column
        ).astype(jnp.bfloat16)


def final_kernel(shards, scale, *refs):
    sums = refs[:shards]
    atoms = refs[shards : 2 * shards]
    weight_ref, join_ref, state_ref, side_ref, chosen_ref = refs[2 * shards : 2 * shards + 5]
    edges_ref, own_ref, table_ref = refs[2 * shards + 5 :]
    count = atoms[0].shape[0]
    part_atoms = count * shards
    total = sums[0][...].astype(jnp.float32)
    for at in range(1, shards):
        piece = sums[at][...].astype(jnp.float32)
        cut = part_atoms - at * count
        total = total + jnp.concatenate([piece[cut:], piece[:cut]], axis=0)
    everyone = jnp.concatenate([ref[...].astype(jnp.float32) for ref in atoms], axis=0)
    scaled = (total * scale).astype(jnp.bfloat16)
    middle = silu(product(scaled, weight_ref[0])).astype(jnp.bfloat16)
    renewed = (everyone + product(middle, weight_ref[1])).astype(jnp.bfloat16)
    own_ref[...] = renewed[:count, :]
    width = renewed.shape[1]
    for end in range(2):
        table_ref[end * part_atoms : (end + 1) * part_atoms, :] = product(
            renewed, join_ref[end * width : (end + 1) * width, :]
        ).astype(jnp.bfloat16)
    for rows in row_chunks(state_ref.shape[0]):
        update = silu(product(chosen_ref[rows, :], table_ref[...]) + side_ref[rows, :])
        state = state_ref[rows, :].astype(jnp.float32)
        edges_ref[rows, :] = ((state + update) * root_half).astype(jnp.bfloat16)


def from_next(value, shards):
    return [
        lax.ppermute(value, "edge", [((at + by) % shards, at) for at in range(shards)])
        for by in range(1, shards)
    ]


def body(
    edges,
    atoms,
    reverse,
    atom_index,
    tile_source,
    tiles,
    weight_edge,
    weight_down,
    weight_up,
    weight_residual,
    weight_message,
    weight_atom,
    weight_join,
):
    rows, wide = edges.shape
    channels = weight_down.shape[0]
    domains = lax.axis_size("dom")
    shards = lax.axis_size("edge")
    count, atom_wide = atoms.shape
    part_atoms = count * shards
    capacity = rows // domains
    partners = domains - 1
    slots = partners * capacity
    packed = (rows // 2, 2 * channels)

    atom_parts = [atoms] + from_next(atoms, shards)
    narrow = call(
        narrow_kernel,
        shaped(packed),
        (edges, weight_edge, weight_down),
        flops=2 * rows * wide * (wide + channels),
        nbytes=2 * (rows * wide + wide * wide),
    )
    narrow_parts = [narrow] + from_next(narrow, shards)
    send, fetch, local = call(
        functools.partial(index_kernel, domains, shards),
        (shaped((slots, rows)), shaped((rows, slots)), shaped((rows, rows))),
        (reverse.reshape(1, rows),),
        flops=40 * rows * rows,
        nbytes=6 * rows * rows,
    )
    trip_out, *outgoing = call(
        functools.partial(mix_kernel, shards),
        (shaped((rows, channels)),) + (shaped((capacity // 2, 2 * channels)),) * partners,
        (tile_source, tiles, *narrow_parts, send),
        smem=(0,),
        scratch=[pltpu.VMEM((shards * rows // 2, 2 * channels), jnp.bfloat16)],
        flops=2 * rows * rows * channels,
        nbytes=2 * rows * rows,
    )
    arrived = [
        lax.ppermute(outgoing[by - 1], "dom", [(at, at ^ by) for at in range(domains)])
        for by in range(1, domains)
    ]
    base = call(
        base_kernel,
        shaped((rows, wide), jnp.float32),
        (edges, trip_out, local, weight_up),
        flops=2 * rows * channels * (rows + 2 * wide),
        nbytes=2 * rows * rows + 6 * rows * wide,
    )
    state, sums = call(
        functools.partial(state_kernel, partners),
        (shaped((rows, wide)), shaped((part_atoms, atom_wide))),
        (base, fetch, weight_up, weight_residual, weight_message, atom_index, *arrived),
        scratch=[pltpu.VMEM((slots, channels), jnp.bfloat16)],
        flops=4 * rows * wide * wide,
        nbytes=8 * rows * wide,
    )
    sums_parts = [sums] + from_next(sums, shards)
    side, chosen = call(
        functools.partial(side_kernel, shards, part_atoms),
        (shaped((rows, wide), jnp.float32), shaped((rows, 2 * part_atoms))),
        (state, weight_join, atom_index),
        flops=2 * rows * wide * wide,
        nbytes=8 * rows * wide,
    )
    return call(
        functools.partial(final_kernel, shards, (rows // count) ** -0.5),
        (shaped((rows, wide)), shaped((count, atom_wide))),
        (*sums_parts, *atom_parts, weight_atom, weight_join, state, side, chosen),
        scratch=[pltpu.VMEM((2 * part_atoms, wide), jnp.bfloat16)],
        flops=4 * rows * part_atoms * wide,
        nbytes=8 * rows * wide,
    )


def solution(mesh):
    split = P(("dom", "edge"))
    placed = (
        P(("dom", "edge"), None),
        P(("dom", "edge"), None),
        split,
        P(None, ("dom", "edge")),
        P(("dom", "edge"), None),
        P(("dom", "edge"), None, None),
    ) + (P(),) * 7
    return jax.shard_map(
        body,
        mesh=mesh,
        in_specs=placed,
        out_specs=(P(("dom", "edge"), None), P(("dom", "edge"), None)),
        check_vma=False,
    )
```

```python
import functools

import jax
import jax.numpy as jnp
from jax import lax
from jax.experimental import pallas as pl
from jax.experimental.pallas import tpu as pltpu
from jax.sharding import PartitionSpec as P

root_half = 0.7071067811865476
MIB = 1 << 20
CHUNK = 256


def product(operand, weights):
    return jnp.dot(operand, weights, preferred_element_type=jnp.float32)


def silu(value):
    halved = 0.5 * value
    return halved + halved * jnp.tanh(halved)


def as_column(row):
    wide = jnp.broadcast_to(row.astype(jnp.float32), (8, row.shape[1]))
    return jnp.transpose(wide)[:, :1].astype(jnp.int32)


def row_chunks(rows):
    step = min(CHUNK, rows)
    return [slice(at, at + step) for at in range(0, rows, step)]


def call(kernel, outs, args, *, smem=(), hbm=(), scratch=(), flops=0, nbytes=0, limit=24):
    def space(at):
        return pltpu.SMEM if at in smem else pltpu.HBM if at in hbm else pltpu.VMEM

    in_specs = [pl.BlockSpec(memory_space=space(at)) for at in range(len(args))]
    args = [
        pltpu.with_memory_space_constraint(arg, pltpu.HBM) if at in hbm else arg
        for at, arg in enumerate(args)
    ]
    return pl.pallas_call(
        kernel,
        out_shape=outs,
        in_specs=in_specs,
        out_specs=jax.tree.map(lambda _: pl.BlockSpec(memory_space=pltpu.VMEM), outs),
        scratch_shapes=list(scratch),
        compiler_params=pltpu.CompilerParams(vmem_limit_bytes=limit * MIB),
        cost_estimate=pl.CostEstimate(flops=flops, bytes_accessed=nbytes, transcendentals=0),
    )(*args)


def shaped(shape, dtype=jnp.bfloat16):
    return jax.ShapeDtypeStruct(shape, dtype)


def narrow_kernel(
    edges_hbm, weight_hbm, down_hbm, atoms_ref, out_ref, edges_ref, weight_ref, down_ref, sems
):
    half = edges_hbm.shape[0] // 2
    pieces = [
        slice(base + rows.start, base + rows.stop)
        for rows in row_chunks(half)
        for base in (0, half)
    ]
    copies = [
        pltpu.make_async_copy(weight_hbm, weight_ref, sems.at[0]),
        pltpu.make_async_copy(down_hbm, down_ref, sems.at[1]),
    ] + [
        pltpu.make_async_copy(edges_hbm.at[piece], edges_ref.at[piece], sems.at[2 + at])
        for at, piece in enumerate(pieces)
    ]
    for copy in [copies[0], copies[2], copies[1]] + copies[3:]:
        copy.start()
    count, wide = atoms_ref.shape
    for at in range(wide // 128):
        out_ref[half + at * count : half + (at + 1) * count, :] = atoms_ref[
            :, at * 128 : (at + 1) * 128
        ]
    copies[0].wait()
    copies[1].wait()
    for at, rows in enumerate(row_chunks(half)):
        sides = []
        for side in range(2):
            copies[2 + 2 * at + side].wait()
            hidden = silu(product(edges_ref[pieces[2 * at + side], :], weight_ref[...]))
            sides.append(
                silu(
                    lax.dot_general(
                        hidden.astype(jnp.bfloat16),
                        down_ref[...],
                        (((1,), (1,)), ((), ())),
                        preferred_element_type=jnp.float32,
                    )
                )
            )
        out_ref[rows, :] = jnp.concatenate(sides, axis=1).astype(jnp.bfloat16)


def index_kernel(domains, shards, reverse_ref, send_ref, fetch_ref, local_ref):
    rows = reverse_ref.shape[1]
    capacity = rows // domains
    half = capacity // 2
    slots = domains * capacity
    own = lax.axis_index("dom")
    reverse = reverse_ref[...]
    holder = reverse // (rows * shards)
    source_row = lax.rem(reverse, rows)
    source_column = as_column(source_row)
    member = (lax.broadcasted_iota(jnp.int32, (domains, rows), 0) == holder).astype(jnp.bfloat16)
    before = (
        lax.broadcasted_iota(jnp.int32, (rows, rows), 0)
        < lax.broadcasted_iota(jnp.int32, (rows, rows), 1)
    ).astype(jnp.bfloat16)
    place = jnp.sum(
        product(member, before) * member.astype(jnp.float32), axis=0, keepdims=True
    ).astype(jnp.int32)
    earlier = (source_column < source_row).astype(jnp.bfloat16)
    far_place = jnp.sum(
        product(member, earlier) * member.astype(jnp.float32), axis=0, keepdims=True
    ).astype(jnp.int32)

    def slot_of(at):
        part = (at >= half).astype(jnp.int32)
        slot = part * (slots // 2) + holder * half + at - part * half
        return jnp.where(holder == own, -1, slot)

    send_slot = slot_of(place)
    send_ref[...] = (
        lax.broadcasted_iota(jnp.int32, (slots, rows), 0) == send_slot
    ).astype(jnp.bfloat16)
    fetch_column = as_column(slot_of(far_place))
    fetch_ref[...] = (
        lax.broadcasted_iota(jnp.int32, (rows, slots), 1) == fetch_column
    ).astype(jnp.bfloat16)
    local_column = as_column(jnp.where(holder == own, source_row, -1))
    local_ref[...] = (
        lax.broadcasted_iota(jnp.int32, (rows, rows), 1) == local_column
    ).astype(jnp.bfloat16)


def mix_kernel(shards, *refs):
    source_ref, tiles_ref = refs[:2]
    parts = refs[2 : 2 + shards]
    send_ref, trip_ref, out_ref, atoms_ref, held_ref = refs[2 + shards :]
    blocks, block_len, width = tiles_ref.shape
    count = width // block_len
    lines = held_ref.shape[0] // shards
    part_atoms, atom_wide = atoms_ref.shape
    near_atoms = part_atoms // shards
    me = lax.axis_index("edge")
    for at in range(shards):
        held_ref[at * lines : (at + 1) * lines, :] = parts[at][:lines, :]
        for piece in range(atom_wide // 128):
            start = lines + piece * near_atoms
            atoms_ref[
                at * near_atoms : (at + 1) * near_atoms, piece * 128 : (piece + 1) * 128
            ] = parts[at][start : start + near_atoms, :]
    half_blocks = blocks // 2
    channels = trip_ref.shape[1]
    for block in range(blocks):
        picks = []
        for tile in range(count):
            source = source_ref[block, tile]
            shard = source // blocks
            within = source - shard * blocks
            upper = within // half_blocks
            near = lax.rem(shard - me + shards, shards)
            start = near * lines + (within - upper * half_blocks) * block_len
            rows = held_ref[pl.ds(pl.multiple_of(start, block_len), block_len), :]
            picks.append(jnp.where(upper == 1, rows[:, channels:], rows[:, :channels]))
        mixed = product(tiles_ref[block], jnp.concatenate(picks, axis=0))
        trip_ref[block * block_len : (block + 1) * block_len, :] = mixed.astype(jnp.bfloat16)
    half_slots = send_ref.shape[0] // 2
    low = product(send_ref[:half_slots, :], trip_ref[...])
    high = product(send_ref[half_slots:, :], trip_ref[...])
    out_ref[...] = jnp.concatenate([low, high], axis=1).astype(jnp.bfloat16)


def base_kernel(edges_ref, trip_ref, local_ref, up_ref, out_ref):
    channels = trip_ref.shape[1]
    for rows in row_chunks(edges_ref.shape[0]):
        picked = product(local_ref[rows, :], trip_ref[...]).astype(jnp.bfloat16)
        joined = product(trip_ref[rows, :], up_ref[0]) + product(picked, up_ref[1])
        out_ref[rows, :] = edges_ref[rows, :].astype(jnp.float32) + joined * root_half


def state_kernel(
    base_ref, fetch_ref, up_ref, residual_ref, message_ref, index_ref, arrived_ref,
    state_ref, sums_ref, slots_ref,
):
    channels = up_ref.shape[1]
    half = arrived_ref.shape[0]
    slots_ref[:half, :] = arrived_ref[:, :channels]
    slots_ref[half:, :] = arrived_ref[:, channels:]
    for rows in row_chunks(base_ref.shape[0]):
        picked = product(fetch_ref[rows, :], slots_ref[...]).astype(jnp.bfloat16)
        state = (base_ref[rows, :] + product(picked, up_ref[1]) * root_half).astype(jnp.bfloat16)
        for layer in range(residual_ref.shape[0]):
            middle = silu(product(state, residual_ref[layer, 0])).astype(jnp.bfloat16)
            branch = silu(product(middle, residual_ref[layer, 1]))
            state = ((state.astype(jnp.float32) + branch) * root_half).astype(jnp.bfloat16)
        state_ref[rows, :] = state
    part_atoms = sums_ref.shape[0]
    shards = lax.axis_size("edge")
    near = near_atoms(index_ref[1:2, :], part_atoms, shards)
    chosen = (
        lax.broadcasted_iota(jnp.int32, (part_atoms, near.shape[1]), 0) == near
    ).astype(jnp.bfloat16)
    gathered = product(chosen, state_ref[...]).astype(jnp.bfloat16)
    sums_ref[...] = product(gathered, message_ref[...]).astype(jnp.bfloat16)


def near_atoms(index, part_atoms, shards):
    first = lax.axis_index("edge") * (part_atoms // shards)
    shifted = index - first
    return jnp.where(shifted < 0, shifted + part_atoms, shifted)


def side_kernel(shards, part_atoms, state_ref, join_ref, index_ref, out_ref, chosen_ref):
    width = join_ref.shape[0] - state_ref.shape[1]
    for rows in row_chunks(state_ref.shape[0]):
        out_ref[rows, :] = product(state_ref[rows, :], join_ref[width:, :])
    index = near_atoms(index_ref[...], part_atoms, shards)
    for end in range(2):
        column = as_column(index[end : end + 1, :])
        chosen_ref[:, end * part_atoms : (end + 1) * part_atoms] = (
            lax.broadcasted_iota(jnp.int32, (column.shape[0], part_atoms), 1) == column
        ).astype(jnp.bfloat16)


def final_kernel(shards, scale, *refs):
    sums = refs[:shards]
    atoms_ref, weight_ref, join_ref, state_ref, side_ref, chosen_ref = refs[shards : shards + 6]
    edges_ref, own_ref, table_ref = refs[shards + 6 :]
    part_atoms = atoms_ref.shape[0]
    count = part_atoms // shards
    total = sums[0][...].astype(jnp.float32)
    for at in range(1, shards):
        piece = sums[at][...].astype(jnp.float32)
        cut = part_atoms - at * count
        total = total + jnp.concatenate([piece[cut:], piece[:cut]], axis=0)
    scaled = (total * scale).astype(jnp.bfloat16)
    middle = silu(product(scaled, weight_ref[0])).astype(jnp.bfloat16)
    renewed = (atoms_ref[...].astype(jnp.float32) + product(middle, weight_ref[1])).astype(jnp.bfloat16)
    own_ref[...] = renewed[:count, :]
    width = renewed.shape[1]
    for end in range(2):
        table_ref[end * part_atoms : (end + 1) * part_atoms, :] = product(
            renewed, join_ref[end * width : (end + 1) * width, :]
        ).astype(jnp.bfloat16)
    for rows in row_chunks(state_ref.shape[0]):
        update = silu(product(chosen_ref[rows, :], table_ref[...]) + side_ref[rows, :])
        state = state_ref[rows, :].astype(jnp.float32)
        edges_ref[rows, :] = ((state + update) * root_half).astype(jnp.bfloat16)


def from_next(value, shards):
    return [
        lax.ppermute(value, "edge", [((at + by) % shards, at) for at in range(shards)])
        for by in range(1, shards)
    ]


def body(
    edges,
    atoms,
    reverse,
    atom_index,
    tile_source,
    tiles,
    weight_edge,
    weight_down,
    weight_up,
    weight_residual,
    weight_message,
    weight_atom,
    weight_join,
):
    rows, wide = edges.shape
    channels = weight_down.shape[0]
    domains = lax.axis_size("dom")
    shards = lax.axis_size("edge")
    count, atom_wide = atoms.shape
    part_atoms = count * shards
    lines = rows // 2
    packed = 2 * channels

    narrow = call(
        narrow_kernel,
        shaped((lines + count * atom_wide // packed, packed)),
        (edges, weight_edge, weight_down, atoms),
        hbm=(0, 1, 2),
        scratch=[
            pltpu.VMEM(edges.shape, jnp.bfloat16),
            pltpu.VMEM(weight_edge.shape, jnp.bfloat16),
            pltpu.VMEM(weight_down.shape, jnp.bfloat16),
            pltpu.SemaphoreType.DMA((2 + 2 * len(row_chunks(lines)),)),
        ],
        flops=2 * rows * wide * (wide + channels),
        nbytes=2 * (rows * wide + wide * wide),
    )
    narrow_parts = [narrow] + from_next(narrow, shards)
    send, fetch, local = call(
        functools.partial(index_kernel, domains, shards),
        (shaped((rows, rows)),) * 3,
        (reverse.reshape(1, rows),),
        flops=40 * rows * rows,
        nbytes=6 * rows * rows,
    )
    trip_out, outgoing, all_atoms = call(
        functools.partial(mix_kernel, shards),
        (
            shaped((rows, channels)),
            shaped((lines, packed)),
            shaped((part_atoms, atom_wide)),
        ),
        (tile_source, tiles, *narrow_parts, send),
        smem=(0,),
        scratch=[pltpu.VMEM((shards * lines, packed), jnp.bfloat16)],
        flops=2 * rows * rows * channels,
        nbytes=2 * rows * rows,
    )
    arrived = lax.all_to_all(outgoing, "dom", split_axis=0, concat_axis=0, tiled=True)
    base = call(
        base_kernel,
        shaped((rows, wide), jnp.float32),
        (edges, trip_out, local, weight_up),
        flops=2 * rows * channels * (rows + 2 * wide),
        nbytes=2 * rows * rows + 6 * rows * wide,
    )
    state, sums = call(
        state_kernel,
        (shaped((rows, wide)), shaped((part_atoms, atom_wide))),
        (base, fetch, weight_up, weight_residual, weight_message, atom_index, arrived),
        scratch=[pltpu.VMEM((rows, channels), jnp.bfloat16)],
        flops=4 * rows * wide * wide,
        nbytes=8 * rows * wide,
    )
    sums_parts = [sums] + from_next(sums, shards)
    side, chosen = call(
        functools.partial(side_kernel, shards, part_atoms),
        (shaped((rows, wide), jnp.float32), shaped((rows, 2 * part_atoms))),
        (state, weight_join, atom_index),
        flops=2 * rows * wide * wide,
        nbytes=8 * rows * wide,
    )
    return call(
        functools.partial(final_kernel, shards, (rows // count) ** -0.5),
        (shaped((rows, wide)), shaped((count, atom_wide))),
        (*sums_parts, all_atoms, weight_atom, weight_join, state, side, chosen),
        scratch=[pltpu.VMEM((2 * part_atoms, wide), jnp.bfloat16)],
        flops=4 * rows * part_atoms * wide,
        nbytes=8 * rows * wide,
    )


def solution(mesh):
    split = P(("dom", "edge"))
    placed = (
        P(("dom", "edge"), None),
        P(("dom", "edge"), None),
        split,
        P(None, ("dom", "edge")),
        P(("dom", "edge"), None),
        P(("dom", "edge"), None, None),
    ) + (P(),) * 7
    return jax.shard_map(
        body,
        mesh=mesh,
        in_specs=placed,
        out_specs=(P(("dom", "edge"), None), P(("dom", "edge"), None)),
        check_vma=False,
    )
```

```python
import functools

import jax
import jax.numpy as jnp
from jax import lax
from jax.experimental import pallas as pl
from jax.experimental.pallas import tpu as pltpu
from jax.sharding import PartitionSpec as P

root_half = 0.7071067811865476
MIB = 1 << 20
CHUNK = 256


def product(operand, weights):
    return jnp.dot(operand, weights, preferred_element_type=jnp.float32)


def silu(value):
    halved = 0.5 * value
    return halved + halved * jnp.tanh(halved)


def as_column(row):
    wide = jnp.broadcast_to(row.astype(jnp.float32), (8, row.shape[1]))
    return jnp.transpose(wide)[:, :1].astype(jnp.int32)


def row_chunks(rows):
    step = min(CHUNK, rows)
    return [slice(at, at + step) for at in range(0, rows, step)]


def call(kernel, outs, args, *, smem=(), hbm=(), scratch=(), flops=0, nbytes=0, limit=24):
    def space(at):
        return pltpu.SMEM if at in smem else pltpu.HBM if at in hbm else pltpu.VMEM

    args = [
        pltpu.with_memory_space_constraint(arg, pltpu.HBM) if at in hbm else arg
        for at, arg in enumerate(args)
    ]
    return pl.pallas_call(
        kernel,
        out_shape=outs,
        in_specs=[pl.BlockSpec(memory_space=space(at)) for at in range(len(args))],
        out_specs=jax.tree.map(
            lambda out: pl.BlockSpec(
                memory_space=pltpu.HBM if out.memory_space == pltpu.HBM else pltpu.VMEM
            ),
            outs,
        ),
        scratch_shapes=list(scratch),
        compiler_params=pltpu.CompilerParams(vmem_limit_bytes=limit * MIB),
        cost_estimate=pl.CostEstimate(flops=flops, bytes_accessed=nbytes, transcendentals=0),
    )(*args)


def shaped(shape, dtype=jnp.bfloat16, space=pltpu.VMEM):
    return space(tuple(shape), dtype)


def narrow_kernel(
    edges_hbm, weight_hbm, down_hbm, atoms_hbm, out_ref, edges_ref, weight_ref, down_ref, sems
):
    half = edges_hbm.shape[0] // 2
    pieces = [
        slice(base + rows.start, base + rows.stop)
        for rows in row_chunks(half)
        for base in (0, half)
    ]
    copies = [
        pltpu.make_async_copy(weight_hbm, weight_ref, sems.at[0]),
        pltpu.make_async_copy(down_hbm, down_ref, sems.at[1]),
    ] + [
        pltpu.make_async_copy(edges_hbm.at[piece], edges_ref.at[piece], sems.at[2 + at])
        for at, piece in enumerate(pieces)
    ]
    for copy in [copies[0], copies[2], copies[3], copies[1]] + copies[4:]:
        copy.start()
    count, wide = atoms_hbm.shape
    lanes = out_ref.shape[1]
    atom_copies = [
        pltpu.make_async_copy(
            atoms_hbm.at[:, at * lanes : (at + 1) * lanes],
            out_ref.at[half + at * count : half + (at + 1) * count, :],
            sems.at[len(copies) + at],
        )
        for at in range(wide // lanes)
    ]
    for copy in atom_copies:
        copy.start()
    copies[0].wait()
    copies[1].wait()
    for at, rows in enumerate(row_chunks(half)):
        copies[2 + 2 * at].wait()
        copies[3 + 2 * at].wait()
        sides = []
        for side in range(2):
            hidden = silu(product(edges_ref[pieces[2 * at + side], :], weight_ref[...]))
            sides.append(
                silu(
                    lax.dot_general(
                        hidden.astype(jnp.bfloat16),
                        down_ref[...],
                        (((1,), (1,)), ((), ())),
                        preferred_element_type=jnp.float32,
                    )
                )
            )
        out_ref[rows, :] = jnp.concatenate(sides, axis=1).astype(jnp.bfloat16)
    for copy in atom_copies:
        copy.wait()


def index_kernel(domains, shards, operands, *refs):
    reverse_ref = refs[0]
    sources = refs[1 : 1 + operands]
    send_ref, fetch_ref, local_ref = refs[1 + operands : 4 + operands]
    targets = refs[4 + operands : 4 + 2 * operands]
    sems = refs[-1]
    copies = [
        pltpu.make_async_copy(source, target, sems.at[at])
        for at, (source, target) in enumerate(zip(sources, targets))
    ]
    for copy in copies:
        copy.start()
    rows = reverse_ref.shape[1]
    capacity = rows // domains
    half = capacity // 2
    slots = domains * capacity
    own = lax.axis_index("dom")
    reverse = reverse_ref[...]
    holder = reverse // (rows * shards)
    source_row = lax.rem(reverse, rows)
    source_column = as_column(source_row)
    member = (lax.broadcasted_iota(jnp.int32, (domains, rows), 0) == holder).astype(jnp.bfloat16)
    before = (
        lax.broadcasted_iota(jnp.int32, (rows, rows), 0)
        < lax.broadcasted_iota(jnp.int32, (rows, rows), 1)
    ).astype(jnp.bfloat16)
    place = jnp.sum(
        product(member, before) * member.astype(jnp.float32), axis=0, keepdims=True
    ).astype(jnp.int32)
    earlier = (source_column < source_row).astype(jnp.bfloat16)
    far_place = jnp.sum(
        product(member, earlier) * member.astype(jnp.float32), axis=0, keepdims=True
    ).astype(jnp.int32)

    def slot_of(at):
        part = (at >= half).astype(jnp.int32)
        slot = part * (slots // 2) + holder * half + at - part * half
        return jnp.where(holder == own, -1, slot)

    send_slot = slot_of(place)
    send_ref[...] = (
        lax.broadcasted_iota(jnp.int32, (slots, rows), 0) == send_slot
    ).astype(jnp.bfloat16)
    fetch_column = as_column(slot_of(far_place))
    fetch_ref[...] = (
        lax.broadcasted_iota(jnp.int32, (rows, slots), 1) == fetch_column
    ).astype(jnp.bfloat16)
    local_column = as_column(jnp.where(holder == own, source_row, -1))
    local_ref[...] = (
        lax.broadcasted_iota(jnp.int32, (rows, rows), 1) == local_column
    ).astype(jnp.bfloat16)
    for copy in copies:
        copy.wait()


def mix_kernel(count_parts, *refs):
    source_ref, place_ref, tiles_ref = refs[:3]
    parts = refs[3 : 3 + count_parts]
    send_ref, trip_ref, out_ref, atoms_ref, held_ref = refs[3 + count_parts :]
    blocks, block_len, width = tiles_ref.shape
    count = width // block_len
    lines = held_ref.shape[0] // count_parts
    atom_wide = atoms_ref.shape[1]
    tail = parts[0].shape[0] - lines
    own_atoms = tail * parts[0].shape[1] // atom_wide
    shards = atoms_ref.shape[0] // own_atoms
    lanes = parts[0].shape[1]
    me = lax.axis_index("edge")
    for at in range(count_parts):
        held_ref[at * lines : (at + 1) * lines, :] = parts[at][:lines, :]
    for by in range(shards):
        place = place_ref[lax.rem(me + by, shards)]
        for piece in range(atom_wide // lanes):
            start = lines + piece * own_atoms
            rows = parts[0][start : start + own_atoms, :]
            for at in range(1, count_parts):
                rows = jnp.where(place == at, parts[at][start : start + own_atoms, :], rows)
            atoms_ref[
                by * own_atoms : (by + 1) * own_atoms, piece * lanes : (piece + 1) * lanes
            ] = rows
    half_blocks = blocks // 2
    channels = trip_ref.shape[1]
    for block in range(blocks):
        picks = []
        for tile in range(count):
            source = source_ref[block, tile]
            shard = source // blocks
            within = source - shard * blocks
            upper = within // half_blocks
            start = place_ref[shard] * lines + (within - upper * half_blocks) * block_len
            rows = held_ref[pl.ds(pl.multiple_of(start, block_len), block_len), :]
            picks.append(jnp.where(upper == 1, rows[:, channels:], rows[:, :channels]))
        mixed = product(tiles_ref[block], jnp.concatenate(picks, axis=0))
        trip_ref[block * block_len : (block + 1) * block_len, :] = mixed.astype(jnp.bfloat16)
    half_slots = send_ref.shape[0] // 2
    low = product(send_ref[:half_slots, :], trip_ref[...])
    high = product(send_ref[half_slots:, :], trip_ref[...])
    out_ref[...] = jnp.concatenate([low, high], axis=1).astype(jnp.bfloat16)


def base_kernel(edges_ref, trip_ref, local_ref, up_ref, out_ref):
    channels = trip_ref.shape[1]
    for rows in row_chunks(edges_ref.shape[0]):
        picked = product(local_ref[rows, :], trip_ref[...]).astype(jnp.bfloat16)
        joined = product(trip_ref[rows, :], up_ref[0]) + product(picked, up_ref[1])
        out_ref[rows, :] = edges_ref[rows, :].astype(jnp.float32) + joined * root_half


def state_kernel(
    base_ref, fetch_ref, up_ref, residual_ref, message_ref, index_ref, arrived_ref,
    state_ref, sums_ref, slots_ref,
):
    channels = up_ref.shape[1]
    half = arrived_ref.shape[0]
    slots_ref[:half, :] = arrived_ref[:, :channels]
    slots_ref[half:, :] = arrived_ref[:, channels:]
    for rows in row_chunks(base_ref.shape[0]):
        picked = product(fetch_ref[rows, :], slots_ref[...]).astype(jnp.bfloat16)
        state = (base_ref[rows, :] + product(picked, up_ref[1]) * root_half).astype(jnp.bfloat16)
        for layer in range(residual_ref.shape[0]):
            middle = silu(product(state, residual_ref[layer, 0])).astype(jnp.bfloat16)
            branch = silu(product(middle, residual_ref[layer, 1]))
            state = ((state.astype(jnp.float32) + branch) * root_half).astype(jnp.bfloat16)
        state_ref[rows, :] = state
    part_atoms = sums_ref.shape[0]
    shards = lax.axis_size("edge")
    near = near_atoms(index_ref[1:2, :], part_atoms, shards)
    chosen = (
        lax.broadcasted_iota(jnp.int32, (part_atoms, near.shape[1]), 0) == near
    ).astype(jnp.bfloat16)
    gathered = product(chosen, state_ref[...]).astype(jnp.bfloat16)
    sums_ref[...] = product(gathered, message_ref[...]).astype(jnp.bfloat16)


def near_atoms(index, part_atoms, shards):
    first = lax.axis_index("edge") * (part_atoms // shards)
    shifted = index - first
    return jnp.where(shifted < 0, shifted + part_atoms, shifted)


def side_kernel(shards, part_atoms, state_ref, join_ref, index_ref, out_ref, chosen_ref):
    width = join_ref.shape[0] - state_ref.shape[1]
    for rows in row_chunks(state_ref.shape[0]):
        out_ref[rows, :] = product(state_ref[rows, :], join_ref[width:, :])
    index = near_atoms(index_ref[...], part_atoms, shards)
    for end in range(2):
        column = as_column(index[end : end + 1, :])
        chosen_ref[:, end * part_atoms : (end + 1) * part_atoms] = (
            lax.broadcasted_iota(jnp.int32, (column.shape[0], part_atoms), 1) == column
        ).astype(jnp.bfloat16)


def final_kernel(shards, scale, *refs):
    sums = refs[:shards]
    atoms_ref, weight_ref, join_ref, state_ref, side_ref, chosen_ref = refs[shards : shards + 6]
    edges_hbm, own_ref, table_ref, edges_ref, sems = refs[shards + 6 :]
    part_atoms = atoms_ref.shape[0]
    count = part_atoms // shards
    total = sums[0][...].astype(jnp.float32)
    for at in range(1, shards):
        piece = sums[at][...].astype(jnp.float32)
        cut = part_atoms - at * count
        total = total + jnp.concatenate([piece[cut:], piece[:cut]], axis=0)
    scaled = (total * scale).astype(jnp.bfloat16)
    middle = silu(product(scaled, weight_ref[0])).astype(jnp.bfloat16)
    renewed = (atoms_ref[...].astype(jnp.float32) + product(middle, weight_ref[1])).astype(jnp.bfloat16)
    own_ref[...] = renewed[:count, :]
    width = renewed.shape[1]
    for end in range(2):
        table_ref[end * part_atoms : (end + 1) * part_atoms, :] = product(
            renewed, join_ref[end * width : (end + 1) * width, :]
        ).astype(jnp.bfloat16)
    copies = []
    for at, rows in enumerate(row_chunks(state_ref.shape[0])):
        update = silu(product(chosen_ref[rows, :], table_ref[...]) + side_ref[rows, :])
        state = state_ref[rows, :].astype(jnp.float32)
        edges_ref[rows, :] = ((state + update) * root_half).astype(jnp.bfloat16)
        copies.append(
            pltpu.make_async_copy(edges_ref.at[rows], edges_hbm.at[rows], sems.at[at])
        )
        copies[-1].start()
    for copy in copies:
        copy.wait()


def from_next(value, shards):
    return [
        lax.ppermute(value, "edge", [((at + by) % shards, at) for at in range(shards)])
        for by in range(1, shards)
    ]


def along_edge(value, shards):
    if shards != 4:
        parts = [value] + from_next(value, shards)
        return parts, [[(to - at) % shards for to in range(shards)] for at in range(shards)]
    far = lax.ppermute(value, "edge", [(0, 2), (2, 0), (1, 3), (3, 1)])
    middle = lax.ppermute(value, "edge", [(1, 2), (2, 1)])
    near = lax.ppermute(value, "edge", [(0, 1), (1, 0), (2, 3), (3, 2)])
    relayed = lax.ppermute(far, "edge", [(2, 3), (1, 0)])
    parts = [value, near, far, middle, relayed]
    return parts, [[0, 1, 2, 4], [1, 0, 3, 2], [2, 3, 0, 1], [4, 2, 1, 0]]


def body(
    edges,
    atoms,
    reverse,
    atom_index,
    tile_source,
    tiles,
    weight_edge,
    weight_down,
    weight_up,
    weight_residual,
    weight_message,
    weight_atom,
    weight_join,
):
    rows, wide = edges.shape
    channels = weight_down.shape[0]
    domains = lax.axis_size("dom")
    shards = lax.axis_size("edge")
    count, atom_wide = atoms.shape
    part_atoms = count * shards
    lines = rows // 2
    packed = 2 * channels

    narrow = call(
        narrow_kernel,
        shaped((lines + count * atom_wide // packed, packed)),
        (edges, weight_edge, weight_down, atoms),
        hbm=(0, 1, 2, 3),
        scratch=[
            pltpu.VMEM(edges.shape, jnp.bfloat16),
            pltpu.VMEM(weight_edge.shape, jnp.bfloat16),
            pltpu.VMEM(weight_down.shape, jnp.bfloat16),
            pltpu.SemaphoreType.DMA((2 + 2 * len(row_chunks(lines)) + atom_wide // packed,)),
        ],
        flops=2 * rows * wide * (wide + channels),
        nbytes=2 * (rows * wide + wide * wide),
    )
    narrow_parts, places = along_edge(narrow, shards)
    place = jnp.asarray(places, jnp.int32)[lax.axis_index("edge")]
    later = (
        edges, tiles, weight_up, weight_residual, weight_message, weight_join, weight_atom, atom_index
    )
    send, fetch, local, *later = call(
        functools.partial(index_kernel, domains, shards, len(later)),
        (shaped((rows, rows)),) * 3 + tuple(shaped(each.shape, each.dtype) for each in later),
        (reverse.reshape(1, rows), *later),
        hbm=range(1, 1 + len(later)),
        scratch=[pltpu.SemaphoreType.DMA((len(later),))],
        flops=40 * rows * rows,
        nbytes=6 * rows * rows,
    )
    edges, tiles, weight_up, weight_residual, weight_message, weight_join, weight_atom, atom_index = later
    trip_out, outgoing, all_atoms = call(
        functools.partial(mix_kernel, len(narrow_parts)),
        (
            shaped((rows, channels)),
            shaped((lines, packed)),
            shaped((part_atoms, atom_wide)),
        ),
        (tile_source, place, tiles, *narrow_parts, send),
        smem=(0, 1),
        scratch=[pltpu.VMEM((len(narrow_parts) * lines, packed), jnp.bfloat16)],
        flops=2 * rows * rows * channels,
        nbytes=2 * rows * rows,
    )
    arrived = lax.all_to_all(outgoing, "dom", split_axis=0, concat_axis=0, tiled=True)
    base = call(
        base_kernel,
        shaped((rows, wide), jnp.float32),
        (edges, trip_out, local, weight_up),
        flops=2 * rows * channels * (rows + 2 * wide),
        nbytes=2 * rows * rows + 6 * rows * wide,
    )
    state, sums = call(
        state_kernel,
        (shaped((rows, wide)), shaped((part_atoms, atom_wide))),
        (base, fetch, weight_up, weight_residual, weight_message, atom_index, arrived),
        scratch=[pltpu.VMEM((rows, channels), jnp.bfloat16)],
        flops=4 * rows * wide * wide,
        nbytes=8 * rows * wide,
    )
    sums_parts = [sums] + from_next(sums, shards)
    side, chosen = call(
        functools.partial(side_kernel, shards, part_atoms),
        (shaped((rows, wide), jnp.float32), shaped((rows, 2 * part_atoms))),
        (state, weight_join, atom_index),
        flops=2 * rows * wide * wide,
        nbytes=8 * rows * wide,
    )
    return call(
        functools.partial(final_kernel, shards, (rows // count) ** -0.5),
        (shaped((rows, wide), space=pltpu.HBM), shaped((count, atom_wide))),
        (*sums_parts, all_atoms, weight_atom, weight_join, state, side, chosen),
        scratch=[
            pltpu.VMEM((2 * part_atoms, wide), jnp.bfloat16),
            pltpu.VMEM((rows, wide), jnp.bfloat16),
            pltpu.SemaphoreType.DMA((len(row_chunks(rows)),)),
        ],
        flops=4 * rows * part_atoms * wide,
        nbytes=8 * rows * wide,
    )


def solution(mesh):
    split = P(("dom", "edge"))
    placed = (
        P(("dom", "edge"), None),
        P(("dom", "edge"), None),
        split,
        P(None, ("dom", "edge")),
        P(("dom", "edge"), None),
        P(("dom", "edge"), None, None),
    ) + (P(),) * 7
    return jax.shard_map(
        body,
        mesh=mesh,
        in_specs=placed,
        out_specs=(P(("dom", "edge"), None), P(("dom", "edge"), None)),
        check_vma=False,
    )
```

```python
import functools

import jax
import jax.numpy as jnp
from jax import lax
from jax.experimental import pallas as pl
from jax.experimental.pallas import tpu as pltpu
from jax.sharding import PartitionSpec as P

root_half = 0.7071067811865476
MIB = 1 << 20
CHUNK = 256


def product(operand, weights):
    return jnp.dot(operand, weights, preferred_element_type=jnp.float32)


def silu(value):
    halved = 0.5 * value
    return halved + halved * jnp.tanh(halved)


def as_column(row):
    wide = jnp.broadcast_to(row.astype(jnp.float32), (8, row.shape[1]))
    return jnp.transpose(wide)[:, :1].astype(jnp.int32)


def row_chunks(rows):
    step = min(CHUNK, rows)
    return [slice(at, at + step) for at in range(0, rows, step)]


def call(kernel, outs, args, *, smem=(), hbm=(), scratch=(), flops=0, nbytes=0, limit=24):
    def space(at):
        return pltpu.SMEM if at in smem else pltpu.HBM if at in hbm else pltpu.VMEM

    args = [
        pltpu.with_memory_space_constraint(arg, pltpu.HBM) if at in hbm else arg
        for at, arg in enumerate(args)
    ]
    return pl.pallas_call(
        kernel,
        out_shape=outs,
        in_specs=[pl.BlockSpec(memory_space=space(at)) for at in range(len(args))],
        out_specs=jax.tree.map(
            lambda out: pl.BlockSpec(
                memory_space=pltpu.HBM if out.memory_space == pltpu.HBM else pltpu.VMEM
            ),
            outs,
        ),
        scratch_shapes=list(scratch),
        compiler_params=pltpu.CompilerParams(vmem_limit_bytes=limit * MIB),
        cost_estimate=pl.CostEstimate(flops=flops, bytes_accessed=nbytes, transcendentals=0),
    )(*args)


def shaped(shape, dtype=jnp.bfloat16, space=pltpu.VMEM):
    return space(tuple(shape), dtype)


def narrow_kernel(
    edges_hbm, weight_hbm, down_hbm, atoms_hbm, out_ref, edges_ref, weight_ref, down_ref, sems
):
    half = edges_hbm.shape[0] // 2
    pieces = [
        slice(base + rows.start, base + rows.stop)
        for rows in row_chunks(half)
        for base in (0, half)
    ]
    copies = [
        pltpu.make_async_copy(weight_hbm, weight_ref, sems.at[0]),
        pltpu.make_async_copy(down_hbm, down_ref, sems.at[1]),
    ] + [
        pltpu.make_async_copy(edges_hbm.at[piece], edges_ref.at[piece], sems.at[2 + at])
        for at, piece in enumerate(pieces)
    ]
    for copy in [copies[0], copies[2], copies[3], copies[1]] + copies[4:]:
        copy.start()
    count, wide = atoms_hbm.shape
    lanes = out_ref.shape[1]
    atom_copies = [
        pltpu.make_async_copy(
            atoms_hbm.at[:, at * lanes : (at + 1) * lanes],
            out_ref.at[half + at * count : half + (at + 1) * count, :],
            sems.at[len(copies) + at],
        )
        for at in range(wide // lanes)
    ]
    for copy in atom_copies:
        copy.start()
    copies[0].wait()
    copies[1].wait()
    for at, rows in enumerate(row_chunks(half)):
        copies[2 + 2 * at].wait()
        copies[3 + 2 * at].wait()
        sides = []
        for side in range(2):
            hidden = silu(product(edges_ref[pieces[2 * at + side], :], weight_ref[...]))
            sides.append(
                silu(
                    lax.dot_general(
                        hidden.astype(jnp.bfloat16),
                        down_ref[...],
                        (((1,), (1,)), ((), ())),
                        preferred_element_type=jnp.float32,
                    )
                )
            )
        out_ref[rows, :] = jnp.concatenate(sides, axis=1).astype(jnp.bfloat16)
    for copy in atom_copies:
        copy.wait()


def index_kernel(domains, shards, operands, *refs):
    reverse_ref = refs[0]
    sources = refs[1 : 1 + operands]
    send_ref, fetch_ref, local_ref = refs[1 + operands : 4 + operands]
    targets = refs[4 + operands : 4 + 2 * operands]
    sems = refs[-1]
    copies = [
        pltpu.make_async_copy(source, target, sems.at[at])
        for at, (source, target) in enumerate(zip(sources, targets))
    ]
    for copy in copies:
        copy.start()
    rows = reverse_ref.shape[1]
    capacity = rows // domains
    half = capacity // 2
    slots = (domains - 1) * capacity
    own = lax.axis_index("dom")
    reverse = reverse_ref[...]
    holder = reverse // (rows * shards)
    source_row = lax.rem(reverse, rows)
    partner = holder ^ own
    source_column = as_column(source_row)
    member = (lax.broadcasted_iota(jnp.int32, (domains, rows), 0) == partner).astype(jnp.bfloat16)
    before = (
        lax.broadcasted_iota(jnp.int32, (rows, rows), 0)
        < lax.broadcasted_iota(jnp.int32, (rows, rows), 1)
    ).astype(jnp.bfloat16)
    place = jnp.sum(
        product(member, before) * member.astype(jnp.float32), axis=0, keepdims=True
    ).astype(jnp.int32)
    earlier = (source_column < source_row).astype(jnp.bfloat16)
    far_place = jnp.sum(
        product(member, earlier) * member.astype(jnp.float32), axis=0, keepdims=True
    ).astype(jnp.int32)

    def slot_of(at):
        part = (at >= half).astype(jnp.int32)
        slot = part * (slots // 2) + (partner - 1) * half + at - part * half
        return jnp.where(partner == 0, -1, slot)

    send_slot = slot_of(place)
    send_ref[...] = (
        lax.broadcasted_iota(jnp.int32, (slots, rows), 0) == send_slot
    ).astype(jnp.bfloat16)
    fetch_column = as_column(slot_of(far_place))
    fetch_ref[...] = (
        lax.broadcasted_iota(jnp.int32, (rows, slots), 1) == fetch_column
    ).astype(jnp.bfloat16)
    local_column = as_column(jnp.where(partner == 0, source_row, -1))
    local_ref[...] = (
        lax.broadcasted_iota(jnp.int32, (rows, rows), 1) == local_column
    ).astype(jnp.bfloat16)
    for copy in copies:
        copy.wait()


def mix_kernel(shards, *refs):
    source_ref, tiles_ref = refs[:2]
    parts = refs[2 : 2 + shards]
    send_ref, trip_ref, atoms_ref = refs[2 + shards : 5 + shards]
    out_refs = refs[5 + shards : -1]
    held_ref = refs[-1]
    blocks, block_len, width = tiles_ref.shape
    count = width // block_len
    lines = held_ref.shape[0] // shards
    own_atoms = atoms_ref.shape[0] // shards
    atom_wide = atoms_ref.shape[1]
    lanes = held_ref.shape[1]
    me = lax.axis_index("edge")
    for at in range(shards):
        held_ref[at * lines : (at + 1) * lines, :] = parts[at][:lines, :]
        for piece in range(atom_wide // lanes):
            start = lines + piece * own_atoms
            atoms_ref[
                at * own_atoms : (at + 1) * own_atoms, piece * lanes : (piece + 1) * lanes
            ] = parts[at][start : start + own_atoms, :]
    half_blocks = blocks // 2
    channels = trip_ref.shape[1]
    for block in range(blocks):
        picks = []
        for tile in range(count):
            source = source_ref[block, tile]
            shard = source // blocks
            within = source - shard * blocks
            upper = within // half_blocks
            near = lax.rem(shard - me + shards, shards)
            start = near * lines + (within - upper * half_blocks) * block_len
            rows = held_ref[pl.ds(pl.multiple_of(start, block_len), block_len), :]
            picks.append(jnp.where(upper == 1, rows[:, channels:], rows[:, :channels]))
        mixed = product(tiles_ref[block], jnp.concatenate(picks, axis=0))
        trip_ref[block * block_len : (block + 1) * block_len, :] = mixed.astype(jnp.bfloat16)
    half_slots = send_ref.shape[0] // 2
    low = product(send_ref[:half_slots, :], trip_ref[...])
    high = product(send_ref[half_slots:, :], trip_ref[...])
    packed = jnp.concatenate([low, high], axis=1).astype(jnp.bfloat16)
    each = half_slots // len(out_refs)
    for at, out_ref in enumerate(out_refs):
        out_ref[...] = packed[at * each : (at + 1) * each, :]


def base_kernel(edges_ref, trip_ref, local_ref, up_ref, out_ref):
    channels = trip_ref.shape[1]
    for rows in row_chunks(edges_ref.shape[0]):
        picked = product(local_ref[rows, :], trip_ref[...]).astype(jnp.bfloat16)
        joined = product(trip_ref[rows, :], up_ref[0]) + product(picked, up_ref[1])
        out_ref[rows, :] = edges_ref[rows, :].astype(jnp.float32) + joined * root_half


def state_kernel(partners, *refs):
    base_ref, fetch_ref, up_ref, residual_ref, message_ref, index_ref = refs[:6]
    arrived = refs[6 : 6 + partners]
    state_ref, sums_ref, slots_ref = refs[6 + partners :]
    channels = up_ref.shape[1]
    each = arrived[0].shape[0]
    for at in range(partners):
        piece = arrived[at][...]
        slots_ref[at * each : (at + 1) * each, :] = piece[:, :channels]
        slots_ref[(partners + at) * each : (partners + at + 1) * each, :] = piece[:, channels:]
    for rows in row_chunks(base_ref.shape[0]):
        picked = product(fetch_ref[rows, :], slots_ref[...]).astype(jnp.bfloat16)
        state = (base_ref[rows, :] + product(picked, up_ref[1]) * root_half).astype(jnp.bfloat16)
        for layer in range(residual_ref.shape[0]):
            middle = silu(product(state, residual_ref[layer, 0])).astype(jnp.bfloat16)
            branch = silu(product(middle, residual_ref[layer, 1]))
            state = ((state.astype(jnp.float32) + branch) * root_half).astype(jnp.bfloat16)
        state_ref[rows, :] = state
    part_atoms = sums_ref.shape[0]
    shards = lax.axis_size("edge")
    near = near_atoms(index_ref[1:2, :], part_atoms, shards)
    chosen = (
        lax.broadcasted_iota(jnp.int32, (part_atoms, near.shape[1]), 0) == near
    ).astype(jnp.bfloat16)
    gathered = product(chosen, state_ref[...]).astype(jnp.bfloat16)
    sums_ref[...] = product(gathered, message_ref[...]).astype(jnp.bfloat16)


def near_atoms(index, part_atoms, shards):
    first = lax.axis_index("edge") * (part_atoms // shards)
    shifted = index - first
    return jnp.where(shifted < 0, shifted + part_atoms, shifted)


def side_kernel(shards, part_atoms, state_ref, join_ref, index_ref, out_ref, chosen_ref):
    width = join_ref.shape[0] - state_ref.shape[1]
    for rows in row_chunks(state_ref.shape[0]):
        out_ref[rows, :] = product(state_ref[rows, :], join_ref[width:, :])
    index = near_atoms(index_ref[...], part_atoms, shards)
    for end in range(2):
        column = as_column(index[end : end + 1, :])
        chosen_ref[:, end * part_atoms : (end + 1) * part_atoms] = (
            lax.broadcasted_iota(jnp.int32, (column.shape[0], part_atoms), 1) == column
        ).astype(jnp.bfloat16)


def final_kernel(shards, scale, *refs):
    sums = refs[:shards]
    atoms_ref, weight_ref, join_ref, state_ref, side_ref, chosen_ref = refs[shards : shards + 6]
    edges_hbm, own_hbm, table_ref, edges_ref, own_ref, sems = refs[shards + 6 :]
    part_atoms = atoms_ref.shape[0]
    count = part_atoms // shards
    total = sums[0][...].astype(jnp.float32)
    for at in range(1, shards):
        piece = sums[at][...].astype(jnp.float32)
        cut = part_atoms - at * count
        total = total + jnp.concatenate([piece[cut:], piece[:cut]], axis=0)
    scaled = (total * scale).astype(jnp.bfloat16)
    middle = silu(product(scaled, weight_ref[0])).astype(jnp.bfloat16)
    renewed = (atoms_ref[...].astype(jnp.float32) + product(middle, weight_ref[1])).astype(jnp.bfloat16)
    own_ref[...] = renewed[:count, :]
    own_copy = pltpu.make_async_copy(own_ref, own_hbm, sems.at[0])
    own_copy.start()
    width = renewed.shape[1]
    for end in range(2):
        table_ref[end * part_atoms : (end + 1) * part_atoms, :] = product(
            renewed, join_ref[end * width : (end + 1) * width, :]
        ).astype(jnp.bfloat16)
    copies = [own_copy]
    for at, rows in enumerate(row_chunks(state_ref.shape[0])):
        update = silu(product(chosen_ref[rows, :], table_ref[...]) + side_ref[rows, :])
        state = state_ref[rows, :].astype(jnp.float32)
        edges_ref[rows, :] = ((state + update) * root_half).astype(jnp.bfloat16)
        copies.append(
            pltpu.make_async_copy(edges_ref.at[rows], edges_hbm.at[rows], sems.at[1 + at])
        )
        copies[-1].start()
    for copy in copies:
        copy.wait()


def from_next(value, shards):
    return [
        lax.ppermute(value, "edge", [((at + by) % shards, at) for at in range(shards)])
        for by in range(1, shards)
    ]


def body(
    edges,
    atoms,
    reverse,
    atom_index,
    tile_source,
    tiles,
    weight_edge,
    weight_down,
    weight_up,
    weight_residual,
    weight_message,
    weight_atom,
    weight_join,
):
    rows, wide = edges.shape
    channels = weight_down.shape[0]
    domains = lax.axis_size("dom")
    shards = lax.axis_size("edge")
    count, atom_wide = atoms.shape
    part_atoms = count * shards
    capacity = rows // domains
    partners = domains - 1
    slots = partners * capacity
    lines = rows // 2
    packed = 2 * channels

    narrow = call(
        narrow_kernel,
        shaped((lines + count * atom_wide // packed, packed)),
        (edges, weight_edge, weight_down, atoms),
        hbm=(0, 1, 2, 3),
        scratch=[
            pltpu.VMEM(edges.shape, jnp.bfloat16),
            pltpu.VMEM(weight_edge.shape, jnp.bfloat16),
            pltpu.VMEM(weight_down.shape, jnp.bfloat16),
            pltpu.SemaphoreType.DMA((2 + 2 * len(row_chunks(lines)) + atom_wide // packed,)),
        ],
        flops=2 * rows * wide * (wide + channels),
        nbytes=2 * (rows * wide + wide * wide),
    )
    narrow_parts = [narrow] + from_next(narrow, shards)
    later = (
        edges, tiles, weight_up, weight_residual, weight_message, weight_join, weight_atom, atom_index
    )
    send, fetch, local, *later = call(
        functools.partial(index_kernel, domains, shards, len(later)),
        (shaped((slots, rows)), shaped((rows, slots)), shaped((rows, rows)))
        + tuple(shaped(each.shape, each.dtype) for each in later),
        (reverse.reshape(1, rows), *later),
        hbm=range(1, 1 + len(later)),
        scratch=[pltpu.SemaphoreType.DMA((len(later),))],
        flops=40 * rows * rows,
        nbytes=6 * rows * rows,
    )
    edges, tiles, weight_up, weight_residual, weight_message, weight_join, weight_atom, atom_index = later
    trip_out, all_atoms, *outgoing = call(
        functools.partial(mix_kernel, shards),
        (shaped((rows, channels)), shaped((part_atoms, atom_wide)))
        + (shaped((capacity // 2, packed)),) * partners,
        (tile_source, tiles, *narrow_parts, send),
        smem=(0,),
        scratch=[pltpu.VMEM((shards * lines, packed), jnp.bfloat16)],
        flops=2 * rows * rows * channels,
        nbytes=2 * rows * rows,
    )
    arrived = [
        lax.ppermute(outgoing[by - 1], "dom", [(at, at ^ by) for at in range(domains)])
        for by in range(1, domains)
    ]
    base = call(
        base_kernel,
        shaped((rows, wide), jnp.float32),
        (edges, trip_out, local, weight_up),
        flops=2 * rows * channels * (rows + 2 * wide),
        nbytes=2 * rows * rows + 6 * rows * wide,
    )
    state, sums = call(
        functools.partial(state_kernel, partners),
        (shaped((rows, wide)), shaped((part_atoms, atom_wide))),
        (base, fetch, weight_up, weight_residual, weight_message, atom_index, *arrived),
        scratch=[pltpu.VMEM((slots, channels), jnp.bfloat16)],
        flops=4 * rows * wide * wide,
        nbytes=8 * rows * wide,
    )
    sums_parts = [sums] + from_next(sums, shards)
    side, chosen = call(
        functools.partial(side_kernel, shards, part_atoms),
        (shaped((rows, wide), jnp.float32), shaped((rows, 2 * part_atoms))),
        (state, weight_join, atom_index),
        flops=2 * rows * wide * wide,
        nbytes=8 * rows * wide,
    )
    return call(
        functools.partial(final_kernel, shards, (rows // count) ** -0.5),
        (shaped((rows, wide), space=pltpu.HBM), shaped((count, atom_wide), space=pltpu.HBM)),
        (*sums_parts, all_atoms, weight_atom, weight_join, state, side, chosen),
        scratch=[
            pltpu.VMEM((2 * part_atoms, wide), jnp.bfloat16),
            pltpu.VMEM((rows, wide), jnp.bfloat16),
            pltpu.VMEM((count, atom_wide), jnp.bfloat16),
            pltpu.SemaphoreType.DMA((1 + len(row_chunks(rows)),)),
        ],
        flops=4 * rows * part_atoms * wide,
        nbytes=8 * rows * wide,
    )


def solution(mesh):
    split = P(("dom", "edge"))
    placed = (
        P(("dom", "edge"), None),
        P(("dom", "edge"), None),
        split,
        P(None, ("dom", "edge")),
        P(("dom", "edge"), None),
        P(("dom", "edge"), None, None),
    ) + (P(),) * 7
    return jax.shard_map(
        body,
        mesh=mesh,
        in_specs=placed,
        out_specs=(P(("dom", "edge"), None), P(("dom", "edge"), None)),
        check_vma=False,
    )
```

```python
import functools

import jax
import jax.numpy as jnp
from jax import lax
from jax.experimental import pallas as pl
from jax.experimental.pallas import tpu as pltpu
from jax.sharding import PartitionSpec as P

root_half = 0.7071067811865476
MIB = 1 << 20
CHUNK = 256


def product(operand, weights):
    return jnp.dot(operand, weights, preferred_element_type=jnp.float32)


def silu(value):
    halved = 0.5 * value
    return halved + halved * jnp.tanh(halved)


def as_column(row):
    wide = jnp.broadcast_to(row.astype(jnp.float32), (8, row.shape[1]))
    return jnp.transpose(wide)[:, :1].astype(jnp.int32)


def row_chunks(rows):
    step = min(CHUNK, rows)
    return [slice(at, at + step) for at in range(0, rows, step)]


def call(kernel, outs, args, *, smem=(), hbm=(), scratch=(), flops=0, nbytes=0, limit=24):
    def space(at):
        return pltpu.SMEM if at in smem else pltpu.HBM if at in hbm else pltpu.VMEM

    args = [
        pltpu.with_memory_space_constraint(arg, pltpu.HBM) if at in hbm else arg
        for at, arg in enumerate(args)
    ]
    return pl.pallas_call(
        kernel,
        out_shape=outs,
        in_specs=[pl.BlockSpec(memory_space=space(at)) for at in range(len(args))],
        out_specs=jax.tree.map(
            lambda out: pl.BlockSpec(
                memory_space=pltpu.HBM if out.memory_space == pltpu.HBM else pltpu.VMEM
            ),
            outs,
        ),
        scratch_shapes=list(scratch),
        compiler_params=pltpu.CompilerParams(vmem_limit_bytes=limit * MIB),
        cost_estimate=pl.CostEstimate(flops=flops, bytes_accessed=nbytes, transcendentals=0),
    )(*args)


def shaped(shape, dtype=jnp.bfloat16, space=pltpu.VMEM):
    return space(tuple(shape), dtype)


def narrow_kernel(
    edges_hbm, weight_hbm, down_hbm, atoms_hbm, out_ref, edges_ref, weight_ref, down_ref, sems
):
    half = edges_hbm.shape[0] // 2
    pieces = [
        slice(base + rows.start, base + rows.stop)
        for rows in row_chunks(half)
        for base in (0, half)
    ]
    copies = [
        pltpu.make_async_copy(weight_hbm, weight_ref, sems.at[0]),
        pltpu.make_async_copy(down_hbm, down_ref, sems.at[1]),
    ] + [
        pltpu.make_async_copy(edges_hbm.at[piece], edges_ref.at[piece], sems.at[2 + at])
        for at, piece in enumerate(pieces)
    ]
    for copy in [copies[0], copies[2], copies[3], copies[1]] + copies[4:]:
        copy.start()
    count, wide = atoms_hbm.shape
    lanes = out_ref.shape[1]
    atom_copies = [
        pltpu.make_async_copy(
            atoms_hbm.at[:, at * lanes : (at + 1) * lanes],
            out_ref.at[half + at * count : half + (at + 1) * count, :],
            sems.at[len(copies) + at],
        )
        for at in range(wide // lanes)
    ]
    for copy in atom_copies:
        copy.start()
    copies[0].wait()
    copies[1].wait()
    for at, rows in enumerate(row_chunks(half)):
        copies[2 + 2 * at].wait()
        copies[3 + 2 * at].wait()
        sides = []
        for side in range(2):
            hidden = silu(product(edges_ref[pieces[2 * at + side], :], weight_ref[...]))
            sides.append(
                silu(
                    lax.dot_general(
                        hidden.astype(jnp.bfloat16),
                        down_ref[...],
                        (((1,), (1,)), ((), ())),
                        preferred_element_type=jnp.float32,
                    )
                )
            )
        out_ref[rows, :] = jnp.concatenate(sides, axis=1).astype(jnp.bfloat16)
    for copy in atom_copies:
        copy.wait()


def index_kernel(domains, shards, operands, *refs):
    reverse_ref = refs[0]
    sources = refs[1 : 1 + operands]
    send_ref, fetch_ref, local_ref = refs[1 + operands : 4 + operands]
    targets = refs[4 + operands : 4 + 2 * operands]
    sems = refs[-1]
    copies = [
        pltpu.make_async_copy(source, target, sems.at[at])
        for at, (source, target) in enumerate(zip(sources, targets))
    ]
    for copy in copies:
        copy.start()
    rows = reverse_ref.shape[1]
    capacity = rows // domains
    half = capacity // 2
    slots = (domains - 1) * capacity
    own = lax.axis_index("dom")
    reverse = reverse_ref[...]
    holder = reverse // (rows * shards)
    source_row = lax.rem(reverse, rows)
    partner = holder ^ own
    source_column = as_column(source_row)
    member = (lax.broadcasted_iota(jnp.int32, (domains, rows), 0) == partner).astype(jnp.bfloat16)
    before = (
        lax.broadcasted_iota(jnp.int32, (rows, rows), 0)
        < lax.broadcasted_iota(jnp.int32, (rows, rows), 1)
    ).astype(jnp.bfloat16)
    place = jnp.sum(
        product(member, before) * member.astype(jnp.float32), axis=0, keepdims=True
    ).astype(jnp.int32)
    earlier = (source_column < source_row).astype(jnp.bfloat16)
    far_place = jnp.sum(
        product(member, earlier) * member.astype(jnp.float32), axis=0, keepdims=True
    ).astype(jnp.int32)

    def slot_of(at):
        part = (at >= half).astype(jnp.int32)
        slot = part * (slots // 2) + (domains - 1 - partner) * half + at - part * half
        return jnp.where(partner == 0, -1, slot)

    send_slot = slot_of(place)
    send_ref[...] = (
        lax.broadcasted_iota(jnp.int32, (slots, rows), 0) == send_slot
    ).astype(jnp.bfloat16)
    fetch_column = as_column(slot_of(far_place))
    fetch_ref[...] = (
        lax.broadcasted_iota(jnp.int32, (rows, slots), 1) == fetch_column
    ).astype(jnp.bfloat16)
    local_column = as_column(jnp.where(partner == 0, source_row, -1))
    local_ref[...] = (
        lax.broadcasted_iota(jnp.int32, (rows, rows), 1) == local_column
    ).astype(jnp.bfloat16)
    for copy in copies:
        copy.wait()


def mix_kernel(shards, *refs):
    source_ref, tiles_ref = refs[:2]
    parts = refs[2 : 2 + shards]
    send_ref, trip_ref, atoms_ref = refs[2 + shards : 5 + shards]
    out_refs = refs[5 + shards : -1]
    held_ref = refs[-1]
    blocks, block_len, width = tiles_ref.shape
    count = width // block_len
    lines = held_ref.shape[0] // shards
    own_atoms = atoms_ref.shape[0] // shards
    atom_wide = atoms_ref.shape[1]
    lanes = held_ref.shape[1]
    me = lax.axis_index("edge")
    for part, at in zip(parts, distances(shards)):
        held_ref[at * lines : (at + 1) * lines, :] = part[:lines, :]
        for piece in range(atom_wide // lanes):
            start = lines + piece * own_atoms
            atoms_ref[
                at * own_atoms : (at + 1) * own_atoms, piece * lanes : (piece + 1) * lanes
            ] = part[start : start + own_atoms, :]
    half_blocks = blocks // 2
    channels = trip_ref.shape[1]
    for block in range(blocks):
        picks = []
        for tile in range(count):
            source = source_ref[block, tile]
            shard = source // blocks
            within = source - shard * blocks
            upper = within // half_blocks
            start = (shard ^ me) * lines + (within - upper * half_blocks) * block_len
            rows = held_ref[pl.ds(pl.multiple_of(start, block_len), block_len), :]
            picks.append(jnp.where(upper == 1, rows[:, channels:], rows[:, :channels]))
        mixed = product(tiles_ref[block], jnp.concatenate(picks, axis=0))
        trip_ref[block * block_len : (block + 1) * block_len, :] = mixed.astype(jnp.bfloat16)
    half_slots = send_ref.shape[0] // 2
    low = product(send_ref[:half_slots, :], trip_ref[...])
    high = product(send_ref[half_slots:, :], trip_ref[...])
    packed = jnp.concatenate([low, high], axis=1).astype(jnp.bfloat16)
    each = half_slots // len(out_refs)
    for at, out_ref in enumerate(out_refs):
        out_ref[...] = packed[at * each : (at + 1) * each, :]


def base_kernel(edges_ref, trip_ref, local_ref, up_ref, out_ref):
    channels = trip_ref.shape[1]
    for rows in row_chunks(edges_ref.shape[0]):
        picked = product(local_ref[rows, :], trip_ref[...]).astype(jnp.bfloat16)
        joined = product(trip_ref[rows, :], up_ref[0]) + product(picked, up_ref[1])
        out_ref[rows, :] = edges_ref[rows, :].astype(jnp.float32) + joined * root_half


def state_kernel(partners, *refs):
    base_ref, fetch_ref, up_ref, residual_ref, message_ref, index_ref = refs[:6]
    arrived = refs[6 : 6 + partners]
    state_ref, sums_ref, slots_ref = refs[6 + partners :]
    channels = up_ref.shape[1]
    each = arrived[0].shape[0]
    for at in range(partners):
        piece = arrived[at][...]
        slots_ref[at * each : (at + 1) * each, :] = piece[:, :channels]
        slots_ref[(partners + at) * each : (partners + at + 1) * each, :] = piece[:, channels:]
    part_atoms = sums_ref.shape[0]
    shards = lax.axis_size("edge")
    near = near_atoms(index_ref[1:2, :], part_atoms, shards)
    chosen = (
        lax.broadcasted_iota(jnp.int32, (part_atoms, near.shape[1]), 0) == near
    ).astype(jnp.bfloat16)
    chunks = row_chunks(base_ref.shape[0])
    gathered = None
    for first in range(0, len(chunks), 2):
        group = chunks[first : first + 2]
        picked = [product(fetch_ref[rows, :], slots_ref[...]).astype(jnp.bfloat16) for rows in group]
        states = [
            (base_ref[rows, :] + product(each, up_ref[1]) * root_half).astype(jnp.bfloat16)
            for rows, each in zip(group, picked)
        ]
        for layer in range(residual_ref.shape[0]):
            middles = [
                silu(product(each, residual_ref[layer, 0])).astype(jnp.bfloat16) for each in states
            ]
            branches = [silu(product(each, residual_ref[layer, 1])) for each in middles]
            states = [
                ((each.astype(jnp.float32) + branch) * root_half).astype(jnp.bfloat16)
                for each, branch in zip(states, branches)
            ]
        for rows, each in zip(group, states):
            state_ref[rows, :] = each
            term = product(chosen[:, rows], each)
            gathered = term if gathered is None else gathered + term
    sums_ref[...] = product(gathered.astype(jnp.bfloat16), message_ref[...]).astype(jnp.bfloat16)


def near_atoms(index, part_atoms, shards):
    count = part_atoms // shards
    holder = index // count
    return (holder ^ lax.axis_index("edge")) * count + lax.rem(index, count)


def side_kernel(shards, part_atoms, state_ref, join_ref, index_ref, out_ref, chosen_ref):
    width = join_ref.shape[0] - state_ref.shape[1]
    for rows in row_chunks(state_ref.shape[0]):
        out_ref[rows, :] = product(state_ref[rows, :], join_ref[width:, :])
    index = near_atoms(index_ref[...], part_atoms, shards)
    for end in range(2):
        column = as_column(index[end : end + 1, :])
        chosen_ref[:, end * part_atoms : (end + 1) * part_atoms] = (
            lax.broadcasted_iota(jnp.int32, (column.shape[0], part_atoms), 1) == column
        ).astype(jnp.bfloat16)


def final_kernel(shards, scale, *refs):
    sums = refs[:shards]
    atoms_ref, weight_ref, join_ref, state_ref, side_ref, chosen_ref = refs[shards : shards + 6]
    edges_hbm, own_hbm, table_ref, edges_ref, own_ref, sems = refs[shards + 6 :]
    part_atoms = atoms_ref.shape[0]
    count = part_atoms // shards
    total = sums[0][...].astype(jnp.float32)
    for by, part in list(zip(distances(shards), sums))[1:]:
        pieces = [part[(at ^ by) * count : ((at ^ by) + 1) * count, :] for at in range(shards)]
        total = total + jnp.concatenate(pieces, axis=0).astype(jnp.float32)
    scaled = (total * scale).astype(jnp.bfloat16)
    middle = silu(product(scaled, weight_ref[0])).astype(jnp.bfloat16)
    renewed = (atoms_ref[...].astype(jnp.float32) + product(middle, weight_ref[1])).astype(jnp.bfloat16)
    own_ref[...] = renewed[:count, :]
    own_copy = pltpu.make_async_copy(own_ref, own_hbm, sems.at[0])
    own_copy.start()
    width = renewed.shape[1]
    for end in range(2):
        table_ref[end * part_atoms : (end + 1) * part_atoms, :] = product(
            renewed, join_ref[end * width : (end + 1) * width, :]
        ).astype(jnp.bfloat16)
    copies = [own_copy]
    for at, rows in enumerate(row_chunks(state_ref.shape[0])):
        update = silu(product(chosen_ref[rows, :], table_ref[...]) + side_ref[rows, :])
        state = state_ref[rows, :].astype(jnp.float32)
        edges_ref[rows, :] = ((state + update) * root_half).astype(jnp.bfloat16)
        copies.append(
            pltpu.make_async_copy(edges_ref.at[rows], edges_hbm.at[rows], sems.at[1 + at])
        )
        copies[-1].start()
    for copy in copies:
        copy.wait()


def distances(shards):
    return [0, 1, 3, 2] if shards == 4 else list(range(shards))


def from_others(value, shards):
    return [value] + [
        lax.ppermute(value, "edge", [(at, at ^ by) for at in range(shards)])
        for by in distances(shards)[1:]
    ]


def body(
    edges,
    atoms,
    reverse,
    atom_index,
    tile_source,
    tiles,
    weight_edge,
    weight_down,
    weight_up,
    weight_residual,
    weight_message,
    weight_atom,
    weight_join,
):
    rows, wide = edges.shape
    channels = weight_down.shape[0]
    domains = lax.axis_size("dom")
    shards = lax.axis_size("edge")
    count, atom_wide = atoms.shape
    part_atoms = count * shards
    capacity = rows // domains
    partners = domains - 1
    slots = partners * capacity
    lines = rows // 2
    packed = 2 * channels

    narrow = call(
        narrow_kernel,
        shaped((lines + count * atom_wide // packed, packed)),
        (edges, weight_edge, weight_down, atoms),
        hbm=(0, 1, 2, 3),
        scratch=[
            pltpu.VMEM(edges.shape, jnp.bfloat16),
            pltpu.VMEM(weight_edge.shape, jnp.bfloat16),
            pltpu.VMEM(weight_down.shape, jnp.bfloat16),
            pltpu.SemaphoreType.DMA((2 + 2 * len(row_chunks(lines)) + atom_wide // packed,)),
        ],
        flops=2 * rows * wide * (wide + channels),
        nbytes=2 * (rows * wide + wide * wide),
    )
    narrow_parts = from_others(narrow, shards)
    later = (
        edges, tiles, weight_up, weight_residual, weight_message, weight_join, weight_atom, atom_index
    )
    send, fetch, local, *later = call(
        functools.partial(index_kernel, domains, shards, len(later)),
        (shaped((slots, rows)), shaped((rows, slots)), shaped((rows, rows)))
        + tuple(shaped(each.shape, each.dtype) for each in later),
        (reverse.reshape(1, rows), *later),
        hbm=range(1, 1 + len(later)),
        scratch=[pltpu.SemaphoreType.DMA((len(later),))],
        flops=40 * rows * rows,
        nbytes=6 * rows * rows,
    )
    edges, tiles, weight_up, weight_residual, weight_message, weight_join, weight_atom, atom_index = later
    trip_out, all_atoms, *outgoing = call(
        functools.partial(mix_kernel, shards),
        (shaped((rows, channels)), shaped((part_atoms, atom_wide)))
        + (shaped((capacity // 2, packed)),) * partners,
        (tile_source, tiles, *narrow_parts, send),
        smem=(0,),
        scratch=[pltpu.VMEM((shards * lines, packed), jnp.bfloat16)],
        flops=2 * rows * rows * channels,
        nbytes=2 * rows * rows,
    )
    arrived = [
        lax.ppermute(block, "dom", [(at, at ^ (partners - place)) for at in range(domains)])
        for place, block in enumerate(outgoing)
    ]
    base = call(
        base_kernel,
        shaped((rows, wide), jnp.float32),
        (edges, trip_out, local, weight_up),
        flops=2 * rows * channels * (rows + 2 * wide),
        nbytes=2 * rows * rows + 6 * rows * wide,
    )
    state, sums = call(
        functools.partial(state_kernel, partners),
        (shaped((rows, wide)), shaped((part_atoms, atom_wide))),
        (base, fetch, weight_up, weight_residual, weight_message, atom_index, *arrived),
        scratch=[pltpu.VMEM((slots, channels), jnp.bfloat16)],
        flops=4 * rows * wide * wide,
        nbytes=8 * rows * wide,
    )
    sums_parts = from_others(sums, shards)
    side, chosen = call(
        functools.partial(side_kernel, shards, part_atoms),
        (shaped((rows, wide), jnp.float32), shaped((rows, 2 * part_atoms))),
        (state, weight_join, atom_index),
        flops=2 * rows * wide * wide,
        nbytes=8 * rows * wide,
    )
    return call(
        functools.partial(final_kernel, shards, (rows // count) ** -0.5),
        (shaped((rows, wide), space=pltpu.HBM), shaped((count, atom_wide), space=pltpu.HBM)),
        (*sums_parts, all_atoms, weight_atom, weight_join, state, side, chosen),
        scratch=[
            pltpu.VMEM((2 * part_atoms, wide), jnp.bfloat16),
            pltpu.VMEM((rows, wide), jnp.bfloat16),
            pltpu.VMEM((count, atom_wide), jnp.bfloat16),
            pltpu.SemaphoreType.DMA((1 + len(row_chunks(rows)),)),
        ],
        flops=4 * rows * part_atoms * wide,
        nbytes=8 * rows * wide,
    )


def solution(mesh):
    split = P(("dom", "edge"))
    placed = (
        P(("dom", "edge"), None),
        P(("dom", "edge"), None),
        split,
        P(None, ("dom", "edge")),
        P(("dom", "edge"), None),
        P(("dom", "edge"), None, None),
    ) + (P(),) * 7
    return jax.shard_map(
        body,
        mesh=mesh,
        in_specs=placed,
        out_specs=(P(("dom", "edge"), None), P(("dom", "edge"), None)),
        check_vma=False,
    )
```

```python
import functools

import jax
import jax.numpy as jnp
from jax import lax
from jax.experimental import pallas as pl
from jax.experimental.pallas import tpu as pltpu
from jax.sharding import PartitionSpec as P

root_half = 0.7071067811865476
MIB = 1 << 20
CHUNK = 256


def product(operand, weights):
    return jnp.dot(operand, weights, preferred_element_type=jnp.float32)


def silu(value):
    halved = 0.5 * value
    return halved + halved * jnp.tanh(halved)


def as_column(row):
    wide = jnp.broadcast_to(row.astype(jnp.float32), (8, row.shape[1]))
    return jnp.transpose(wide)[:, :1].astype(jnp.int32)


def row_chunks(rows):
    step = min(CHUNK, rows)
    return [slice(at, at + step) for at in range(0, rows, step)]


def call(kernel, outs, args, *, smem=(), hbm=(), scratch=(), flops=0, nbytes=0, limit=24):
    def space(at):
        return pltpu.SMEM if at in smem else pltpu.HBM if at in hbm else pltpu.VMEM

    args = [
        pltpu.with_memory_space_constraint(arg, pltpu.HBM) if at in hbm else arg
        for at, arg in enumerate(args)
    ]
    return pl.pallas_call(
        kernel,
        out_shape=outs,
        in_specs=[pl.BlockSpec(memory_space=space(at)) for at in range(len(args))],
        out_specs=jax.tree.map(
            lambda out: pl.BlockSpec(
                memory_space=pltpu.HBM if out.memory_space == pltpu.HBM else pltpu.VMEM
            ),
            outs,
        ),
        scratch_shapes=list(scratch),
        compiler_params=pltpu.CompilerParams(vmem_limit_bytes=limit * MIB),
        cost_estimate=pl.CostEstimate(flops=flops, bytes_accessed=nbytes, transcendentals=0),
    )(*args)


def shaped(shape, dtype=jnp.bfloat16, space=pltpu.VMEM):
    return space(tuple(shape), dtype)


def narrow_kernel(
    edges_hbm, weight_hbm, down_hbm, atoms_hbm, out_ref, edges_ref, weight_ref, down_ref, sems
):
    half = edges_hbm.shape[0] // 2
    pieces = [
        slice(base + rows.start, base + rows.stop)
        for rows in row_chunks(half)
        for base in (0, half)
    ]
    copies = [
        pltpu.make_async_copy(weight_hbm, weight_ref, sems.at[0]),
        pltpu.make_async_copy(down_hbm, down_ref, sems.at[1]),
    ] + [
        pltpu.make_async_copy(edges_hbm.at[piece], edges_ref.at[piece], sems.at[2 + at])
        for at, piece in enumerate(pieces)
    ]
    for copy in [copies[0], copies[2], copies[3], copies[1]] + copies[4:]:
        copy.start()
    count, wide = atoms_hbm.shape
    lanes = out_ref.shape[1]
    atom_copies = [
        pltpu.make_async_copy(
            atoms_hbm.at[:, at * lanes : (at + 1) * lanes],
            out_ref.at[half + at * count : half + (at + 1) * count, :],
            sems.at[len(copies) + at],
        )
        for at in range(wide // lanes)
    ]
    for copy in atom_copies:
        copy.start()
    copies[0].wait()
    copies[1].wait()
    for at, rows in enumerate(row_chunks(half)):
        copies[2 + 2 * at].wait()
        copies[3 + 2 * at].wait()
        sides = []
        for side in range(2):
            hidden = silu(product(edges_ref[pieces[2 * at + side], :], weight_ref[...]))
            sides.append(
                silu(
                    lax.dot_general(
                        hidden.astype(jnp.bfloat16),
                        down_ref[...],
                        (((1,), (1,)), ((), ())),
                        preferred_element_type=jnp.float32,
                    )
                )
            )
        out_ref[rows, :] = jnp.concatenate(sides, axis=1).astype(jnp.bfloat16)
    for copy in atom_copies:
        copy.wait()


def index_kernel(domains, shards, operands, *refs):
    reverse_ref = refs[0]
    sources = refs[1 : 1 + operands]
    send_ref, fetch_ref, local_ref = refs[1 + operands : 4 + operands]
    targets = refs[4 + operands : 4 + 2 * operands]
    sems = refs[-1]
    copies = [
        pltpu.make_async_copy(source, target, sems.at[at])
        for at, (source, target) in enumerate(zip(sources, targets))
    ]
    for copy in copies:
        copy.start()
    rows = reverse_ref.shape[1]
    capacity = rows // domains
    half = capacity // 2
    slots = (domains - 1) * capacity
    own = lax.axis_index("dom")
    reverse = reverse_ref[...]
    holder = reverse // (rows * shards)
    source_row = lax.rem(reverse, rows)
    partner = holder ^ own
    source_column = as_column(source_row)
    member = (lax.broadcasted_iota(jnp.int32, (domains, rows), 0) == partner).astype(jnp.bfloat16)
    before = (
        lax.broadcasted_iota(jnp.int32, (rows, rows), 0)
        < lax.broadcasted_iota(jnp.int32, (rows, rows), 1)
    ).astype(jnp.bfloat16)
    place = jnp.sum(
        product(member, before) * member.astype(jnp.float32), axis=0, keepdims=True
    ).astype(jnp.int32)
    earlier = (source_column < source_row).astype(jnp.bfloat16)
    far_place = jnp.sum(
        product(member, earlier) * member.astype(jnp.float32), axis=0, keepdims=True
    ).astype(jnp.int32)

    def slot_of(at):
        part = (at >= half).astype(jnp.int32)
        slot = part * (slots // 2) + (domains - 1 - partner) * half + at - part * half
        return jnp.where(partner == 0, -1, slot)

    send_slot = slot_of(place)
    send_ref[...] = (
        lax.broadcasted_iota(jnp.int32, (slots, rows), 0) == send_slot
    ).astype(jnp.bfloat16)
    fetch_column = as_column(slot_of(far_place))
    fetch_ref[...] = (
        lax.broadcasted_iota(jnp.int32, (rows, slots), 1) == fetch_column
    ).astype(jnp.bfloat16)
    local_column = as_column(jnp.where(partner == 0, source_row, -1))
    local_ref[...] = (
        lax.broadcasted_iota(jnp.int32, (rows, rows), 1) == local_column
    ).astype(jnp.bfloat16)
    for copy in copies:
        copy.wait()


def mix_kernel(shards, count_parts, *refs):
    source_ref, tiles_ref = refs[:2]
    parts = refs[2 : 2 + count_parts]
    send_ref, trip_ref, atoms_ref = refs[2 + count_parts : 5 + count_parts]
    out_refs = refs[5 + count_parts : -1]
    held_ref = refs[-1]
    blocks, block_len, width = tiles_ref.shape
    count = width // block_len
    lines = held_ref.shape[0] // shards
    own_atoms = atoms_ref.shape[0] // shards
    atom_wide = atoms_ref.shape[1]
    lanes = held_ref.shape[1]
    me = lax.axis_index("edge")

    def keep(part, at):
        held_ref[at * lines : (at + 1) * lines, :] = part[:lines, :]
        for piece in range(atom_wide // lanes):
            start = lines + piece * own_atoms
            atoms_ref[
                at * own_atoms : (at + 1) * own_atoms, piece * lanes : (piece + 1) * lanes
            ] = part[start : start + own_atoms, :]

    if count_parts == shards:
        for part, at in zip(parts, distances(shards)):
            keep(part, at)
    else:
        for at in range(shards - 1):
            keep(parts[at], at)
        inner = (me > 0) & (me < shards - 1)
        pl.when(inner)(lambda: keep(parts[shards - 1], shards - 1))
        pl.when(jnp.logical_not(inner))(lambda: keep(parts[shards], shards - 1))
    half_blocks = blocks // 2
    channels = trip_ref.shape[1]
    for block in range(blocks):
        picks = []
        for tile in range(count):
            source = source_ref[block, tile]
            shard = source // blocks
            within = source - shard * blocks
            upper = within // half_blocks
            start = (shard ^ me) * lines + (within - upper * half_blocks) * block_len
            rows = held_ref[pl.ds(pl.multiple_of(start, block_len), block_len), :]
            picks.append(jnp.where(upper == 1, rows[:, channels:], rows[:, :channels]))
        mixed = product(tiles_ref[block], jnp.concatenate(picks, axis=0))
        trip_ref[block * block_len : (block + 1) * block_len, :] = mixed.astype(jnp.bfloat16)
    half_slots = send_ref.shape[0] // 2
    low = product(send_ref[:half_slots, :], trip_ref[...])
    high = product(send_ref[half_slots:, :], trip_ref[...])
    packed = jnp.concatenate([low, high], axis=1).astype(jnp.bfloat16)
    each = half_slots // len(out_refs)
    for at, out_ref in enumerate(out_refs):
        out_ref[...] = packed[at * each : (at + 1) * each, :]


def base_kernel(edges_ref, trip_ref, local_ref, up_ref, out_ref):
    channels = trip_ref.shape[1]
    for rows in row_chunks(edges_ref.shape[0]):
        picked = product(local_ref[rows, :], trip_ref[...]).astype(jnp.bfloat16)
        joined = product(trip_ref[rows, :], up_ref[0]) + product(picked, up_ref[1])
        out_ref[rows, :] = edges_ref[rows, :].astype(jnp.float32) + joined * root_half


def state_kernel(partners, *refs):
    base_ref, fetch_ref, up_ref, residual_ref, message_ref, index_ref = refs[:6]
    arrived = refs[6 : 6 + partners]
    state_ref, sums_ref, slots_ref = refs[6 + partners :]
    channels = up_ref.shape[1]
    each = arrived[0].shape[0]
    for at in range(partners):
        piece = arrived[at][...]
        slots_ref[at * each : (at + 1) * each, :] = piece[:, :channels]
        slots_ref[(partners + at) * each : (partners + at + 1) * each, :] = piece[:, channels:]
    part_atoms = sums_ref.shape[0]
    shards = lax.axis_size("edge")
    near = near_atoms(index_ref[1:2, :], part_atoms, shards)
    chosen = (
        lax.broadcasted_iota(jnp.int32, (part_atoms, near.shape[1]), 0) == near
    ).astype(jnp.bfloat16)
    chunks = row_chunks(base_ref.shape[0])
    gathered = None
    for first in range(0, len(chunks), 2):
        group = chunks[first : first + 2]
        picked = [product(fetch_ref[rows, :], slots_ref[...]).astype(jnp.bfloat16) for rows in group]
        states = [
            (base_ref[rows, :] + product(each, up_ref[1]) * root_half).astype(jnp.bfloat16)
            for rows, each in zip(group, picked)
        ]
        for layer in range(residual_ref.shape[0]):
            middles = [
                silu(product(each, residual_ref[layer, 0])).astype(jnp.bfloat16) for each in states
            ]
            branches = [silu(product(each, residual_ref[layer, 1])) for each in middles]
            states = [
                ((each.astype(jnp.float32) + branch) * root_half).astype(jnp.bfloat16)
                for each, branch in zip(states, branches)
            ]
        for rows, each in zip(group, states):
            state_ref[rows, :] = each
            term = product(chosen[:, rows], each)
            gathered = term if gathered is None else gathered + term
    sums_ref[...] = product(gathered.astype(jnp.bfloat16), message_ref[...]).astype(jnp.bfloat16)


def near_atoms(index, part_atoms, shards):
    count = part_atoms // shards
    holder = index // count
    return (holder ^ lax.axis_index("edge")) * count + lax.rem(index, count)


def side_kernel(shards, part_atoms, state_ref, join_ref, index_ref, out_ref, chosen_ref):
    width = join_ref.shape[0] - state_ref.shape[1]
    for rows in row_chunks(state_ref.shape[0]):
        out_ref[rows, :] = product(state_ref[rows, :], join_ref[width:, :])
    index = near_atoms(index_ref[...], part_atoms, shards)
    for end in range(2):
        column = as_column(index[end : end + 1, :])
        chosen_ref[:, end * part_atoms : (end + 1) * part_atoms] = (
            lax.broadcasted_iota(jnp.int32, (column.shape[0], part_atoms), 1) == column
        ).astype(jnp.bfloat16)


def final_kernel(shards, scale, *refs):
    sums = refs[:shards]
    atoms_ref, weight_ref, join_ref, state_ref, side_ref, chosen_ref = refs[shards : shards + 6]
    edges_hbm, own_hbm, table_ref, edges_ref, own_ref, sems = refs[shards + 6 :]
    part_atoms = atoms_ref.shape[0]
    count = part_atoms // shards
    total = sums[0][...].astype(jnp.float32)
    for by, part in list(zip(distances(shards), sums))[1:]:
        pieces = [part[(at ^ by) * count : ((at ^ by) + 1) * count, :] for at in range(shards)]
        total = total + jnp.concatenate(pieces, axis=0).astype(jnp.float32)
    scaled = (total * scale).astype(jnp.bfloat16)
    middle = silu(product(scaled, weight_ref[0])).astype(jnp.bfloat16)
    renewed = (atoms_ref[...].astype(jnp.float32) + product(middle, weight_ref[1])).astype(jnp.bfloat16)
    own_ref[...] = renewed[:count, :]
    own_copy = pltpu.make_async_copy(own_ref, own_hbm, sems.at[0])
    own_copy.start()
    width = renewed.shape[1]
    for end in range(2):
        table_ref[end * part_atoms : (end + 1) * part_atoms, :] = product(
            renewed, join_ref[end * width : (end + 1) * width, :]
        ).astype(jnp.bfloat16)
    copies = [own_copy]
    for at, rows in enumerate(row_chunks(state_ref.shape[0])):
        update = silu(product(chosen_ref[rows, :], table_ref[...]) + side_ref[rows, :])
        state = state_ref[rows, :].astype(jnp.float32)
        edges_ref[rows, :] = ((state + update) * root_half).astype(jnp.bfloat16)
        copies.append(
            pltpu.make_async_copy(edges_ref.at[rows], edges_hbm.at[rows], sems.at[1 + at])
        )
        copies[-1].start()
    for copy in copies:
        copy.wait()


def distances(shards):
    return [0, 1, 3, 2] if shards == 4 else list(range(shards))


def from_others(value, shards):
    return [value] + [
        lax.ppermute(value, "edge", [(at, at ^ by) for at in range(shards)])
        for by in distances(shards)[1:]
    ]


def by_relay(value, shards, between):
    if shards != 4:
        return from_others(value, shards), between()
    near = lax.ppermute(value, "edge", [(at, at ^ 1) for at in range(4)])
    far = lax.ppermute(value, "edge", [(at, at ^ 2) for at in range(4)])
    others = between()
    held, *others = lax.optimization_barrier((value, *others))
    middle = lax.ppermute(held, "edge", [(1, 2), (2, 1)])
    relayed = lax.ppermute(far, "edge", [(2, 3), (1, 0)])
    return [value, near, far, middle, relayed], others


def body(
    edges,
    atoms,
    reverse,
    atom_index,
    tile_source,
    tiles,
    weight_edge,
    weight_down,
    weight_up,
    weight_residual,
    weight_message,
    weight_atom,
    weight_join,
):
    rows, wide = edges.shape
    channels = weight_down.shape[0]
    domains = lax.axis_size("dom")
    shards = lax.axis_size("edge")
    count, atom_wide = atoms.shape
    part_atoms = count * shards
    capacity = rows // domains
    partners = domains - 1
    slots = partners * capacity
    lines = rows // 2
    packed = 2 * channels

    narrow = call(
        narrow_kernel,
        shaped((lines + count * atom_wide // packed, packed)),
        (edges, weight_edge, weight_down, atoms),
        hbm=(0, 1, 2, 3),
        scratch=[
            pltpu.VMEM(edges.shape, jnp.bfloat16),
            pltpu.VMEM(weight_edge.shape, jnp.bfloat16),
            pltpu.VMEM(weight_down.shape, jnp.bfloat16),
            pltpu.SemaphoreType.DMA((2 + 2 * len(row_chunks(lines)) + atom_wide // packed,)),
        ],
        flops=2 * rows * wide * (wide + channels),
        nbytes=2 * (rows * wide + wide * wide),
    )
    later = (
        edges, tiles, weight_up, weight_residual, weight_message, weight_join, weight_atom, atom_index
    )
    index_call = functools.partial(
        call,
        functools.partial(index_kernel, domains, shards, len(later)),
        (shaped((slots, rows)), shaped((rows, slots)), shaped((rows, rows)))
        + tuple(shaped(each.shape, each.dtype) for each in later),
        (reverse.reshape(1, rows), *later),
        hbm=range(1, 1 + len(later)),
        scratch=[pltpu.SemaphoreType.DMA((len(later),))],
        flops=40 * rows * rows,
        nbytes=6 * rows * rows,
    )
    narrow_parts, (send, fetch, local, *later) = by_relay(narrow, shards, index_call)
    edges, tiles, weight_up, weight_residual, weight_message, weight_join, weight_atom, atom_index = later
    trip_out, all_atoms, *outgoing = call(
        functools.partial(mix_kernel, shards, len(narrow_parts)),
        (shaped((rows, channels)), shaped((part_atoms, atom_wide)))
        + (shaped((capacity // 2, packed)),) * partners,
        (tile_source, tiles, *narrow_parts, send),
        smem=(0,),
        scratch=[pltpu.VMEM((shards * lines, packed), jnp.bfloat16)],
        flops=2 * rows * rows * channels,
        nbytes=2 * rows * rows,
    )
    arrived = [
        lax.ppermute(block, "dom", [(at, at ^ (partners - place)) for at in range(domains)])
        for place, block in enumerate(outgoing)
    ]
    base = call(
        base_kernel,
        shaped((rows, wide), jnp.float32),
        (edges, trip_out, local, weight_up),
        flops=2 * rows * channels * (rows + 2 * wide),
        nbytes=2 * rows * rows + 6 * rows * wide,
    )
    state, sums = call(
        functools.partial(state_kernel, partners),
        (shaped((rows, wide)), shaped((part_atoms, atom_wide))),
        (base, fetch, weight_up, weight_residual, weight_message, atom_index, *arrived),
        scratch=[pltpu.VMEM((slots, channels), jnp.bfloat16)],
        flops=4 * rows * wide * wide,
        nbytes=8 * rows * wide,
    )
    sums_parts = from_others(sums, shards)
    side, chosen = call(
        functools.partial(side_kernel, shards, part_atoms),
        (shaped((rows, wide), jnp.float32), shaped((rows, 2 * part_atoms))),
        (state, weight_join, atom_index),
        flops=2 * rows * wide * wide,
        nbytes=8 * rows * wide,
    )
    return call(
        functools.partial(final_kernel, shards, (rows // count) ** -0.5),
        (shaped((rows, wide), space=pltpu.HBM), shaped((count, atom_wide), space=pltpu.HBM)),
        (*sums_parts, all_atoms, weight_atom, weight_join, state, side, chosen),
        scratch=[
            pltpu.VMEM((2 * part_atoms, wide), jnp.bfloat16),
            pltpu.VMEM((rows, wide), jnp.bfloat16),
            pltpu.VMEM((count, atom_wide), jnp.bfloat16),
            pltpu.SemaphoreType.DMA((1 + len(row_chunks(rows)),)),
        ],
        flops=4 * rows * part_atoms * wide,
        nbytes=8 * rows * wide,
    )


def solution(mesh):
    split = P(("dom", "edge"))
    placed = (
        P(("dom", "edge"), None),
        P(("dom", "edge"), None),
        split,
        P(None, ("dom", "edge")),
        P(("dom", "edge"), None),
        P(("dom", "edge"), None, None),
    ) + (P(),) * 7
    return jax.shard_map(
        body,
        mesh=mesh,
        in_specs=placed,
        out_specs=(P(("dom", "edge"), None), P(("dom", "edge"), None)),
        check_vma=False,
    )
```

```python
import functools

import jax
import jax.numpy as jnp
from jax import lax
from jax.experimental import pallas as pl
from jax.experimental.pallas import tpu as pltpu
from jax.sharding import PartitionSpec as P

root_half = 0.7071067811865476
MIB = 1 << 20
CHUNK = 256


def product(operand, weights):
    return jnp.dot(operand, weights, preferred_element_type=jnp.float32)


def silu(value):
    halved = 0.5 * value
    return halved + halved * jnp.tanh(halved)


def as_column(row):
    wide = jnp.broadcast_to(row.astype(jnp.float32), (8, row.shape[1]))
    return jnp.transpose(wide)[:, :1].astype(jnp.int32)


def row_chunks(rows):
    step = min(CHUNK, rows)
    return [slice(at, at + step) for at in range(0, rows, step)]


def call(kernel, outs, args, *, smem=(), hbm=(), scratch=(), flops=0, nbytes=0, limit=24):
    def space(at):
        return pltpu.SMEM if at in smem else pltpu.HBM if at in hbm else pltpu.VMEM

    args = [
        pltpu.with_memory_space_constraint(arg, pltpu.HBM) if at in hbm else arg
        for at, arg in enumerate(args)
    ]
    return pl.pallas_call(
        kernel,
        out_shape=outs,
        in_specs=[pl.BlockSpec(memory_space=space(at)) for at in range(len(args))],
        out_specs=jax.tree.map(
            lambda out: pl.BlockSpec(
                memory_space=pltpu.HBM if out.memory_space == pltpu.HBM else pltpu.VMEM
            ),
            outs,
        ),
        scratch_shapes=list(scratch),
        compiler_params=pltpu.CompilerParams(vmem_limit_bytes=limit * MIB),
        cost_estimate=pl.CostEstimate(flops=flops, bytes_accessed=nbytes, transcendentals=0),
    )(*args)


def shaped(shape, dtype=jnp.bfloat16, space=pltpu.VMEM):
    return space(tuple(shape), dtype)


def narrow_kernel(
    edges_hbm, weight_hbm, down_hbm, atoms_hbm, out_ref, edges_ref, weight_ref, down_ref, sems
):
    half = edges_hbm.shape[0] // 2
    pieces = [
        slice(base + rows.start, base + rows.stop)
        for rows in row_chunks(half)
        for base in (0, half)
    ]
    copies = [
        pltpu.make_async_copy(weight_hbm, weight_ref, sems.at[0]),
        pltpu.make_async_copy(down_hbm, down_ref, sems.at[1]),
    ] + [
        pltpu.make_async_copy(edges_hbm.at[piece], edges_ref.at[piece], sems.at[2 + at])
        for at, piece in enumerate(pieces)
    ]
    for copy in [copies[0], copies[2], copies[3], copies[1]] + copies[4:]:
        copy.start()
    count, wide = atoms_hbm.shape
    lanes = out_ref.shape[1]
    atom_copies = [
        pltpu.make_async_copy(
            atoms_hbm.at[:, at * lanes : (at + 1) * lanes],
            out_ref.at[half + at * count : half + (at + 1) * count, :],
            sems.at[len(copies) + at],
        )
        for at in range(wide // lanes)
    ]
    for copy in atom_copies:
        copy.start()
    copies[0].wait()
    copies[1].wait()
    for at, rows in enumerate(row_chunks(half)):
        copies[2 + 2 * at].wait()
        copies[3 + 2 * at].wait()
        sides = []
        for side in range(2):
            hidden = silu(product(edges_ref[pieces[2 * at + side], :], weight_ref[...]))
            sides.append(
                silu(
                    lax.dot_general(
                        hidden.astype(jnp.bfloat16),
                        down_ref[...],
                        (((1,), (1,)), ((), ())),
                        preferred_element_type=jnp.float32,
                    )
                )
            )
        out_ref[rows, :] = jnp.concatenate(sides, axis=1).astype(jnp.bfloat16)
    for copy in atom_copies:
        copy.wait()


def index_kernel(domains, shards, operands, *refs):
    reverse_ref, narrow_ref = refs[:2]
    sources = refs[2 : 2 + operands]
    again_ref, send_ref, fetch_ref, local_ref = refs[2 + operands : 6 + operands]
    targets = refs[6 + operands : 6 + 2 * operands]
    sems = refs[-1]
    copies = [
        pltpu.make_async_copy(source, target, sems.at[at])
        for at, (source, target) in enumerate(zip(sources, targets))
    ]
    for copy in copies:
        copy.start()
    again_ref[...] = narrow_ref[...]
    rows = reverse_ref.shape[1]
    capacity = rows // domains
    half = capacity // 2
    slots = (domains - 1) * capacity
    own = lax.axis_index("dom")
    reverse = reverse_ref[...]
    holder = reverse // (rows * shards)
    source_row = lax.rem(reverse, rows)
    partner = holder ^ own
    source_column = as_column(source_row)
    member = (lax.broadcasted_iota(jnp.int32, (domains, rows), 0) == partner).astype(jnp.bfloat16)
    before = (
        lax.broadcasted_iota(jnp.int32, (rows, rows), 0)
        < lax.broadcasted_iota(jnp.int32, (rows, rows), 1)
    ).astype(jnp.bfloat16)
    place = jnp.sum(
        product(member, before) * member.astype(jnp.float32), axis=0, keepdims=True
    ).astype(jnp.int32)
    earlier = (source_column < source_row).astype(jnp.bfloat16)
    far_place = jnp.sum(
        product(member, earlier) * member.astype(jnp.float32), axis=0, keepdims=True
    ).astype(jnp.int32)

    def slot_of(at):
        part = (at >= half).astype(jnp.int32)
        slot = part * (slots // 2) + (domains - 1 - partner) * half + at - part * half
        return jnp.where(partner == 0, -1, slot)

    send_slot = slot_of(place)
    send_ref[...] = (
        lax.broadcasted_iota(jnp.int32, (slots, rows), 0) == send_slot
    ).astype(jnp.bfloat16)
    fetch_column = as_column(slot_of(far_place))
    fetch_ref[...] = (
        lax.broadcasted_iota(jnp.int32, (rows, slots), 1) == fetch_column
    ).astype(jnp.bfloat16)
    local_column = as_column(jnp.where(partner == 0, source_row, -1))
    local_ref[...] = (
        lax.broadcasted_iota(jnp.int32, (rows, rows), 1) == local_column
    ).astype(jnp.bfloat16)
    for copy in copies:
        copy.wait()


def mix_kernel(shards, count_parts, *refs):
    source_ref, tiles_ref = refs[:2]
    parts = refs[2 : 2 + count_parts]
    send_ref, trip_ref, atoms_ref = refs[2 + count_parts : 5 + count_parts]
    out_refs = refs[5 + count_parts : -1]
    held_ref = refs[-1]
    blocks, block_len, width = tiles_ref.shape
    count = width // block_len
    lines = held_ref.shape[0] // shards
    own_atoms = atoms_ref.shape[0] // shards
    atom_wide = atoms_ref.shape[1]
    lanes = held_ref.shape[1]
    me = lax.axis_index("edge")

    def keep(part, at):
        held_ref[at * lines : (at + 1) * lines, :] = part[:lines, :]
        for piece in range(atom_wide // lanes):
            start = lines + piece * own_atoms
            atoms_ref[
                at * own_atoms : (at + 1) * own_atoms, piece * lanes : (piece + 1) * lanes
            ] = part[start : start + own_atoms, :]

    if count_parts == shards:
        for part, at in zip(parts, distances(shards)):
            keep(part, at)
    else:
        for at in range(shards - 1):
            keep(parts[at], at)
        inner = (me > 0) & (me < shards - 1)
        pl.when(inner)(lambda: keep(parts[shards - 1], shards - 1))
        pl.when(jnp.logical_not(inner))(lambda: keep(parts[shards], shards - 1))
    half_blocks = blocks // 2
    channels = trip_ref.shape[1]
    for block in range(blocks):
        picks = []
        for tile in range(count):
            source = source_ref[block, tile]
            shard = source // blocks
            within = source - shard * blocks
            upper = within // half_blocks
            start = (shard ^ me) * lines + (within - upper * half_blocks) * block_len
            rows = held_ref[pl.ds(pl.multiple_of(start, block_len), block_len), :]
            picks.append(jnp.where(upper == 1, rows[:, channels:], rows[:, :channels]))
        mixed = product(tiles_ref[block], jnp.concatenate(picks, axis=0))
        trip_ref[block * block_len : (block + 1) * block_len, :] = mixed.astype(jnp.bfloat16)
    half_slots = send_ref.shape[0] // 2
    low = product(send_ref[:half_slots, :], trip_ref[...])
    high = product(send_ref[half_slots:, :], trip_ref[...])
    packed = jnp.concatenate([low, high], axis=1).astype(jnp.bfloat16)
    each = half_slots // len(out_refs)
    for at, out_ref in enumerate(out_refs):
        out_ref[...] = packed[at * each : (at + 1) * each, :]


def base_kernel(edges_ref, trip_ref, local_ref, up_ref, out_ref):
    channels = trip_ref.shape[1]
    for rows in row_chunks(edges_ref.shape[0]):
        picked = product(local_ref[rows, :], trip_ref[...]).astype(jnp.bfloat16)
        joined = product(trip_ref[rows, :], up_ref[0]) + product(picked, up_ref[1])
        out_ref[rows, :] = edges_ref[rows, :].astype(jnp.float32) + joined * root_half


def state_kernel(partners, *refs):
    base_ref, fetch_ref, up_ref, residual_ref, message_ref, index_ref = refs[:6]
    arrived = refs[6 : 6 + partners]
    state_ref, sums_ref, slots_ref = refs[6 + partners :]
    channels = up_ref.shape[1]
    each = arrived[0].shape[0]
    for at in range(partners):
        piece = arrived[at][...]
        slots_ref[at * each : (at + 1) * each, :] = piece[:, :channels]
        slots_ref[(partners + at) * each : (partners + at + 1) * each, :] = piece[:, channels:]
    part_atoms = sums_ref.shape[0]
    shards = lax.axis_size("edge")
    near = near_atoms(index_ref[1:2, :], part_atoms, shards)
    chosen = (
        lax.broadcasted_iota(jnp.int32, (part_atoms, near.shape[1]), 0) == near
    ).astype(jnp.bfloat16)
    chunks = row_chunks(base_ref.shape[0])
    gathered = None
    for first in range(0, len(chunks), 2):
        group = chunks[first : first + 2]
        picked = [product(fetch_ref[rows, :], slots_ref[...]).astype(jnp.bfloat16) for rows in group]
        states = [
            (base_ref[rows, :] + product(each, up_ref[1]) * root_half).astype(jnp.bfloat16)
            for rows, each in zip(group, picked)
        ]
        for layer in range(residual_ref.shape[0]):
            middles = [
                silu(product(each, residual_ref[layer, 0])).astype(jnp.bfloat16) for each in states
            ]
            branches = [silu(product(each, residual_ref[layer, 1])) for each in middles]
            states = [
                ((each.astype(jnp.float32) + branch) * root_half).astype(jnp.bfloat16)
                for each, branch in zip(states, branches)
            ]
        for rows, each in zip(group, states):
            state_ref[rows, :] = each
            term = product(chosen[:, rows], each)
            gathered = term if gathered is None else gathered + term
    sums_ref[...] = product(gathered.astype(jnp.bfloat16), message_ref[...]).astype(jnp.bfloat16)


def near_atoms(index, part_atoms, shards):
    count = part_atoms // shards
    holder = index // count
    return (holder ^ lax.axis_index("edge")) * count + lax.rem(index, count)


def side_kernel(shards, part_atoms, state_ref, join_ref, index_ref, out_ref, chosen_ref):
    width = join_ref.shape[0] - state_ref.shape[1]
    for rows in row_chunks(state_ref.shape[0]):
        out_ref[rows, :] = product(state_ref[rows, :], join_ref[width:, :])
    index = near_atoms(index_ref[...], part_atoms, shards)
    for end in range(2):
        column = as_column(index[end : end + 1, :])
        chosen_ref[:, end * part_atoms : (end + 1) * part_atoms] = (
            lax.broadcasted_iota(jnp.int32, (column.shape[0], part_atoms), 1) == column
        ).astype(jnp.bfloat16)


def final_kernel(shards, scale, *refs):
    sums = refs[:shards]
    atoms_ref, weight_ref, join_ref, state_ref, side_ref, chosen_ref = refs[shards : shards + 6]
    edges_hbm, own_hbm, table_ref, edges_ref, own_ref, sems = refs[shards + 6 :]
    part_atoms = atoms_ref.shape[0]
    count = part_atoms // shards
    total = sums[0][...].astype(jnp.float32)
    for by, part in list(zip(distances(shards), sums))[1:]:
        pieces = [part[(at ^ by) * count : ((at ^ by) + 1) * count, :] for at in range(shards)]
        total = total + jnp.concatenate(pieces, axis=0).astype(jnp.float32)
    scaled = (total * scale).astype(jnp.bfloat16)
    middle = silu(product(scaled, weight_ref[0])).astype(jnp.bfloat16)
    renewed = (atoms_ref[...].astype(jnp.float32) + product(middle, weight_ref[1])).astype(jnp.bfloat16)
    own_ref[...] = renewed[:count, :]
    own_copy = pltpu.make_async_copy(own_ref, own_hbm, sems.at[0])
    own_copy.start()
    width = renewed.shape[1]
    for end in range(2):
        table_ref[end * part_atoms : (end + 1) * part_atoms, :] = product(
            renewed, join_ref[end * width : (end + 1) * width, :]
        ).astype(jnp.bfloat16)
    copies = [own_copy]
    for at, rows in enumerate(row_chunks(state_ref.shape[0])):
        update = silu(product(chosen_ref[rows, :], table_ref[...]) + side_ref[rows, :])
        state = state_ref[rows, :].astype(jnp.float32)
        edges_ref[rows, :] = ((state + update) * root_half).astype(jnp.bfloat16)
        copies.append(
            pltpu.make_async_copy(edges_ref.at[rows], edges_hbm.at[rows], sems.at[1 + at])
        )
        copies[-1].start()
    for copy in copies:
        copy.wait()


def distances(shards):
    return [0, 1, 3, 2] if shards == 4 else list(range(shards))


def from_others(value, shards):
    return [value] + [
        lax.ppermute(value, "edge", [(at, at ^ by) for at in range(shards)])
        for by in distances(shards)[1:]
    ]


def by_relay(value, shards, between):
    if shards != 4:
        return from_others(value, shards), between(value)
    near = lax.ppermute(value, "edge", [(at, at ^ 1) for at in range(4)])
    far = lax.ppermute(value, "edge", [(at, at ^ 2) for at in range(4)])
    others = between(value)
    middle = lax.ppermute(others[0], "edge", [(1, 2), (2, 1)])
    relayed = lax.ppermute(far, "edge", [(2, 3), (1, 0)])
    return [value, near, far, middle, relayed], others


def body(
    edges,
    atoms,
    reverse,
    atom_index,
    tile_source,
    tiles,
    weight_edge,
    weight_down,
    weight_up,
    weight_residual,
    weight_message,
    weight_atom,
    weight_join,
):
    rows, wide = edges.shape
    channels = weight_down.shape[0]
    domains = lax.axis_size("dom")
    shards = lax.axis_size("edge")
    count, atom_wide = atoms.shape
    part_atoms = count * shards
    capacity = rows // domains
    partners = domains - 1
    slots = partners * capacity
    lines = rows // 2
    packed = 2 * channels

    narrow = call(
        narrow_kernel,
        shaped((lines + count * atom_wide // packed, packed)),
        (edges, weight_edge, weight_down, atoms),
        hbm=(0, 1, 2, 3),
        scratch=[
            pltpu.VMEM(edges.shape, jnp.bfloat16),
            pltpu.VMEM(weight_edge.shape, jnp.bfloat16),
            pltpu.VMEM(weight_down.shape, jnp.bfloat16),
            pltpu.SemaphoreType.DMA((2 + 2 * len(row_chunks(lines)) + atom_wide // packed,)),
        ],
        flops=2 * rows * wide * (wide + channels),
        nbytes=2 * (rows * wide + wide * wide),
    )
    later = (
        edges, tiles, weight_up, weight_residual, weight_message, weight_join, weight_atom, atom_index
    )
    def index_call(value):
        return call(
            functools.partial(index_kernel, domains, shards, len(later)),
            (
                shaped(value.shape),
                shaped((slots, rows)),
                shaped((rows, slots)),
                shaped((rows, rows)),
            )
            + tuple(shaped(each.shape, each.dtype) for each in later),
            (reverse.reshape(1, rows), value, *later),
            hbm=range(2, 2 + len(later)),
            scratch=[pltpu.SemaphoreType.DMA((len(later),))],
            flops=40 * rows * rows,
            nbytes=6 * rows * rows,
        )

    narrow_parts, (_, send, fetch, local, *later) = by_relay(narrow, shards, index_call)
    edges, tiles, weight_up, weight_residual, weight_message, weight_join, weight_atom, atom_index = later
    trip_out, all_atoms, *outgoing = call(
        functools.partial(mix_kernel, shards, len(narrow_parts)),
        (shaped((rows, channels)), shaped((part_atoms, atom_wide)))
        + (shaped((capacity // 2, packed)),) * partners,
        (tile_source, tiles, *narrow_parts, send),
        smem=(0,),
        scratch=[pltpu.VMEM((shards * lines, packed), jnp.bfloat16)],
        flops=2 * rows * rows * channels,
        nbytes=2 * rows * rows,
    )
    arrived = [
        lax.ppermute(block, "dom", [(at, at ^ (partners - place)) for at in range(domains)])
        for place, block in enumerate(outgoing)
    ]
    base = call(
        base_kernel,
        shaped((rows, wide), jnp.float32),
        (edges, trip_out, local, weight_up),
        flops=2 * rows * channels * (rows + 2 * wide),
        nbytes=2 * rows * rows + 6 * rows * wide,
    )
    state, sums = call(
        functools.partial(state_kernel, partners),
        (shaped((rows, wide)), shaped((part_atoms, atom_wide))),
        (base, fetch, weight_up, weight_residual, weight_message, atom_index, *arrived),
        scratch=[pltpu.VMEM((slots, channels), jnp.bfloat16)],
        flops=4 * rows * wide * wide,
        nbytes=8 * rows * wide,
    )
    sums_parts = from_others(sums, shards)
    side, chosen = call(
        functools.partial(side_kernel, shards, part_atoms),
        (shaped((rows, wide), jnp.float32), shaped((rows, 2 * part_atoms))),
        (state, weight_join, atom_index),
        flops=2 * rows * wide * wide,
        nbytes=8 * rows * wide,
    )
    return call(
        functools.partial(final_kernel, shards, (rows // count) ** -0.5),
        (shaped((rows, wide), space=pltpu.HBM), shaped((count, atom_wide), space=pltpu.HBM)),
        (*sums_parts, all_atoms, weight_atom, weight_join, state, side, chosen),
        scratch=[
            pltpu.VMEM((2 * part_atoms, wide), jnp.bfloat16),
            pltpu.VMEM((rows, wide), jnp.bfloat16),
            pltpu.VMEM((count, atom_wide), jnp.bfloat16),
            pltpu.SemaphoreType.DMA((1 + len(row_chunks(rows)),)),
        ],
        flops=4 * rows * part_atoms * wide,
        nbytes=8 * rows * wide,
    )


def solution(mesh):
    split = P(("dom", "edge"))
    placed = (
        P(("dom", "edge"), None),
        P(("dom", "edge"), None),
        split,
        P(None, ("dom", "edge")),
        P(("dom", "edge"), None),
        P(("dom", "edge"), None, None),
    ) + (P(),) * 7
    return jax.shard_map(
        body,
        mesh=mesh,
        in_specs=placed,
        out_specs=(P(("dom", "edge"), None), P(("dom", "edge"), None)),
        check_vma=False,
    )
```

```python
import functools

import jax
import jax.numpy as jnp
from jax import lax
from jax.experimental import pallas as pl
from jax.experimental.pallas import tpu as pltpu
from jax.sharding import PartitionSpec as P

root_half = 0.7071067811865476
MIB = 1 << 20
CHUNK = 256


def product(operand, weights):
    return jnp.dot(operand, weights, preferred_element_type=jnp.float32)


def silu(value):
    halved = 0.5 * value
    return halved + halved * jnp.tanh(halved)


def as_column(row):
    wide = jnp.broadcast_to(row.astype(jnp.float32), (8, row.shape[1]))
    return jnp.transpose(wide)[:, :1].astype(jnp.int32)


def row_chunks(rows):
    step = min(CHUNK, rows)
    return [slice(at, at + step) for at in range(0, rows, step)]


def call(kernel, outs, args, *, smem=(), hbm=(), scratch=(), flops=0, nbytes=0, limit=24):
    def space(at):
        return pltpu.SMEM if at in smem else pltpu.HBM if at in hbm else pltpu.VMEM

    args = [
        pltpu.with_memory_space_constraint(arg, pltpu.HBM) if at in hbm else arg
        for at, arg in enumerate(args)
    ]
    return pl.pallas_call(
        kernel,
        out_shape=outs,
        in_specs=[pl.BlockSpec(memory_space=space(at)) for at in range(len(args))],
        out_specs=jax.tree.map(
            lambda out: pl.BlockSpec(
                memory_space=pltpu.HBM if out.memory_space == pltpu.HBM else pltpu.VMEM
            ),
            outs,
        ),
        scratch_shapes=list(scratch),
        compiler_params=pltpu.CompilerParams(vmem_limit_bytes=limit * MIB),
        cost_estimate=pl.CostEstimate(flops=flops, bytes_accessed=nbytes, transcendentals=0),
    )(*args)


def shaped(shape, dtype=jnp.bfloat16, space=pltpu.VMEM):
    return space(tuple(shape), dtype)


def narrow_kernel(
    edges_hbm, weight_hbm, down_hbm, atoms_hbm, out_ref, edges_ref, weight_ref, down_ref, sems
):
    half = edges_hbm.shape[0] // 2
    pieces = [
        slice(base + rows.start, base + rows.stop)
        for rows in row_chunks(half)
        for base in (0, half)
    ]
    copies = [
        pltpu.make_async_copy(weight_hbm, weight_ref, sems.at[0]),
        pltpu.make_async_copy(down_hbm, down_ref, sems.at[1]),
    ] + [
        pltpu.make_async_copy(edges_hbm.at[piece], edges_ref.at[piece], sems.at[2 + at])
        for at, piece in enumerate(pieces)
    ]
    for copy in [copies[0], copies[2], copies[3], copies[1]] + copies[4:]:
        copy.start()
    count, wide = atoms_hbm.shape
    lanes = out_ref.shape[1]
    atom_copies = [
        pltpu.make_async_copy(
            atoms_hbm.at[:, at * lanes : (at + 1) * lanes],
            out_ref.at[half + at * count : half + (at + 1) * count, :],
            sems.at[len(copies) + at],
        )
        for at in range(wide // lanes)
    ]
    for copy in atom_copies:
        copy.start()
    copies[0].wait()
    copies[1].wait()
    for at, rows in enumerate(row_chunks(half)):
        copies[2 + 2 * at].wait()
        copies[3 + 2 * at].wait()
        sides = []
        for side in range(2):
            hidden = silu(product(edges_ref[pieces[2 * at + side], :], weight_ref[...]))
            sides.append(
                silu(
                    lax.dot_general(
                        hidden.astype(jnp.bfloat16),
                        down_ref[...],
                        (((1,), (1,)), ((), ())),
                        preferred_element_type=jnp.float32,
                    )
                )
            )
        out_ref[rows, :] = jnp.concatenate(sides, axis=1).astype(jnp.bfloat16)
    for copy in atom_copies:
        copy.wait()


def index_kernel(domains, shards, operands, *refs):
    reverse_ref, narrow_ref = refs[:2]
    sources = refs[2 : 2 + operands]
    again_ref, send_ref, fetch_ref, local_ref = refs[2 + operands : 6 + operands]
    targets = refs[6 + operands : 6 + 2 * operands]
    sems = refs[-1]
    copies = [
        pltpu.make_async_copy(source, target, sems.at[at])
        for at, (source, target) in enumerate(zip(sources, targets))
    ]
    for copy in copies:
        copy.start()
    again_ref[...] = narrow_ref[...]
    rows = reverse_ref.shape[1]
    capacity = rows // domains
    half = capacity // 2
    slots = (domains - 1) * capacity
    own = lax.axis_index("dom")
    reverse = reverse_ref[...]
    holder = reverse // (rows * shards)
    source_row = lax.rem(reverse, rows)
    partner = holder ^ own
    source_column = as_column(source_row)
    member = (lax.broadcasted_iota(jnp.int32, (domains, rows), 0) == partner).astype(jnp.bfloat16)
    before = (
        lax.broadcasted_iota(jnp.int32, (rows, rows), 0)
        < lax.broadcasted_iota(jnp.int32, (rows, rows), 1)
    ).astype(jnp.bfloat16)
    place = jnp.sum(
        product(member, before) * member.astype(jnp.float32), axis=0, keepdims=True
    ).astype(jnp.int32)
    earlier = (source_column < source_row).astype(jnp.bfloat16)
    far_place = jnp.sum(
        product(member, earlier) * member.astype(jnp.float32), axis=0, keepdims=True
    ).astype(jnp.int32)

    def slot_of(at):
        part = (at >= half).astype(jnp.int32)
        slot = part * (slots // 2) + (domains - 1 - partner) * half + at - part * half
        return jnp.where(partner == 0, -1, slot)

    send_slot = slot_of(place)
    send_ref[...] = (
        lax.broadcasted_iota(jnp.int32, (slots, rows), 0) == send_slot
    ).astype(jnp.bfloat16)
    fetch_column = as_column(slot_of(far_place))
    fetch_ref[...] = (
        lax.broadcasted_iota(jnp.int32, (rows, slots), 1) == fetch_column
    ).astype(jnp.bfloat16)
    local_column = as_column(jnp.where(partner == 0, source_row, -1))
    local_ref[...] = (
        lax.broadcasted_iota(jnp.int32, (rows, rows), 1) == local_column
    ).astype(jnp.bfloat16)
    for copy in copies:
        copy.wait()


def mix_kernel(shards, count_parts, *refs):
    source_ref, tiles_ref = refs[:2]
    parts = refs[2 : 2 + count_parts]
    send_ref, trip_ref, atoms_ref = refs[2 + count_parts : 5 + count_parts]
    out_refs = refs[5 + count_parts : -1]
    held_ref = refs[-1]
    blocks, block_len, width = tiles_ref.shape
    count = width // block_len
    lines = held_ref.shape[0] // shards
    own_atoms = atoms_ref.shape[0] // shards
    atom_wide = atoms_ref.shape[1]
    lanes = held_ref.shape[1]
    me = lax.axis_index("edge")

    def keep(part, at):
        held_ref[at * lines : (at + 1) * lines, :] = part[:lines, :]
        for piece in range(atom_wide // lanes):
            start = lines + piece * own_atoms
            atoms_ref[
                at * own_atoms : (at + 1) * own_atoms, piece * lanes : (piece + 1) * lanes
            ] = part[start : start + own_atoms, :]

    if count_parts == shards:
        for part, at in zip(parts, distances(shards)):
            keep(part, at)
    else:
        for at in range(shards - 1):
            keep(parts[at], at)
        inner = (me > 0) & (me < shards - 1)
        pl.when(inner)(lambda: keep(parts[shards - 1], shards - 1))
        pl.when(jnp.logical_not(inner))(lambda: keep(parts[shards], shards - 1))
    half_blocks = blocks // 2
    channels = trip_ref.shape[1]
    for block in range(blocks):
        picks = []
        for tile in range(count):
            source = source_ref[block, tile]
            shard = source // blocks
            within = source - shard * blocks
            upper = within // half_blocks
            start = (shard ^ me) * lines + (within - upper * half_blocks) * block_len
            rows = held_ref[pl.ds(pl.multiple_of(start, block_len), block_len), :]
            picks.append(jnp.where(upper == 1, rows[:, channels:], rows[:, :channels]))
        mixed = product(tiles_ref[block], jnp.concatenate(picks, axis=0))
        trip_ref[block * block_len : (block + 1) * block_len, :] = mixed.astype(jnp.bfloat16)
    half_slots = send_ref.shape[0] // 2
    low = product(send_ref[:half_slots, :], trip_ref[...])
    high = product(send_ref[half_slots:, :], trip_ref[...])
    packed = jnp.concatenate([low, high], axis=1).astype(jnp.bfloat16)
    each = half_slots // len(out_refs)
    for at, out_ref in enumerate(out_refs):
        out_ref[...] = packed[at * each : (at + 1) * each, :]


def base_kernel(edges_ref, trip_ref, local_ref, up_ref, out_ref):
    channels = trip_ref.shape[1]
    for rows in row_chunks(edges_ref.shape[0]):
        picked = product(local_ref[rows, :], trip_ref[...]).astype(jnp.bfloat16)
        joined = product(trip_ref[rows, :], up_ref[0]) + product(picked, up_ref[1])
        out_ref[rows, :] = edges_ref[rows, :].astype(jnp.float32) + joined * root_half


def state_kernel(partners, *refs):
    base_ref, fetch_ref, up_ref, residual_ref, message_ref, index_ref = refs[:6]
    arrived = refs[6 : 6 + partners]
    state_ref, sums_ref, slots_ref = refs[6 + partners :]
    channels = up_ref.shape[1]
    each = arrived[0].shape[0]
    for at in range(partners):
        piece = arrived[at][...]
        slots_ref[at * each : (at + 1) * each, :] = piece[:, :channels]
        slots_ref[(partners + at) * each : (partners + at + 1) * each, :] = piece[:, channels:]
    part_atoms = sums_ref.shape[0]
    shards = lax.axis_size("edge")
    near = near_atoms(index_ref[1:2, :], part_atoms, shards)
    chosen = (
        lax.broadcasted_iota(jnp.int32, (part_atoms, near.shape[1]), 0) == near
    ).astype(jnp.bfloat16)
    chunks = row_chunks(base_ref.shape[0])
    gathered = None
    for first in range(0, len(chunks), 2):
        group = chunks[first : first + 2]
        picked = [product(fetch_ref[rows, :], slots_ref[...]).astype(jnp.bfloat16) for rows in group]
        states = [
            (base_ref[rows, :] + product(each, up_ref[1]) * root_half).astype(jnp.bfloat16)
            for rows, each in zip(group, picked)
        ]
        for layer in range(residual_ref.shape[0]):
            middles = [
                silu(product(each, residual_ref[layer, 0])).astype(jnp.bfloat16) for each in states
            ]
            branches = [silu(product(each, residual_ref[layer, 1])) for each in middles]
            states = [
                ((each.astype(jnp.float32) + branch) * root_half).astype(jnp.bfloat16)
                for each, branch in zip(states, branches)
            ]
        for rows, each in zip(group, states):
            state_ref[rows, :] = each
            term = product(chosen[:, rows], each)
            gathered = term if gathered is None else gathered + term
    sums_ref[...] = product(gathered.astype(jnp.bfloat16), message_ref[...]).astype(jnp.bfloat16)


def near_atoms(index, part_atoms, shards):
    count = part_atoms // shards
    holder = index // count
    return (holder ^ lax.axis_index("edge")) * count + lax.rem(index, count)


def side_kernel(shards, part_atoms, state_ref, join_ref, index_ref, out_ref, chosen_ref):
    width = join_ref.shape[0] - state_ref.shape[1]
    for rows in row_chunks(state_ref.shape[0]):
        out_ref[rows, :] = product(state_ref[rows, :], join_ref[width:, :])
    index = near_atoms(index_ref[...], part_atoms, shards)
    for end in range(2):
        column = as_column(index[end : end + 1, :])
        chosen_ref[:, end * part_atoms : (end + 1) * part_atoms] = (
            lax.broadcasted_iota(jnp.int32, (column.shape[0], part_atoms), 1) == column
        ).astype(jnp.bfloat16)


def final_kernel(shards, scale, *refs):
    sums = refs[:shards]
    atoms_ref, weight_ref, join_ref, state_ref, side_ref, chosen_ref = refs[shards : shards + 6]
    edges_hbm, own_hbm, table_ref, edges_ref, own_ref, sems = refs[shards + 6 :]
    part_atoms = atoms_ref.shape[0]
    count = part_atoms // shards
    total = sums[0][...].astype(jnp.float32)
    for by, part in list(zip(distances(shards), sums))[1:]:
        pieces = [part[(at ^ by) * count : ((at ^ by) + 1) * count, :] for at in range(shards)]
        total = total + jnp.concatenate(pieces, axis=0).astype(jnp.float32)
    scaled = (total * scale).astype(jnp.bfloat16)
    middle = silu(product(scaled, weight_ref[0])).astype(jnp.bfloat16)
    renewed = (atoms_ref[...].astype(jnp.float32) + product(middle, weight_ref[1])).astype(jnp.bfloat16)
    own_ref[...] = renewed[:count, :]
    own_copy = pltpu.make_async_copy(own_ref, own_hbm, sems.at[0])
    own_copy.start()
    width = renewed.shape[1]
    for end in range(2):
        table_ref[end * part_atoms : (end + 1) * part_atoms, :] = product(
            renewed, join_ref[end * width : (end + 1) * width, :]
        ).astype(jnp.bfloat16)
    copies = [own_copy]
    for at, rows in enumerate(row_chunks(state_ref.shape[0])):
        update = silu(product(chosen_ref[rows, :], table_ref[...]) + side_ref[rows, :])
        state = state_ref[rows, :].astype(jnp.float32)
        edges_ref[rows, :] = ((state + update) * root_half).astype(jnp.bfloat16)
        copies.append(
            pltpu.make_async_copy(edges_ref.at[rows], edges_hbm.at[rows], sems.at[1 + at])
        )
        copies[-1].start()
    for copy in copies:
        copy.wait()


def distances(shards):
    return [0, 1, 3, 2] if shards == 4 else list(range(shards))


def from_others(value, shards):
    return [value] + [
        lax.ppermute(value, "edge", [(at, at ^ by) for at in range(shards)])
        for by in distances(shards)[1:]
    ]


def by_relay(value, shards, between):
    if shards != 4:
        return from_others(value, shards), between(value)
    near = lax.ppermute(value, "edge", [(at, at ^ 1) for at in range(4)])
    far = lax.ppermute(value, "edge", [(at, at ^ 2) for at in range(4)])
    others = between(value)
    middle = lax.ppermute(others[0], "edge", [(0, 0), (1, 2), (2, 1), (3, 3)])
    relayed = lax.ppermute(far, "edge", [(at, at ^ 1) for at in range(4)])
    return [value, near, far, middle, relayed], others


def body(
    edges,
    atoms,
    reverse,
    atom_index,
    tile_source,
    tiles,
    weight_edge,
    weight_down,
    weight_up,
    weight_residual,
    weight_message,
    weight_atom,
    weight_join,
):
    rows, wide = edges.shape
    channels = weight_down.shape[0]
    domains = lax.axis_size("dom")
    shards = lax.axis_size("edge")
    count, atom_wide = atoms.shape
    part_atoms = count * shards
    capacity = rows // domains
    partners = domains - 1
    slots = partners * capacity
    lines = rows // 2
    packed = 2 * channels

    narrow = call(
        narrow_kernel,
        shaped((lines + count * atom_wide // packed, packed)),
        (edges, weight_edge, weight_down, atoms),
        hbm=(0, 1, 2, 3),
        scratch=[
            pltpu.VMEM(edges.shape, jnp.bfloat16),
            pltpu.VMEM(weight_edge.shape, jnp.bfloat16),
            pltpu.VMEM(weight_down.shape, jnp.bfloat16),
            pltpu.SemaphoreType.DMA((2 + 2 * len(row_chunks(lines)) + atom_wide // packed,)),
        ],
        flops=2 * rows * wide * (wide + channels),
        nbytes=2 * (rows * wide + wide * wide),
    )
    later = (
        edges, tiles, weight_up, weight_residual, weight_message, weight_join, weight_atom, atom_index
    )
    def index_call(value):
        return call(
            functools.partial(index_kernel, domains, shards, len(later)),
            (
                shaped(value.shape),
                shaped((slots, rows)),
                shaped((rows, slots)),
                shaped((rows, rows)),
            )
            + tuple(shaped(each.shape, each.dtype) for each in later),
            (reverse.reshape(1, rows), value, *later),
            hbm=range(2, 2 + len(later)),
            scratch=[pltpu.SemaphoreType.DMA((len(later),))],
            flops=40 * rows * rows,
            nbytes=6 * rows * rows,
        )

    narrow_parts, (_, send, fetch, local, *later) = by_relay(narrow, shards, index_call)
    edges, tiles, weight_up, weight_residual, weight_message, weight_join, weight_atom, atom_index = later
    trip_out, all_atoms, *outgoing = call(
        functools.partial(mix_kernel, shards, len(narrow_parts)),
        (shaped((rows, channels)), shaped((part_atoms, atom_wide)))
        + (shaped((capacity // 2, packed)),) * partners,
        (tile_source, tiles, *narrow_parts, send),
        smem=(0,),
        scratch=[pltpu.VMEM((shards * lines, packed), jnp.bfloat16)],
        flops=2 * rows * rows * channels,
        nbytes=2 * rows * rows,
    )
    arrived = [
        lax.ppermute(block, "dom", [(at, at ^ (partners - place)) for at in range(domains)])
        for place, block in enumerate(outgoing)
    ]
    base = call(
        base_kernel,
        shaped((rows, wide), jnp.float32),
        (edges, trip_out, local, weight_up),
        flops=2 * rows * channels * (rows + 2 * wide),
        nbytes=2 * rows * rows + 6 * rows * wide,
    )
    state, sums = call(
        functools.partial(state_kernel, partners),
        (shaped((rows, wide)), shaped((part_atoms, atom_wide))),
        (base, fetch, weight_up, weight_residual, weight_message, atom_index, *arrived),
        scratch=[pltpu.VMEM((slots, channels), jnp.bfloat16)],
        flops=4 * rows * wide * wide,
        nbytes=8 * rows * wide,
    )
    sums_parts = from_others(sums, shards)
    side, chosen = call(
        functools.partial(side_kernel, shards, part_atoms),
        (shaped((rows, wide), jnp.float32), shaped((rows, 2 * part_atoms))),
        (state, weight_join, atom_index),
        flops=2 * rows * wide * wide,
        nbytes=8 * rows * wide,
    )
    return call(
        functools.partial(final_kernel, shards, (rows // count) ** -0.5),
        (shaped((rows, wide), space=pltpu.HBM), shaped((count, atom_wide), space=pltpu.HBM)),
        (*sums_parts, all_atoms, weight_atom, weight_join, state, side, chosen),
        scratch=[
            pltpu.VMEM((2 * part_atoms, wide), jnp.bfloat16),
            pltpu.VMEM((rows, wide), jnp.bfloat16),
            pltpu.VMEM((count, atom_wide), jnp.bfloat16),
            pltpu.SemaphoreType.DMA((1 + len(row_chunks(rows)),)),
        ],
        flops=4 * rows * part_atoms * wide,
        nbytes=8 * rows * wide,
    )


def solution(mesh):
    split = P(("dom", "edge"))
    placed = (
        P(("dom", "edge"), None),
        P(("dom", "edge"), None),
        split,
        P(None, ("dom", "edge")),
        P(("dom", "edge"), None),
        P(("dom", "edge"), None, None),
    ) + (P(),) * 7
    return jax.shard_map(
        body,
        mesh=mesh,
        in_specs=placed,
        out_specs=(P(("dom", "edge"), None), P(("dom", "edge"), None)),
        check_vma=False,
    )
```

```python
import functools

import jax
import jax.numpy as jnp
from jax import lax
from jax.experimental import pallas as pl
from jax.experimental.pallas import tpu as pltpu
from jax.sharding import PartitionSpec as P

root_half = 0.7071067811865476
MIB = 1 << 20
CHUNK = 256
GROUPS = 4


def product(operand, weights):
    return jnp.dot(operand, weights, preferred_element_type=jnp.float32)


def silu(value):
    halved = 0.5 * value
    return halved + halved * jnp.tanh(halved)


def as_column(row):
    wide = jnp.broadcast_to(row.astype(jnp.float32), (8, row.shape[1]))
    return jnp.transpose(wide)[:, :1].astype(jnp.int32)


def row_chunks(rows):
    step = min(CHUNK, rows)
    return [slice(at, at + step) for at in range(0, rows, step)]


def call(kernel, outs, args, *, smem=(), hbm=(), scratch=(), flops=0, nbytes=0, limit=24):
    def space(at):
        return pltpu.SMEM if at in smem else pltpu.HBM if at in hbm else pltpu.VMEM

    args = [
        pltpu.with_memory_space_constraint(arg, pltpu.HBM) if at in hbm else arg
        for at, arg in enumerate(args)
    ]
    return pl.pallas_call(
        kernel,
        out_shape=outs,
        in_specs=[pl.BlockSpec(memory_space=space(at)) for at in range(len(args))],
        out_specs=jax.tree.map(
            lambda out: pl.BlockSpec(
                memory_space=pltpu.HBM if out.memory_space == pltpu.HBM else pltpu.VMEM
            ),
            outs,
        ),
        scratch_shapes=list(scratch),
        compiler_params=pltpu.CompilerParams(vmem_limit_bytes=limit * MIB),
        cost_estimate=pl.CostEstimate(flops=flops, bytes_accessed=nbytes, transcendentals=0),
    )(*args)


def shaped(shape, dtype=jnp.bfloat16, space=pltpu.VMEM):
    return space(tuple(shape), dtype)


def narrow_kernel(
    edges_hbm, weight_hbm, down_hbm, atoms_hbm, out_ref, edges_ref, weight_ref, down_ref, sems
):
    half = edges_hbm.shape[0] // 2
    pieces = [
        slice(base + rows.start, base + rows.stop)
        for rows in row_chunks(half)
        for base in (0, half)
    ]
    copies = [
        pltpu.make_async_copy(weight_hbm, weight_ref, sems.at[0]),
        pltpu.make_async_copy(down_hbm, down_ref, sems.at[1]),
    ] + [
        pltpu.make_async_copy(edges_hbm.at[piece], edges_ref.at[piece], sems.at[2 + at])
        for at, piece in enumerate(pieces)
    ]
    for copy in [copies[0], copies[2], copies[3], copies[1]] + copies[4:]:
        copy.start()
    count, wide = atoms_hbm.shape
    lanes = out_ref.shape[1]
    atom_copies = [
        pltpu.make_async_copy(
            atoms_hbm.at[:, at * lanes : (at + 1) * lanes],
            out_ref.at[half + at * count : half + (at + 1) * count, :],
            sems.at[len(copies) + at],
        )
        for at in range(wide // lanes)
    ]
    for copy in atom_copies:
        copy.start()
    copies[0].wait()
    copies[1].wait()
    for at, rows in enumerate(row_chunks(half)):
        copies[2 + 2 * at].wait()
        copies[3 + 2 * at].wait()
        hidden = [
            silu(product(edges_ref[piece, :], weight_ref[...])).astype(jnp.bfloat16)
            for piece in pieces[2 * at : 2 * at + 2]
        ]
        sides = [
            lax.dot_general(
                each, down_ref[...], (((1,), (1,)), ((), ())), preferred_element_type=jnp.float32
            )
            for each in hidden
        ]
        out_ref[rows, :] = silu(jnp.concatenate(sides, axis=1)).astype(jnp.bfloat16)
    for copy in atom_copies:
        copy.wait()


def one_hot(shape, axis, chosen):
    return (lax.broadcasted_iota(jnp.int32, shape, axis) == chosen).astype(jnp.bfloat16)


def group_mask(group, channels):
    column = lax.broadcasted_iota(jnp.int32, (group.shape[0], GROUPS * channels), 1)
    return (column // channels == group).astype(jnp.bfloat16)


def index_kernel(domains, shards, channels, operands, *refs):
    reverse_ref = refs[0]
    sources = refs[1 : 1 + operands]
    send_ref, send_mask_ref, fetch_ref, fetch_mask_ref, local_ref, local_mask_ref, stack_ref = refs[
        1 + operands : 8 + operands
    ]
    targets = refs[8 + operands : 8 + 2 * operands]
    sems = refs[-1]
    copies = [
        pltpu.make_async_copy(source, target, sems.at[at])
        for at, (source, target) in enumerate(zip(sources, targets))
    ] + [
        pltpu.make_async_copy(
            sources[0].at[1],
            stack_ref.at[at * channels : (at + 1) * channels, :],
            sems.at[operands + at],
        )
        for at in range(GROUPS)
    ]
    for copy in copies:
        copy.start()
    rows = reverse_ref.shape[1]
    each = rows // GROUPS
    capacity = rows // domains
    half = capacity // 2
    slots = (domains - 1) * capacity
    own = lax.axis_index("dom")
    reverse = reverse_ref[...]
    holder = reverse // (rows * shards)
    source_row = lax.rem(reverse, rows)
    partner = holder ^ own
    remote = partner != 0
    block = domains - 1 - partner
    member = one_hot((domains, rows), 0, partner)
    before = (
        lax.broadcasted_iota(jnp.int32, (rows, rows), 0)
        < lax.broadcasted_iota(jnp.int32, (rows, rows), 1)
    ).astype(jnp.bfloat16)
    earlier = (as_column(source_row) < source_row).astype(jnp.bfloat16)

    def rank(matrix):
        counts = product(member, matrix) * member.astype(jnp.float32)
        return jnp.sum(counts, axis=0, keepdims=True).astype(jnp.int32)

    place = rank(before)
    part = (place >= half).astype(jnp.int32)
    send_slot = part * (slots // 2) + block * half + place - part * half
    sent = one_hot((slots, rows), 0, jnp.where(remote, send_slot, -1))
    owner = (
        lax.broadcasted_iota(jnp.int32, (rows, GROUPS * channels), 0) // each
        == lax.broadcasted_iota(jnp.int32, (rows, GROUPS * channels), 1) // channels
    ).astype(jnp.bfloat16)
    send_mask_ref[...] = product(sent, owner).astype(jnp.bfloat16)
    folded = sent[:, :each]
    for at in range(1, GROUPS):
        folded = folded + sent[:, at * each : (at + 1) * each]
    send_ref[...] = folded

    far_place = rank(earlier)
    part = (far_place >= half).astype(jnp.int32)
    side = (block >= domains // 2).astype(jnp.int32)
    fetch_row = (block - side * (domains // 2)) * half + far_place - part * half
    fetch_ref[...] = one_hot(
        fetch_ref.shape, 1, as_column(jnp.where(remote, fetch_row, -1))
    )
    fetch_mask_ref[...] = group_mask(as_column(2 * side + part), channels)
    local_group = source_row // each
    local_row = source_row - local_group * each
    local_ref[...] = one_hot(local_ref.shape, 1, as_column(jnp.where(remote, -1, local_row)))
    local_mask_ref[...] = group_mask(as_column(local_group), channels)
    for copy in copies:
        copy.wait()


def picked_rows(chosen, table, mask):
    return product(chosen, table).astype(jnp.bfloat16) * mask


def mix_kernel(shards, *refs):
    source_ref, tiles_ref = refs[:2]
    parts = refs[2 : 2 + shards]
    send_ref, mask_ref, trip_ref, atoms_ref = refs[2 + shards : 6 + shards]
    out_refs = refs[6 + shards : -1]
    held_ref = refs[-1]
    blocks, block_len, width = tiles_ref.shape
    count = width // block_len
    lines = held_ref.shape[0] // shards
    own_atoms = atoms_ref.shape[0] // shards
    atom_wide = atoms_ref.shape[1]
    lanes = held_ref.shape[1]
    me = lax.axis_index("edge")
    for part, at in zip(parts, distances(shards)):
        held_ref[at * lines : (at + 1) * lines, :] = part[:lines, :]
        for piece in range(atom_wide // lanes):
            start = lines + piece * own_atoms
            atoms_ref[
                at * own_atoms : (at + 1) * own_atoms, piece * lanes : (piece + 1) * lanes
            ] = part[start : start + own_atoms, :]
    half_blocks = blocks // 2
    channels = trip_ref.shape[1] // GROUPS
    per = blocks // GROUPS

    def mixed(block):
        picks = []
        for tile in range(count):
            source = source_ref[block, tile]
            shard = source // blocks
            within = source - shard * blocks
            upper = within // half_blocks
            start = (shard ^ me) * lines + (within - upper * half_blocks) * block_len
            rows = held_ref[pl.ds(pl.multiple_of(start, block_len), block_len), :]
            picks.append(jnp.where(upper == 1, rows[:, channels:], rows[:, :channels]))
        return product(tiles_ref[block], jnp.concatenate(picks, axis=0))

    for at in range(per):
        for group in range(0, GROUPS, 2):
            pair = [mixed((group + side) * per + at) for side in range(2)]
            trip_ref[
                at * block_len : (at + 1) * block_len, group * channels : (group + 2) * channels
            ] = jnp.concatenate(pair, axis=1).astype(jnp.bfloat16)
    half_slots = send_ref.shape[0] // 2
    parts = []
    for side in range(2):
        rows = slice(side * half_slots, (side + 1) * half_slots)
        found = product(send_ref[rows, :], trip_ref[...]) * mask_ref[rows, :].astype(jnp.float32)
        both = found[:, : 2 * channels] + found[:, 2 * channels :]
        parts.append(both + pltpu.roll(both, channels, 1))
    lane = lax.broadcasted_iota(jnp.int32, parts[0].shape, 1)
    packed = jnp.where(lane < channels, parts[0], parts[1]).astype(jnp.bfloat16)
    each = half_slots // len(out_refs)
    for at, out_ref in enumerate(out_refs):
        out_ref[...] = packed[at * each : (at + 1) * each, :]


def base_kernel(edges_ref, trip_ref, local_ref, mask_ref, up_ref, stack_ref, out_ref):
    each = trip_ref.shape[0]
    channels = up_ref.shape[1]
    for group in range(GROUPS):
        rows = slice(group * each, (group + 1) * each)
        picked = picked_rows(local_ref[rows, :], trip_ref[...], mask_ref[rows, :])
        direct = trip_ref[:, group * channels : (group + 1) * channels]
        joined = product(direct, up_ref[0]) + product(picked, stack_ref[...])
        out_ref[rows, :] = edges_ref[rows, :].astype(jnp.float32) + joined * root_half


def state_kernel(partners, *refs):
    base_ref, fetch_ref, mask_ref, stack_ref, residual_ref, message_ref, index_ref = refs[:7]
    arrived = refs[7 : 7 + partners]
    state_ref, sums_ref, slots_ref = refs[7 + partners :]
    each, lanes = arrived[0].shape
    column = (partners + 1) // 2
    for at in range(partners):
        down, right = at % column, at // column
        slots_ref[down * each : (down + 1) * each, right * lanes : (right + 1) * lanes] = arrived[at][...]
    down, right = partners % column, partners // column
    slots_ref[down * each : (down + 1) * each, right * lanes : (right + 1) * lanes] = jnp.zeros(
        (each, lanes), slots_ref.dtype
    )
    part_atoms = sums_ref.shape[0]
    shards = lax.axis_size("edge")
    near = near_atoms(index_ref[1:2, :], part_atoms, shards)
    chosen = (
        lax.broadcasted_iota(jnp.int32, (part_atoms, near.shape[1]), 0) == near
    ).astype(jnp.bfloat16)
    chunks = row_chunks(base_ref.shape[0])
    gathered = None
    for first in range(0, len(chunks), 2):
        group = chunks[first : first + 2]
        picked = [
            picked_rows(fetch_ref[rows, :], slots_ref[...], mask_ref[rows, :]) for rows in group
        ]
        states = [
            (base_ref[rows, :] + product(each, stack_ref[...]) * root_half).astype(jnp.bfloat16)
            for rows, each in zip(group, picked)
        ]
        for layer in range(residual_ref.shape[0]):
            middles = [
                silu(product(each, residual_ref[layer, 0])).astype(jnp.bfloat16) for each in states
            ]
            branches = [silu(product(each, residual_ref[layer, 1])) for each in middles]
            states = [
                ((each.astype(jnp.float32) + branch) * root_half).astype(jnp.bfloat16)
                for each, branch in zip(states, branches)
            ]
        for rows, each in zip(group, states):
            state_ref[rows, :] = each
            term = product(chosen[:, rows], each)
            gathered = term if gathered is None else gathered + term
    sums_ref[...] = product(gathered.astype(jnp.bfloat16), message_ref[...]).astype(jnp.bfloat16)


def near_atoms(index, part_atoms, shards):
    count = part_atoms // shards
    holder = index // count
    return (holder ^ lax.axis_index("edge")) * count + lax.rem(index, count)


def side_kernel(shards, part_atoms, state_ref, join_ref, index_ref, out_ref, chosen_ref):
    width = join_ref.shape[0] - state_ref.shape[1]
    for rows in row_chunks(state_ref.shape[0]):
        out_ref[rows, :] = product(state_ref[rows, :], join_ref[width:, :])
    index = near_atoms(index_ref[...], part_atoms, shards)
    for end in range(2):
        column = as_column(index[end : end + 1, :])
        chosen_ref[:, end * part_atoms : (end + 1) * part_atoms] = (
            lax.broadcasted_iota(jnp.int32, (column.shape[0], part_atoms), 1) == column
        ).astype(jnp.bfloat16)


def final_kernel(shards, scale, *refs):
    sums = refs[:shards]
    atoms_ref, weight_ref, join_ref, state_ref, side_ref, chosen_ref = refs[shards : shards + 6]
    edges_hbm, own_hbm, table_ref, edges_ref, own_ref, sems = refs[shards + 6 :]
    part_atoms = atoms_ref.shape[0]
    count = part_atoms // shards
    total = sums[0][...].astype(jnp.float32)
    for by, part in list(zip(distances(shards), sums))[1:]:
        pieces = [part[(at ^ by) * count : ((at ^ by) + 1) * count, :] for at in range(shards)]
        total = total + jnp.concatenate(pieces, axis=0).astype(jnp.float32)
    scaled = (total * scale).astype(jnp.bfloat16)
    middle = silu(product(scaled, weight_ref[0])).astype(jnp.bfloat16)
    renewed = (atoms_ref[...].astype(jnp.float32) + product(middle, weight_ref[1])).astype(jnp.bfloat16)
    own_ref[...] = renewed[:count, :]
    own_copy = pltpu.make_async_copy(own_ref, own_hbm, sems.at[0])
    own_copy.start()
    width = renewed.shape[1]
    for end in range(2):
        table_ref[end * part_atoms : (end + 1) * part_atoms, :] = product(
            renewed, join_ref[end * width : (end + 1) * width, :]
        ).astype(jnp.bfloat16)
    copies = [own_copy]
    chunks = row_chunks(state_ref.shape[0])
    for first in range(0, len(chunks), 2):
        group = chunks[first : first + 2]
        found = [product(chosen_ref[rows, :], table_ref[...]) + side_ref[rows, :] for rows in group]
        for at, (rows, each) in enumerate(zip(group, found)):
            state = state_ref[rows, :].astype(jnp.float32)
            edges_ref[rows, :] = ((state + silu(each)) * root_half).astype(jnp.bfloat16)
            copies.append(
                pltpu.make_async_copy(
                    edges_ref.at[rows], edges_hbm.at[rows], sems.at[1 + first + at]
                )
            )
            copies[-1].start()
    for copy in copies:
        copy.wait()


def distances(shards):
    return [0, 1, 3, 2] if shards == 4 else list(range(shards))


def from_others(value, shards):
    return [value] + [
        lax.ppermute(value, "edge", [(at, at ^ by) for at in range(shards)])
        for by in distances(shards)[1:]
    ]


def body(
    edges,
    atoms,
    reverse,
    atom_index,
    tile_source,
    tiles,
    weight_edge,
    weight_down,
    weight_up,
    weight_residual,
    weight_message,
    weight_atom,
    weight_join,
):
    rows, wide = edges.shape
    channels = weight_down.shape[0]
    domains = lax.axis_size("dom")
    shards = lax.axis_size("edge")
    count, atom_wide = atoms.shape
    part_atoms = count * shards
    capacity = rows // domains
    partners = domains - 1
    slots = partners * capacity
    lines = rows // 2
    packed = 2 * channels

    narrow = call(
        narrow_kernel,
        shaped((lines + count * atom_wide // packed, packed)),
        (edges, weight_edge, weight_down, atoms),
        hbm=(0, 1, 2, 3),
        scratch=[
            pltpu.VMEM(edges.shape, jnp.bfloat16),
            pltpu.VMEM(weight_edge.shape, jnp.bfloat16),
            pltpu.VMEM(weight_down.shape, jnp.bfloat16),
            pltpu.SemaphoreType.DMA((2 + 2 * len(row_chunks(lines)) + atom_wide // packed,)),
        ],
        flops=2 * rows * wide * (wide + channels),
        nbytes=2 * (rows * wide + wide * wide),
    )
    narrow_parts = from_others(narrow, shards)
    later = (
        weight_up, edges, tiles, weight_residual, weight_message, weight_join, weight_atom, atom_index
    )
    each, grouped = rows // GROUPS, GROUPS * channels
    column = domains // 2 * (capacity // 2)
    send, send_mask, fetch, fetch_mask, local, local_mask, up_stack, *later = call(
        functools.partial(index_kernel, domains, shards, channels, len(later)),
        (
            shaped((slots, each)),
            shaped((slots, grouped)),
            shaped((rows, column)),
            shaped((rows, grouped)),
            shaped((rows, each)),
            shaped((rows, grouped)),
            shaped((grouped, wide)),
        )
        + tuple(shaped(each.shape, each.dtype) for each in later),
        (reverse.reshape(1, rows), *later),
        hbm=range(1, 1 + len(later)),
        scratch=[pltpu.SemaphoreType.DMA((len(later) + GROUPS,))],
        flops=40 * rows * rows,
        nbytes=6 * rows * rows,
    )
    weight_up, edges, tiles, weight_residual, weight_message, weight_join, weight_atom, atom_index = later
    trip_out, all_atoms, *outgoing = call(
        functools.partial(mix_kernel, shards),
        (shaped((each, grouped)), shaped((part_atoms, atom_wide)))
        + (shaped((capacity // 2, packed)),) * partners,
        (tile_source, tiles, *narrow_parts, send, send_mask),
        smem=(0,),
        scratch=[pltpu.VMEM((shards * lines, packed), jnp.bfloat16)],
        flops=2 * rows * rows * channels,
        nbytes=2 * rows * rows,
    )
    arrived = [
        lax.ppermute(block, "dom", [(at, at ^ (partners - place)) for at in range(domains)])
        for place, block in enumerate(outgoing)
    ]
    base = call(
        base_kernel,
        shaped((rows, wide), jnp.float32),
        (edges, trip_out, local, local_mask, weight_up, up_stack),
        flops=2 * rows * channels * (rows + 2 * wide),
        nbytes=2 * rows * rows + 6 * rows * wide,
    )
    state, sums = call(
        functools.partial(state_kernel, partners),
        (shaped((rows, wide)), shaped((part_atoms, atom_wide))),
        (base, fetch, fetch_mask, up_stack, weight_residual, weight_message, atom_index, *arrived),
        scratch=[pltpu.VMEM((column, grouped), jnp.bfloat16)],
        flops=4 * rows * wide * wide,
        nbytes=8 * rows * wide,
    )
    sums_parts = from_others(sums, shards)
    side, chosen = call(
        functools.partial(side_kernel, shards, part_atoms),
        (shaped((rows, wide), jnp.float32), shaped((rows, 2 * part_atoms))),
        (state, weight_join, atom_index),
        flops=2 * rows * wide * wide,
        nbytes=8 * rows * wide,
    )
    return call(
        functools.partial(final_kernel, shards, (rows // count) ** -0.5),
        (shaped((rows, wide), space=pltpu.HBM), shaped((count, atom_wide), space=pltpu.HBM)),
        (*sums_parts, all_atoms, weight_atom, weight_join, state, side, chosen),
        scratch=[
            pltpu.VMEM((2 * part_atoms, wide), jnp.bfloat16),
            pltpu.VMEM((rows, wide), jnp.bfloat16),
            pltpu.VMEM((count, atom_wide), jnp.bfloat16),
            pltpu.SemaphoreType.DMA((1 + len(row_chunks(rows)),)),
        ],
        flops=4 * rows * part_atoms * wide,
        nbytes=8 * rows * wide,
    )


def solution(mesh):
    split = P(("dom", "edge"))
    placed = (
        P(("dom", "edge"), None),
        P(("dom", "edge"), None),
        split,
        P(None, ("dom", "edge")),
        P(("dom", "edge"), None),
        P(("dom", "edge"), None, None),
    ) + (P(),) * 7
    return jax.shard_map(
        body,
        mesh=mesh,
        in_specs=placed,
        out_specs=(P(("dom", "edge"), None), P(("dom", "edge"), None)),
        check_vma=False,
    )
```

```python
import functools

import jax
import jax.numpy as jnp
from jax import lax
from jax.experimental import pallas as pl
from jax.experimental.pallas import tpu as pltpu
from jax.sharding import PartitionSpec as P

root_half = 0.7071067811865476
MIB = 1 << 20
CHUNK = 256
GROUPS = 4


def product(operand, weights):
    return jnp.dot(operand, weights, preferred_element_type=jnp.float32)


def silu(value):
    halved = 0.5 * value
    return halved + halved * jnp.tanh(halved)


def as_column(row):
    wide = jnp.broadcast_to(row.astype(jnp.float32), (8, row.shape[1]))
    return jnp.transpose(wide)[:, :1].astype(jnp.int32)


def row_chunks(rows):
    step = min(CHUNK, rows)
    return [slice(at, at + step) for at in range(0, rows, step)]


def call(kernel, outs, args, *, smem=(), hbm=(), scratch=(), flops=0, nbytes=0, limit=24):
    def space(at):
        return pltpu.SMEM if at in smem else pltpu.HBM if at in hbm else pltpu.VMEM

    args = [
        pltpu.with_memory_space_constraint(arg, pltpu.HBM) if at in hbm else arg
        for at, arg in enumerate(args)
    ]
    return pl.pallas_call(
        kernel,
        out_shape=outs,
        in_specs=[pl.BlockSpec(memory_space=space(at)) for at in range(len(args))],
        out_specs=jax.tree.map(
            lambda out: pl.BlockSpec(
                memory_space=pltpu.HBM if out.memory_space == pltpu.HBM else pltpu.VMEM
            ),
            outs,
        ),
        scratch_shapes=list(scratch),
        compiler_params=pltpu.CompilerParams(vmem_limit_bytes=limit * MIB),
        cost_estimate=pl.CostEstimate(flops=flops, bytes_accessed=nbytes, transcendentals=0),
    )(*args)


def shaped(shape, dtype=jnp.bfloat16, space=pltpu.VMEM):
    return space(tuple(shape), dtype)


def narrow_kernel(
    edges_hbm, weight_hbm, down_hbm, atoms_hbm, out_ref, edges_ref, weight_ref, down_ref, sems
):
    half = edges_hbm.shape[0] // 2
    pieces = [
        slice(base + rows.start, base + rows.stop)
        for rows in row_chunks(half)
        for base in (0, half)
    ]
    copies = [
        pltpu.make_async_copy(weight_hbm, weight_ref, sems.at[0]),
        pltpu.make_async_copy(down_hbm, down_ref, sems.at[1]),
    ] + [
        pltpu.make_async_copy(edges_hbm.at[piece], edges_ref.at[piece], sems.at[2 + at])
        for at, piece in enumerate(pieces)
    ]
    for copy in [copies[0], copies[2], copies[3], copies[1]] + copies[4:]:
        copy.start()
    count, wide = atoms_hbm.shape
    lanes = out_ref.shape[1]
    atom_copies = [
        pltpu.make_async_copy(
            atoms_hbm.at[:, at * lanes : (at + 1) * lanes],
            out_ref.at[half + at * count : half + (at + 1) * count, :],
            sems.at[len(copies) + at],
        )
        for at in range(wide // lanes)
    ]
    for copy in atom_copies:
        copy.start()
    copies[0].wait()
    copies[1].wait()
    for at, rows in enumerate(row_chunks(half)):
        copies[2 + 2 * at].wait()
        copies[3 + 2 * at].wait()
        hidden = [
            silu(product(edges_ref[piece, :], weight_ref[...])).astype(jnp.bfloat16)
            for piece in pieces[2 * at : 2 * at + 2]
        ]
        sides = [
            lax.dot_general(
                each, down_ref[...], (((1,), (1,)), ((), ())), preferred_element_type=jnp.float32
            )
            for each in hidden
        ]
        out_ref[rows, :] = silu(jnp.concatenate(sides, axis=1)).astype(jnp.bfloat16)
    for copy in atom_copies:
        copy.wait()


def one_hot(shape, axis, chosen):
    return (lax.broadcasted_iota(jnp.int32, shape, axis) == chosen).astype(jnp.bfloat16)


def group_mask(group, channels):
    column = lax.broadcasted_iota(jnp.int32, (group.shape[0], GROUPS * channels), 1)
    return (column // channels == group).astype(jnp.bfloat16)


def index_kernel(domains, shards, channels, operands, *refs):
    reverse_ref = refs[0]
    sources = refs[1 : 1 + operands]
    send_ref, send_mask_ref, fetch_ref, fetch_mask_ref, local_ref, local_mask_ref, stack_ref = refs[
        1 + operands : 8 + operands
    ]
    targets = refs[8 + operands : 8 + 2 * operands]
    sems = refs[-1]
    copies = [
        pltpu.make_async_copy(source, target, sems.at[at])
        for at, (source, target) in enumerate(zip(sources, targets))
    ] + [
        pltpu.make_async_copy(
            sources[0].at[1],
            stack_ref.at[at * channels : (at + 1) * channels, :],
            sems.at[operands + at],
        )
        for at in range(GROUPS)
    ]
    for copy in copies:
        copy.start()
    rows = reverse_ref.shape[1]
    each = rows // GROUPS
    capacity = rows // domains
    half = capacity // 2
    slots = (domains - 1) * capacity
    own = lax.axis_index("dom")
    reverse = reverse_ref[...]
    holder = reverse // (rows * shards)
    source_row = lax.rem(reverse, rows)
    partner = holder ^ own
    remote = partner != 0
    block = domains - 1 - partner
    member = one_hot((domains, rows), 0, partner)
    before = (
        lax.broadcasted_iota(jnp.int32, (rows, rows), 0)
        < lax.broadcasted_iota(jnp.int32, (rows, rows), 1)
    ).astype(jnp.bfloat16)
    earlier = (as_column(source_row) < source_row).astype(jnp.bfloat16)

    def rank(matrix):
        counts = product(member, matrix) * member.astype(jnp.float32)
        return jnp.sum(counts, axis=0, keepdims=True).astype(jnp.int32)

    place = rank(before)
    part = (place >= half).astype(jnp.int32)
    send_slot = part * (slots // 2) + block * half + place - part * half
    sent = one_hot((slots, rows), 0, jnp.where(remote, send_slot, -1))
    owner = (
        lax.broadcasted_iota(jnp.int32, (rows, GROUPS * channels), 0) // each
        == lax.broadcasted_iota(jnp.int32, (rows, GROUPS * channels), 1) // channels
    ).astype(jnp.bfloat16)
    send_mask_ref[...] = product(sent, owner).astype(jnp.bfloat16)
    folded = sent[:, :each]
    for at in range(1, GROUPS):
        folded = folded + sent[:, at * each : (at + 1) * each]
    send_ref[...] = folded

    far_place = rank(earlier)
    part = (far_place >= half).astype(jnp.int32)
    side = (block >= domains // 2).astype(jnp.int32)
    fetch_row = (block - side * (domains // 2)) * half + far_place - part * half
    fetch_ref[...] = one_hot(
        fetch_ref.shape, 1, as_column(jnp.where(remote, fetch_row, -1))
    )
    fetch_mask_ref[...] = group_mask(as_column(2 * side + part), channels)
    local_group = source_row // each
    local_row = source_row - local_group * each
    local_ref[...] = one_hot(local_ref.shape, 1, as_column(jnp.where(remote, -1, local_row)))
    local_mask_ref[...] = group_mask(as_column(local_group), channels)
    for copy in copies:
        copy.wait()


def picked_rows(chosen, table, mask):
    return product(chosen, table).astype(jnp.bfloat16) * mask


def mix_kernel(shards, *refs):
    source_ref, tiles_ref = refs[:2]
    parts = refs[2 : 2 + shards]
    send_ref, mask_ref, trip_ref, atoms_ref = refs[2 + shards : 6 + shards]
    out_refs = refs[6 + shards : -1]
    held_ref = refs[-1]
    blocks, block_len, width = tiles_ref.shape
    count = width // block_len
    lines = held_ref.shape[0] // shards
    own_atoms = atoms_ref.shape[0] // shards
    atom_wide = atoms_ref.shape[1]
    lanes = held_ref.shape[1]
    me = lax.axis_index("edge")
    for part, at in zip(parts, distances(shards)):
        held_ref[at * lines : (at + 1) * lines, :] = part[:lines, :]
        for piece in range(atom_wide // lanes):
            start = lines + piece * own_atoms
            atoms_ref[
                at * own_atoms : (at + 1) * own_atoms, piece * lanes : (piece + 1) * lanes
            ] = part[start : start + own_atoms, :]
    half_blocks = blocks // 2
    channels = trip_ref.shape[1] // GROUPS
    per = blocks // GROUPS

    def mixed(block):
        picks = []
        for tile in range(count):
            source = source_ref[block, tile]
            shard = source // blocks
            within = source - shard * blocks
            upper = within // half_blocks
            start = (shard ^ me) * lines + (within - upper * half_blocks) * block_len
            rows = held_ref[pl.ds(pl.multiple_of(start, block_len), block_len), :]
            picks.append(jnp.where(upper == 1, rows[:, channels:], rows[:, :channels]))
        return product(tiles_ref[block], jnp.concatenate(picks, axis=0))

    for at in range(per):
        for group in range(0, GROUPS, 2):
            pair = [mixed((group + side) * per + at) for side in range(2)]
            trip_ref[
                at * block_len : (at + 1) * block_len, group * channels : (group + 2) * channels
            ] = jnp.concatenate(pair, axis=1).astype(jnp.bfloat16)
    half_slots = send_ref.shape[0] // 2
    parts = []
    for side in range(2):
        rows = slice(side * half_slots, (side + 1) * half_slots)
        found = product(send_ref[rows, :], trip_ref[...]) * mask_ref[rows, :].astype(jnp.float32)
        both = found[:, : 2 * channels] + found[:, 2 * channels :]
        parts.append(both + pltpu.roll(both, channels, 1))
    lane = lax.broadcasted_iota(jnp.int32, parts[0].shape, 1)
    packed = jnp.where(lane < channels, parts[0], parts[1]).astype(jnp.bfloat16)
    each = half_slots // len(out_refs)
    for at, out_ref in enumerate(out_refs):
        out_ref[...] = packed[at * each : (at + 1) * each, :]


def base_kernel(edges_ref, trip_ref, local_ref, mask_ref, up_ref, stack_ref, out_ref):
    each = trip_ref.shape[0]
    channels = up_ref.shape[1]
    for group in range(GROUPS):
        rows = slice(group * each, (group + 1) * each)
        picked = picked_rows(local_ref[rows, :], trip_ref[...], mask_ref[rows, :])
        direct = trip_ref[:, group * channels : (group + 1) * channels]
        joined = product(direct, up_ref[0]) + product(picked, stack_ref[...])
        out_ref[rows, :] = edges_ref[rows, :].astype(jnp.float32) + joined * root_half


def state_kernel(partners, *refs):
    base_ref, fetch_ref, mask_ref, stack_ref, residual_ref, message_ref, index_ref = refs[:7]
    arrived = refs[7 : 7 + partners]
    state_ref, sums_ref, slots_ref = refs[7 + partners :]
    each, lanes = arrived[0].shape
    column = (partners + 1) // 2
    for at in range(partners):
        down, right = at % column, at // column
        slots_ref[down * each : (down + 1) * each, right * lanes : (right + 1) * lanes] = arrived[at][...]
    down, right = partners % column, partners // column
    slots_ref[down * each : (down + 1) * each, right * lanes : (right + 1) * lanes] = jnp.zeros(
        (each, lanes), slots_ref.dtype
    )
    part_atoms = sums_ref.shape[0]
    shards = lax.axis_size("edge")
    near = near_atoms(index_ref[1:2, :], part_atoms, shards)
    chosen = (
        lax.broadcasted_iota(jnp.int32, (part_atoms, near.shape[1]), 0) == near
    ).astype(jnp.bfloat16)
    chunks = row_chunks(base_ref.shape[0])
    gathered = None
    for first in range(0, len(chunks), 2):
        group = chunks[first : first + 2]
        picked = [
            picked_rows(fetch_ref[rows, :], slots_ref[...], mask_ref[rows, :]) for rows in group
        ]
        states = [
            (base_ref[rows, :] + product(each, stack_ref[...]) * root_half).astype(jnp.bfloat16)
            for rows, each in zip(group, picked)
        ]
        for layer in range(residual_ref.shape[0]):
            middles = [
                silu(product(each, residual_ref[layer, 0])).astype(jnp.bfloat16) for each in states
            ]
            branches = [silu(product(each, residual_ref[layer, 1])) for each in middles]
            states = [
                ((each.astype(jnp.float32) + branch) * root_half).astype(jnp.bfloat16)
                for each, branch in zip(states, branches)
            ]
        for rows, each in zip(group, states):
            state_ref[rows, :] = each
            term = product(chosen[:, rows], each)
            gathered = term if gathered is None else gathered + term
    sums_ref[...] = product(gathered.astype(jnp.bfloat16), message_ref[...]).astype(jnp.bfloat16)


def near_atoms(index, part_atoms, shards):
    count = part_atoms // shards
    holder = index // count
    return (holder ^ lax.axis_index("edge")) * count + lax.rem(index, count)


def side_kernel(shards, part_atoms, state_ref, join_ref, index_ref, out_ref, chosen_ref):
    width = join_ref.shape[0] - state_ref.shape[1]
    for rows in row_chunks(state_ref.shape[0]):
        out_ref[rows, :] = product(state_ref[rows, :], join_ref[width:, :])
    index = near_atoms(index_ref[...], part_atoms, shards)
    for end in range(2):
        column = as_column(index[end : end + 1, :])
        chosen_ref[:, end * part_atoms : (end + 1) * part_atoms] = (
            lax.broadcasted_iota(jnp.int32, (column.shape[0], part_atoms), 1) == column
        ).astype(jnp.bfloat16)


def final_kernel(shards, scale, *refs):
    sums = refs[:shards]
    atoms_ref, weight_ref, join_ref, state_ref, side_ref, chosen_ref = refs[shards : shards + 6]
    edges_hbm, own_hbm, table_ref, edges_ref, own_ref, sems = refs[shards + 6 :]
    part_atoms = atoms_ref.shape[0]
    count = part_atoms // shards
    total = sums[0][...].astype(jnp.float32)
    for by, part in list(zip(distances(shards), sums))[1:]:
        pieces = [part[(at ^ by) * count : ((at ^ by) + 1) * count, :] for at in range(shards)]
        total = total + jnp.concatenate(pieces, axis=0).astype(jnp.float32)
    scaled = (total * scale).astype(jnp.bfloat16)
    middle = silu(product(scaled, weight_ref[0])).astype(jnp.bfloat16)
    renewed = (atoms_ref[...].astype(jnp.float32) + product(middle, weight_ref[1])).astype(jnp.bfloat16)
    own_ref[...] = renewed[:count, :]
    own_copy = pltpu.make_async_copy(own_ref, own_hbm, sems.at[0])
    own_copy.start()
    width = renewed.shape[1]
    for end in range(2):
        table_ref[end * part_atoms : (end + 1) * part_atoms, :] = product(
            renewed, join_ref[end * width : (end + 1) * width, :]
        ).astype(jnp.bfloat16)
    copies = [own_copy]
    chunks = row_chunks(state_ref.shape[0])
    for first in range(0, len(chunks), 2):
        group = chunks[first : first + 2]
        found = [product(chosen_ref[rows, :], table_ref[...]) + side_ref[rows, :] for rows in group]
        for at, (rows, each) in enumerate(zip(group, found)):
            state = state_ref[rows, :].astype(jnp.float32)
            edges_ref[rows, :] = ((state + silu(each)) * root_half).astype(jnp.bfloat16)
            copies.append(
                pltpu.make_async_copy(
                    edges_ref.at[rows], edges_hbm.at[rows], sems.at[1 + first + at]
                )
            )
            copies[-1].start()
    for copy in copies:
        copy.wait()


def distances(shards):
    return list(range(shards))


def from_others(value, shards):
    return [value] + [
        lax.ppermute(value, "edge", [(at, at ^ by) for at in range(shards)])
        for by in distances(shards)[1:]
    ]


def body(
    edges,
    atoms,
    reverse,
    atom_index,
    tile_source,
    tiles,
    weight_edge,
    weight_down,
    weight_up,
    weight_residual,
    weight_message,
    weight_atom,
    weight_join,
):
    rows, wide = edges.shape
    channels = weight_down.shape[0]
    domains = lax.axis_size("dom")
    shards = lax.axis_size("edge")
    count, atom_wide = atoms.shape
    part_atoms = count * shards
    capacity = rows // domains
    partners = domains - 1
    slots = partners * capacity
    lines = rows // 2
    packed = 2 * channels

    narrow = call(
        narrow_kernel,
        shaped((lines + count * atom_wide // packed, packed)),
        (edges, weight_edge, weight_down, atoms),
        hbm=(0, 1, 2, 3),
        scratch=[
            pltpu.VMEM(edges.shape, jnp.bfloat16),
            pltpu.VMEM(weight_edge.shape, jnp.bfloat16),
            pltpu.VMEM(weight_down.shape, jnp.bfloat16),
            pltpu.SemaphoreType.DMA((2 + 2 * len(row_chunks(lines)) + atom_wide // packed,)),
        ],
        flops=2 * rows * wide * (wide + channels),
        nbytes=2 * (rows * wide + wide * wide),
    )
    narrow_parts = from_others(narrow, shards)
    later = (
        weight_up, edges, tiles, weight_residual, weight_message, weight_join, weight_atom, atom_index
    )
    each, grouped = rows // GROUPS, GROUPS * channels
    column = domains // 2 * (capacity // 2)
    send, send_mask, fetch, fetch_mask, local, local_mask, up_stack, *later = call(
        functools.partial(index_kernel, domains, shards, channels, len(later)),
        (
            shaped((slots, each)),
            shaped((slots, grouped)),
            shaped((rows, column)),
            shaped((rows, grouped)),
            shaped((rows, each)),
            shaped((rows, grouped)),
            shaped((grouped, wide)),
        )
        + tuple(shaped(each.shape, each.dtype) for each in later),
        (reverse.reshape(1, rows), *later),
        hbm=range(1, 1 + len(later)),
        scratch=[pltpu.SemaphoreType.DMA((len(later) + GROUPS,))],
        flops=40 * rows * rows,
        nbytes=6 * rows * rows,
    )
    weight_up, edges, tiles, weight_residual, weight_message, weight_join, weight_atom, atom_index = later
    trip_out, all_atoms, *outgoing = call(
        functools.partial(mix_kernel, shards),
        (shaped((each, grouped)), shaped((part_atoms, atom_wide)))
        + (shaped((capacity // 2, packed)),) * partners,
        (tile_source, tiles, *narrow_parts, send, send_mask),
        smem=(0,),
        scratch=[pltpu.VMEM((shards * lines, packed), jnp.bfloat16)],
        flops=2 * rows * rows * channels,
        nbytes=2 * rows * rows,
    )
    arrived = [
        lax.ppermute(block, "dom", [(at, at ^ (partners - place)) for at in range(domains)])
        for place, block in enumerate(outgoing)
    ]
    base = call(
        base_kernel,
        shaped((rows, wide), jnp.float32),
        (edges, trip_out, local, local_mask, weight_up, up_stack),
        flops=2 * rows * channels * (rows + 2 * wide),
        nbytes=2 * rows * rows + 6 * rows * wide,
    )
    state, sums = call(
        functools.partial(state_kernel, partners),
        (shaped((rows, wide)), shaped((part_atoms, atom_wide))),
        (base, fetch, fetch_mask, up_stack, weight_residual, weight_message, atom_index, *arrived),
        scratch=[pltpu.VMEM((column, grouped), jnp.bfloat16)],
        flops=4 * rows * wide * wide,
        nbytes=8 * rows * wide,
    )
    sums_parts = from_others(sums, shards)
    side, chosen = call(
        functools.partial(side_kernel, shards, part_atoms),
        (shaped((rows, wide), jnp.float32), shaped((rows, 2 * part_atoms))),
        (state, weight_join, atom_index),
        flops=2 * rows * wide * wide,
        nbytes=8 * rows * wide,
    )
    return call(
        functools.partial(final_kernel, shards, (rows // count) ** -0.5),
        (shaped((rows, wide), space=pltpu.HBM), shaped((count, atom_wide), space=pltpu.HBM)),
        (*sums_parts, all_atoms, weight_atom, weight_join, state, side, chosen),
        scratch=[
            pltpu.VMEM((2 * part_atoms, wide), jnp.bfloat16),
            pltpu.VMEM((rows, wide), jnp.bfloat16),
            pltpu.VMEM((count, atom_wide), jnp.bfloat16),
            pltpu.SemaphoreType.DMA((1 + len(row_chunks(rows)),)),
        ],
        flops=4 * rows * part_atoms * wide,
        nbytes=8 * rows * wide,
    )


def solution(mesh):
    split = P(("dom", "edge"))
    placed = (
        P(("dom", "edge"), None),
        P(("dom", "edge"), None),
        split,
        P(None, ("dom", "edge")),
        P(("dom", "edge"), None),
        P(("dom", "edge"), None, None),
    ) + (P(),) * 7
    return jax.shard_map(
        body,
        mesh=mesh,
        in_specs=placed,
        out_specs=(P(("dom", "edge"), None), P(("dom", "edge"), None)),
        check_vma=False,
    )
```

```python
import functools

import jax
import jax.numpy as jnp
from jax import lax
from jax.experimental import pallas as pl
from jax.experimental.pallas import tpu as pltpu
from jax.sharding import PartitionSpec as P

root_half = 0.7071067811865476
MIB = 1 << 20
CHUNK = 256
GROUPS = 4


def product(operand, weights):
    return jnp.dot(operand, weights, preferred_element_type=jnp.float32)


def silu(value):
    halved = 0.5 * value
    return halved + halved * jnp.tanh(halved)


def as_column(row):
    wide = jnp.broadcast_to(row.astype(jnp.float32), (8, row.shape[1]))
    return jnp.transpose(wide)[:, :1].astype(jnp.int32)


def row_chunks(rows):
    step = min(CHUNK, rows)
    return [slice(at, at + step) for at in range(0, rows, step)]


def call(kernel, outs, args, *, smem=(), hbm=(), scratch=(), flops=0, nbytes=0, limit=24):
    def space(at):
        return pltpu.SMEM if at in smem else pltpu.HBM if at in hbm else pltpu.VMEM

    args = [
        pltpu.with_memory_space_constraint(arg, pltpu.HBM) if at in hbm else arg
        for at, arg in enumerate(args)
    ]
    return pl.pallas_call(
        kernel,
        out_shape=outs,
        in_specs=[pl.BlockSpec(memory_space=space(at)) for at in range(len(args))],
        out_specs=jax.tree.map(
            lambda out: pl.BlockSpec(
                memory_space=pltpu.HBM if out.memory_space == pltpu.HBM else pltpu.VMEM
            ),
            outs,
        ),
        scratch_shapes=list(scratch),
        compiler_params=pltpu.CompilerParams(vmem_limit_bytes=limit * MIB),
        cost_estimate=pl.CostEstimate(flops=flops, bytes_accessed=nbytes, transcendentals=0),
    )(*args)


def shaped(shape, dtype=jnp.bfloat16, space=pltpu.VMEM):
    return space(tuple(shape), dtype)


def narrow_kernel(
    edges_hbm, weight_hbm, down_hbm, out_ref, edges_ref, weight_ref, down_ref, sems
):
    half = edges_hbm.shape[0] // 2
    pieces = [
        slice(base + rows.start, base + rows.stop)
        for rows in row_chunks(half)
        for base in (0, half)
    ]
    copies = [
        pltpu.make_async_copy(weight_hbm, weight_ref, sems.at[0]),
        pltpu.make_async_copy(down_hbm, down_ref, sems.at[1]),
    ] + [
        pltpu.make_async_copy(edges_hbm.at[piece], edges_ref.at[piece], sems.at[2 + at])
        for at, piece in enumerate(pieces)
    ]
    for copy in [copies[0], copies[2], copies[3], copies[1]] + copies[4:]:
        copy.start()
    copies[0].wait()
    copies[1].wait()
    for at, rows in enumerate(row_chunks(half)):
        copies[2 + 2 * at].wait()
        copies[3 + 2 * at].wait()
        hidden = [
            silu(product(edges_ref[piece, :], weight_ref[...])).astype(jnp.bfloat16)
            for piece in pieces[2 * at : 2 * at + 2]
        ]
        sides = [
            lax.dot_general(
                each, down_ref[...], (((1,), (1,)), ((), ())), preferred_element_type=jnp.float32
            )
            for each in hidden
        ]
        out_ref[rows, :] = silu(jnp.concatenate(sides, axis=1)).astype(jnp.bfloat16)


def one_hot(shape, axis, chosen):
    return (lax.broadcasted_iota(jnp.int32, shape, axis) == chosen).astype(jnp.bfloat16)


def group_mask(group, channels):
    column = lax.broadcasted_iota(jnp.int32, (group.shape[0], GROUPS * channels), 1)
    return (column // channels == group).astype(jnp.bfloat16)


def index_kernel(domains, shards, channels, operands, *refs):
    reverse_ref = refs[0]
    sources = refs[1 : 1 + operands]
    send_ref, send_mask_ref, fetch_ref, fetch_mask_ref, local_ref, local_mask_ref, stack_ref = refs[
        1 + operands : 8 + operands
    ]
    targets = refs[8 + operands : 8 + 2 * operands]
    sems = refs[-1]
    copies = [
        pltpu.make_async_copy(source, target, sems.at[at])
        for at, (source, target) in enumerate(zip(sources, targets))
    ] + [
        pltpu.make_async_copy(
            sources[0].at[1],
            stack_ref.at[at * channels : (at + 1) * channels, :],
            sems.at[operands + at],
        )
        for at in range(GROUPS)
    ]
    for copy in copies:
        copy.start()
    rows = reverse_ref.shape[1]
    each = rows // GROUPS
    capacity = rows // domains
    half = capacity // 2
    slots = (domains - 1) * capacity
    own = lax.axis_index("dom")
    reverse = reverse_ref[...]
    holder = reverse // (rows * shards)
    source_row = lax.rem(reverse, rows)
    partner = holder ^ own
    remote = partner != 0
    block = domains - 1 - partner
    member = one_hot((domains, rows), 0, partner)
    before = (
        lax.broadcasted_iota(jnp.int32, (rows, rows), 0)
        < lax.broadcasted_iota(jnp.int32, (rows, rows), 1)
    ).astype(jnp.bfloat16)
    earlier = (as_column(source_row) < source_row).astype(jnp.bfloat16)

    def rank(matrix):
        counts = product(member, matrix) * member.astype(jnp.float32)
        return jnp.sum(counts, axis=0, keepdims=True).astype(jnp.int32)

    place = rank(before)
    part = (place >= half).astype(jnp.int32)
    send_slot = part * (slots // 2) + block * half + place - part * half
    sent = one_hot((slots, rows), 0, jnp.where(remote, send_slot, -1))
    owner = (
        lax.broadcasted_iota(jnp.int32, (rows, GROUPS * channels), 0) // each
        == lax.broadcasted_iota(jnp.int32, (rows, GROUPS * channels), 1) // channels
    ).astype(jnp.bfloat16)
    send_mask_ref[...] = product(sent, owner).astype(jnp.bfloat16)
    folded = sent[:, :each]
    for at in range(1, GROUPS):
        folded = folded + sent[:, at * each : (at + 1) * each]
    send_ref[...] = folded

    far_place = rank(earlier)
    part = (far_place >= half).astype(jnp.int32)
    side = (block >= domains // 2).astype(jnp.int32)
    fetch_row = (block - side * (domains // 2)) * half + far_place - part * half
    fetch_ref[...] = one_hot(
        fetch_ref.shape, 1, as_column(jnp.where(remote, fetch_row, -1))
    )
    fetch_mask_ref[...] = group_mask(as_column(2 * side + part), channels)
    local_group = source_row // each
    local_row = source_row - local_group * each
    local_ref[...] = one_hot(local_ref.shape, 1, as_column(jnp.where(remote, -1, local_row)))
    local_mask_ref[...] = group_mask(as_column(local_group), channels)
    for copy in copies:
        copy.wait()


def picked_rows(chosen, table, mask):
    return product(chosen, table).astype(jnp.bfloat16) * mask


def mix_kernel(shards, *refs):
    source_ref, tiles_ref = refs[:2]
    parts = refs[2 : 2 + shards]
    send_ref, mask_ref, trip_ref = refs[2 + shards : 5 + shards]
    out_refs = refs[5 + shards : -1]
    held_ref = refs[-1]
    blocks, block_len, width = tiles_ref.shape
    count = width // block_len
    lines = held_ref.shape[0] // shards
    me = lax.axis_index("edge")
    for part, at in zip(parts, orders(shards)[0]):
        held_ref[at * lines : (at + 1) * lines, :] = part[...]
    half_blocks = blocks // 2
    channels = trip_ref.shape[1] // GROUPS
    per = blocks // GROUPS

    def mixed(block):
        picks = []
        for tile in range(count):
            source = source_ref[block, tile]
            shard = source // blocks
            within = source - shard * blocks
            upper = within // half_blocks
            start = (shard ^ me) * lines + (within - upper * half_blocks) * block_len
            rows = held_ref[pl.ds(pl.multiple_of(start, block_len), block_len), :]
            picks.append(jnp.where(upper == 1, rows[:, channels:], rows[:, :channels]))
        return product(tiles_ref[block], jnp.concatenate(picks, axis=0))

    for at in range(per):
        for group in range(0, GROUPS, 2):
            pair = [mixed((group + side) * per + at) for side in range(2)]
            trip_ref[
                at * block_len : (at + 1) * block_len, group * channels : (group + 2) * channels
            ] = jnp.concatenate(pair, axis=1).astype(jnp.bfloat16)
    half_slots = send_ref.shape[0] // 2
    parts = []
    for side in range(2):
        rows = slice(side * half_slots, (side + 1) * half_slots)
        found = product(send_ref[rows, :], trip_ref[...]) * mask_ref[rows, :].astype(jnp.float32)
        both = found[:, : 2 * channels] + found[:, 2 * channels :]
        parts.append(both + pltpu.roll(both, channels, 1))
    lane = lax.broadcasted_iota(jnp.int32, parts[0].shape, 1)
    packed = jnp.where(lane < channels, parts[0], parts[1]).astype(jnp.bfloat16)
    each = half_slots // len(out_refs)
    for at, out_ref in enumerate(out_refs):
        out_ref[...] = packed[at * each : (at + 1) * each, :]


def base_kernel(shards, *refs):
    edges_ref, trip_ref, local_ref, mask_ref, up_ref, stack_ref = refs[:6]
    atoms = refs[6 : 6 + shards]
    out_ref, atoms_ref = refs[6 + shards :]
    count = atoms[0].shape[0]
    for part, at in zip(atoms, orders(shards)[0]):
        atoms_ref[at * count : (at + 1) * count, :] = part[...]
    each = trip_ref.shape[0]
    channels = up_ref.shape[1]
    for group in range(GROUPS):
        rows = slice(group * each, (group + 1) * each)
        picked = picked_rows(local_ref[rows, :], trip_ref[...], mask_ref[rows, :])
        direct = trip_ref[:, group * channels : (group + 1) * channels]
        joined = product(direct, up_ref[0]) + product(picked, stack_ref[...])
        out_ref[rows, :] = edges_ref[rows, :].astype(jnp.float32) + joined * root_half


def state_kernel(partners, *refs):
    base_ref, fetch_ref, mask_ref, stack_ref, residual_ref, message_ref, index_ref = refs[:7]
    arrived = refs[7 : 7 + partners]
    state_ref, sums_ref, slots_ref = refs[7 + partners :]
    each, lanes = arrived[0].shape
    column = (partners + 1) // 2
    for at in range(partners):
        down, right = at % column, at // column
        slots_ref[down * each : (down + 1) * each, right * lanes : (right + 1) * lanes] = arrived[at][...]
    down, right = partners % column, partners // column
    slots_ref[down * each : (down + 1) * each, right * lanes : (right + 1) * lanes] = jnp.zeros(
        (each, lanes), slots_ref.dtype
    )
    part_atoms = sums_ref.shape[0]
    shards = lax.axis_size("edge")
    near = near_atoms(index_ref[1:2, :], part_atoms, shards)
    chosen = (
        lax.broadcasted_iota(jnp.int32, (part_atoms, near.shape[1]), 0) == near
    ).astype(jnp.bfloat16)
    chunks = row_chunks(base_ref.shape[0])
    gathered = None
    for first in range(0, len(chunks), 2):
        group = chunks[first : first + 2]
        picked = [
            picked_rows(fetch_ref[rows, :], slots_ref[...], mask_ref[rows, :]) for rows in group
        ]
        states = [
            (base_ref[rows, :] + product(each, stack_ref[...]) * root_half).astype(jnp.bfloat16)
            for rows, each in zip(group, picked)
        ]
        for layer in range(residual_ref.shape[0]):
            middles = [
                silu(product(each, residual_ref[layer, 0])).astype(jnp.bfloat16) for each in states
            ]
            branches = [silu(product(each, residual_ref[layer, 1])) for each in middles]
            states = [
                ((each.astype(jnp.float32) + branch) * root_half).astype(jnp.bfloat16)
                for each, branch in zip(states, branches)
            ]
        for rows, each in zip(group, states):
            state_ref[rows, :] = each
            term = product(chosen[:, rows], each)
            gathered = term if gathered is None else gathered + term
    sums_ref[...] = product(gathered.astype(jnp.bfloat16), message_ref[...]).astype(jnp.bfloat16)


def near_atoms(index, part_atoms, shards):
    count = part_atoms // shards
    holder = index // count
    return (holder ^ lax.axis_index("edge")) * count + lax.rem(index, count)


def side_kernel(shards, part_atoms, state_ref, join_ref, index_ref, out_ref, chosen_ref):
    width = join_ref.shape[0] - state_ref.shape[1]
    for rows in row_chunks(state_ref.shape[0]):
        out_ref[rows, :] = product(state_ref[rows, :], join_ref[width:, :])
    index = near_atoms(index_ref[...], part_atoms, shards)
    for end in range(2):
        column = as_column(index[end : end + 1, :])
        chosen_ref[:, end * part_atoms : (end + 1) * part_atoms] = (
            lax.broadcasted_iota(jnp.int32, (column.shape[0], part_atoms), 1) == column
        ).astype(jnp.bfloat16)


def final_kernel(shards, scale, *refs):
    sums = refs[:shards]
    atoms_ref, weight_ref, join_ref, state_ref, side_ref, chosen_ref = refs[shards : shards + 6]
    edges_hbm, own_hbm, table_ref, edges_ref, own_ref, sems = refs[shards + 6 :]
    part_atoms = atoms_ref.shape[0]
    count = part_atoms // shards
    total = sums[0][...].astype(jnp.float32)
    for by, part in list(zip(orders(shards)[1], sums))[1:]:
        pieces = [part[(at ^ by) * count : ((at ^ by) + 1) * count, :] for at in range(shards)]
        total = total + jnp.concatenate(pieces, axis=0).astype(jnp.float32)
    scaled = (total * scale).astype(jnp.bfloat16)
    middle = silu(product(scaled, weight_ref[0])).astype(jnp.bfloat16)
    renewed = (atoms_ref[...].astype(jnp.float32) + product(middle, weight_ref[1])).astype(jnp.bfloat16)
    own_ref[...] = renewed[:count, :]
    own_copy = pltpu.make_async_copy(own_ref, own_hbm, sems.at[0])
    own_copy.start()
    width = renewed.shape[1]
    for end in range(2):
        table_ref[end * part_atoms : (end + 1) * part_atoms, :] = product(
            renewed, join_ref[end * width : (end + 1) * width, :]
        ).astype(jnp.bfloat16)
    copies = [own_copy]
    chunks = row_chunks(state_ref.shape[0])
    for first in range(0, len(chunks), 2):
        group = chunks[first : first + 2]
        found = [product(chosen_ref[rows, :], table_ref[...]) + side_ref[rows, :] for rows in group]
        for at, (rows, each) in enumerate(zip(group, found)):
            state = state_ref[rows, :].astype(jnp.float32)
            edges_ref[rows, :] = ((state + silu(each)) * root_half).astype(jnp.bfloat16)
            copies.append(
                pltpu.make_async_copy(
                    edges_ref.at[rows], edges_hbm.at[rows], sems.at[1 + first + at]
                )
            )
            copies[-1].start()
    for copy in copies:
        copy.wait()


def orders(shards):
    if shards == 4:
        return [0, 1, 2, 3], [0, 1, 3, 2]
    return list(range(shards)), list(range(shards))


def from_others(value, order):
    return [value] + [
        lax.ppermute(value, "edge", [(at, at ^ by) for at in range(len(order))])
        for by in order[1:]
    ]


def body(
    edges,
    atoms,
    reverse,
    atom_index,
    tile_source,
    tiles,
    weight_edge,
    weight_down,
    weight_up,
    weight_residual,
    weight_message,
    weight_atom,
    weight_join,
):
    rows, wide = edges.shape
    channels = weight_down.shape[0]
    domains = lax.axis_size("dom")
    shards = lax.axis_size("edge")
    count, atom_wide = atoms.shape
    part_atoms = count * shards
    capacity = rows // domains
    partners = domains - 1
    slots = partners * capacity
    lines = rows // 2
    packed = 2 * channels

    narrow = call(
        narrow_kernel,
        shaped((lines, packed)),
        (edges, weight_edge, weight_down),
        hbm=(0, 1, 2),
        scratch=[
            pltpu.VMEM(edges.shape, jnp.bfloat16),
            pltpu.VMEM(weight_edge.shape, jnp.bfloat16),
            pltpu.VMEM(weight_down.shape, jnp.bfloat16),
            pltpu.SemaphoreType.DMA((2 + 2 * len(row_chunks(lines)),)),
        ],
        flops=2 * rows * wide * (wide + channels),
        nbytes=2 * (rows * wide + wide * wide),
    )
    atom_parts = from_others(atoms, orders(shards)[0])
    narrow_parts = from_others(narrow, orders(shards)[0])
    later = (
        weight_up, edges, tiles, weight_residual, weight_message, weight_join, weight_atom, atom_index
    )
    each, grouped = rows // GROUPS, GROUPS * channels
    column = domains // 2 * (capacity // 2)
    send, send_mask, fetch, fetch_mask, local, local_mask, up_stack, *later = call(
        functools.partial(index_kernel, domains, shards, channels, len(later)),
        (
            shaped((slots, each)),
            shaped((slots, grouped)),
            shaped((rows, column)),
            shaped((rows, grouped)),
            shaped((rows, each)),
            shaped((rows, grouped)),
            shaped((grouped, wide)),
        )
        + tuple(shaped(each.shape, each.dtype) for each in later),
        (reverse.reshape(1, rows), *later),
        hbm=range(1, 1 + len(later)),
        scratch=[pltpu.SemaphoreType.DMA((len(later) + GROUPS,))],
        flops=40 * rows * rows,
        nbytes=6 * rows * rows,
    )
    weight_up, edges, tiles, weight_residual, weight_message, weight_join, weight_atom, atom_index = later
    trip_out, *outgoing = call(
        functools.partial(mix_kernel, shards),
        (shaped((each, grouped)),) + (shaped((capacity // 2, packed)),) * partners,
        (tile_source, tiles, *narrow_parts, send, send_mask),
        smem=(0,),
        scratch=[pltpu.VMEM((shards * lines, packed), jnp.bfloat16)],
        flops=2 * rows * rows * channels,
        nbytes=2 * rows * rows,
    )
    arrived = [
        lax.ppermute(block, "dom", [(at, at ^ (partners - place)) for at in range(domains)])
        for place, block in enumerate(outgoing)
    ]
    base, all_atoms = call(
        functools.partial(base_kernel, shards),
        (shaped((rows, wide), jnp.float32), shaped((part_atoms, atom_wide))),
        (edges, trip_out, local, local_mask, weight_up, up_stack, *atom_parts),
        flops=2 * rows * channels * (rows + 2 * wide),
        nbytes=2 * rows * rows + 6 * rows * wide,
    )
    state, sums = call(
        functools.partial(state_kernel, partners),
        (shaped((rows, wide)), shaped((part_atoms, atom_wide))),
        (base, fetch, fetch_mask, up_stack, weight_residual, weight_message, atom_index, *arrived),
        scratch=[pltpu.VMEM((column, grouped), jnp.bfloat16)],
        flops=4 * rows * wide * wide,
        nbytes=8 * rows * wide,
    )
    sums_parts = from_others(sums, orders(shards)[1])
    side, chosen = call(
        functools.partial(side_kernel, shards, part_atoms),
        (shaped((rows, wide), jnp.float32), shaped((rows, 2 * part_atoms))),
        (state, weight_join, atom_index),
        flops=2 * rows * wide * wide,
        nbytes=8 * rows * wide,
    )
    return call(
        functools.partial(final_kernel, shards, (rows // count) ** -0.5),
        (shaped((rows, wide), space=pltpu.HBM), shaped((count, atom_wide), space=pltpu.HBM)),
        (*sums_parts, all_atoms, weight_atom, weight_join, state, side, chosen),
        scratch=[
            pltpu.VMEM((2 * part_atoms, wide), jnp.bfloat16),
            pltpu.VMEM((rows, wide), jnp.bfloat16),
            pltpu.VMEM((count, atom_wide), jnp.bfloat16),
            pltpu.SemaphoreType.DMA((1 + len(row_chunks(rows)),)),
        ],
        flops=4 * rows * part_atoms * wide,
        nbytes=8 * rows * wide,
    )


def solution(mesh):
    split = P(("dom", "edge"))
    placed = (
        P(("dom", "edge"), None),
        P(("dom", "edge"), None),
        split,
        P(None, ("dom", "edge")),
        P(("dom", "edge"), None),
        P(("dom", "edge"), None, None),
    ) + (P(),) * 7
    return jax.shard_map(
        body,
        mesh=mesh,
        in_specs=placed,
        out_specs=(P(("dom", "edge"), None), P(("dom", "edge"), None)),
        check_vma=False,
    )
```

```python
import functools

import jax
import jax.numpy as jnp
from jax import lax
from jax.experimental import pallas as pl
from jax.experimental.pallas import tpu as pltpu
from jax.sharding import PartitionSpec as P

root_half = 0.7071067811865476
MIB = 1 << 20
CHUNK = 256
LONG = 512
GROUPS = 4


def product(operand, weights):
    return jnp.dot(operand, weights, preferred_element_type=jnp.float32)


def silu(value):
    halved = 0.5 * value
    return halved + halved * jnp.tanh(halved)


def as_column(row):
    wide = jnp.broadcast_to(row.astype(jnp.float32), (8, row.shape[1]))
    return jnp.transpose(wide)[:, :1].astype(jnp.int32)


def row_chunks(rows, step=CHUNK):
    step = min(step, rows)
    return [slice(at, at + step) for at in range(0, rows, step)]


def call(kernel, outs, args, *, smem=(), hbm=(), scratch=(), flops=0, nbytes=0, limit=24):
    def space(at):
        return pltpu.SMEM if at in smem else pltpu.HBM if at in hbm else pltpu.VMEM

    args = [
        pltpu.with_memory_space_constraint(arg, pltpu.HBM) if at in hbm else arg
        for at, arg in enumerate(args)
    ]
    return pl.pallas_call(
        kernel,
        out_shape=outs,
        in_specs=[pl.BlockSpec(memory_space=space(at)) for at in range(len(args))],
        out_specs=jax.tree.map(
            lambda out: pl.BlockSpec(
                memory_space=pltpu.HBM if out.memory_space == pltpu.HBM else pltpu.VMEM
            ),
            outs,
        ),
        scratch_shapes=list(scratch),
        compiler_params=pltpu.CompilerParams(vmem_limit_bytes=limit * MIB),
        cost_estimate=pl.CostEstimate(flops=flops, bytes_accessed=nbytes, transcendentals=0),
    )(*args)


def shaped(shape, dtype=jnp.bfloat16, space=pltpu.VMEM):
    return space(tuple(shape), dtype)


def narrow_kernel(
    edges_hbm, weight_hbm, down_hbm, out_ref, edges_ref, weight_ref, down_ref, sems
):
    half = edges_hbm.shape[0] // 2
    pieces = [
        slice(base + rows.start, base + rows.stop)
        for rows in row_chunks(half, LONG)
        for base in (0, half)
    ]
    copies = [
        pltpu.make_async_copy(weight_hbm, weight_ref, sems.at[0]),
        pltpu.make_async_copy(down_hbm, down_ref, sems.at[1]),
    ] + [
        pltpu.make_async_copy(edges_hbm.at[piece], edges_ref.at[piece], sems.at[2 + at])
        for at, piece in enumerate(pieces)
    ]
    for copy in [copies[0], copies[2], copies[3], copies[1]] + copies[4:]:
        copy.start()
    copies[0].wait()
    copies[1].wait()
    for at, rows in enumerate(row_chunks(half, LONG)):
        copies[2 + 2 * at].wait()
        copies[3 + 2 * at].wait()
        hidden = [
            silu(product(edges_ref[piece, :], weight_ref[...])).astype(jnp.bfloat16)
            for piece in pieces[2 * at : 2 * at + 2]
        ]
        sides = [
            lax.dot_general(
                each, down_ref[...], (((1,), (1,)), ((), ())), preferred_element_type=jnp.float32
            )
            for each in hidden
        ]
        out_ref[rows, :] = silu(jnp.concatenate(sides, axis=1)).astype(jnp.bfloat16)


def one_hot(shape, axis, chosen):
    return (lax.broadcasted_iota(jnp.int32, shape, axis) == chosen).astype(jnp.bfloat16)


def group_mask(group, channels):
    column = lax.broadcasted_iota(jnp.int32, (group.shape[0], GROUPS * channels), 1)
    return (column // channels == group).astype(jnp.bfloat16)


def index_kernel(domains, shards, channels, operands, *refs):
    reverse_ref = refs[0]
    sources = refs[1 : 1 + operands]
    send_ref, send_mask_ref, fetch_ref, fetch_mask_ref, local_ref, local_mask_ref, stack_ref = refs[
        1 + operands : 8 + operands
    ]
    targets = refs[8 + operands : 8 + 2 * operands]
    sems = refs[-1]
    copies = [
        pltpu.make_async_copy(source, target, sems.at[at])
        for at, (source, target) in enumerate(zip(sources, targets))
    ] + [
        pltpu.make_async_copy(
            sources[0].at[1],
            stack_ref.at[at * channels : (at + 1) * channels, :],
            sems.at[operands + at],
        )
        for at in range(GROUPS)
    ]
    for copy in copies:
        copy.start()
    rows = reverse_ref.shape[1]
    each = rows // GROUPS
    capacity = rows // domains
    half = capacity // 2
    slots = (domains - 1) * capacity
    own = lax.axis_index("dom")
    reverse = reverse_ref[...]
    holder = reverse // (rows * shards)
    source_row = lax.rem(reverse, rows)
    partner = holder ^ own
    remote = partner != 0
    block = domains - 1 - partner
    member = one_hot((domains, rows), 0, partner)
    before = (
        lax.broadcasted_iota(jnp.int32, (rows, rows), 0)
        < lax.broadcasted_iota(jnp.int32, (rows, rows), 1)
    ).astype(jnp.bfloat16)
    earlier = (as_column(source_row) < source_row).astype(jnp.bfloat16)

    def rank(matrix):
        counts = product(member, matrix) * member.astype(jnp.float32)
        return jnp.sum(counts, axis=0, keepdims=True).astype(jnp.int32)

    place = rank(before)
    part = (place >= half).astype(jnp.int32)
    send_slot = part * (slots // 2) + block * half + place - part * half
    sent = one_hot((slots, rows), 0, jnp.where(remote, send_slot, -1))
    owner = (
        lax.broadcasted_iota(jnp.int32, (rows, GROUPS * channels), 0) // each
        == lax.broadcasted_iota(jnp.int32, (rows, GROUPS * channels), 1) // channels
    ).astype(jnp.bfloat16)
    send_mask_ref[...] = product(sent, owner).astype(jnp.bfloat16)
    folded = sent[:, :each]
    for at in range(1, GROUPS):
        folded = folded + sent[:, at * each : (at + 1) * each]
    send_ref[...] = folded

    far_place = rank(earlier)
    part = (far_place >= half).astype(jnp.int32)
    side = (block >= domains // 2).astype(jnp.int32)
    fetch_row = (block - side * (domains // 2)) * half + far_place - part * half
    fetch_ref[...] = one_hot(
        fetch_ref.shape, 1, as_column(jnp.where(remote, fetch_row, -1))
    )
    fetch_mask_ref[...] = group_mask(as_column(2 * side + part), channels)
    local_group = source_row // each
    local_row = source_row - local_group * each
    local_ref[...] = one_hot(local_ref.shape, 1, as_column(jnp.where(remote, -1, local_row)))
    local_mask_ref[...] = group_mask(as_column(local_group), channels)
    for copy in copies:
        copy.wait()


def picked_rows(chosen, table, mask):
    return product(chosen, table).astype(jnp.bfloat16) * mask


def mix_kernel(shards, *refs):
    source_ref, tiles_ref = refs[:2]
    parts = refs[2 : 2 + shards]
    send_ref, mask_ref, trip_ref = refs[2 + shards : 5 + shards]
    out_refs = refs[5 + shards : -1]
    held_ref = refs[-1]
    blocks, block_len, width = tiles_ref.shape
    count = width // block_len
    lines = held_ref.shape[0] // shards
    me = lax.axis_index("edge")
    for part, at in zip(parts, orders(shards)[0]):
        held_ref[at * lines : (at + 1) * lines, :] = part[...]
    half_blocks = blocks // 2
    channels = trip_ref.shape[1] // GROUPS
    per = blocks // GROUPS

    def mixed(block):
        picks = []
        for tile in range(count):
            source = source_ref[block, tile]
            shard = source // blocks
            within = source - shard * blocks
            upper = within // half_blocks
            start = (shard ^ me) * lines + (within - upper * half_blocks) * block_len
            rows = held_ref[pl.ds(pl.multiple_of(start, block_len), block_len), :]
            picks.append(jnp.where(upper == 1, rows[:, channels:], rows[:, :channels]))
        return product(tiles_ref[block], jnp.concatenate(picks, axis=0))

    for at in range(per):
        for group in range(0, GROUPS, 2):
            pair = [mixed((group + side) * per + at) for side in range(2)]
            trip_ref[
                at * block_len : (at + 1) * block_len, group * channels : (group + 2) * channels
            ] = jnp.concatenate(pair, axis=1).astype(jnp.bfloat16)
    half_slots = send_ref.shape[0] // 2
    parts = []
    for side in range(2):
        rows = slice(side * half_slots, (side + 1) * half_slots)
        found = product(send_ref[rows, :], trip_ref[...]) * mask_ref[rows, :].astype(jnp.float32)
        both = found[:, : 2 * channels] + found[:, 2 * channels :]
        parts.append(both + pltpu.roll(both, channels, 1))
    lane = lax.broadcasted_iota(jnp.int32, parts[0].shape, 1)
    packed = jnp.where(lane < channels, parts[0], parts[1]).astype(jnp.bfloat16)
    each = half_slots // len(out_refs)
    for at, out_ref in enumerate(out_refs):
        out_ref[...] = packed[at * each : (at + 1) * each, :]


def base_kernel(shards, *refs):
    edges_ref, trip_ref, local_ref, mask_ref, up_ref, stack_ref = refs[:6]
    atoms = refs[6 : 6 + shards]
    out_ref, atoms_ref = refs[6 + shards :]
    count = atoms[0].shape[0]
    for part, at in zip(atoms, orders(shards)[0]):
        atoms_ref[at * count : (at + 1) * count, :] = part[...]
    each = trip_ref.shape[0]
    channels = up_ref.shape[1]
    for group in range(GROUPS):
        rows = slice(group * each, (group + 1) * each)
        picked = picked_rows(local_ref[rows, :], trip_ref[...], mask_ref[rows, :])
        direct = trip_ref[:, group * channels : (group + 1) * channels]
        joined = product(direct, up_ref[0]) + product(picked, stack_ref[...])
        out_ref[rows, :] = edges_ref[rows, :].astype(jnp.float32) + joined * root_half


def state_kernel(partners, *refs):
    base_ref, fetch_ref, mask_ref, stack_ref, residual_ref, message_ref, index_ref = refs[:7]
    arrived = refs[7 : 7 + partners]
    state_ref, sums_ref, slots_ref = refs[7 + partners :]
    each, lanes = arrived[0].shape
    column = (partners + 1) // 2
    for at in range(partners):
        down, right = at % column, at // column
        slots_ref[down * each : (down + 1) * each, right * lanes : (right + 1) * lanes] = arrived[at][...]
    down, right = partners % column, partners // column
    slots_ref[down * each : (down + 1) * each, right * lanes : (right + 1) * lanes] = jnp.zeros(
        (each, lanes), slots_ref.dtype
    )
    part_atoms = sums_ref.shape[0]
    shards = lax.axis_size("edge")
    near = near_atoms(index_ref[1:2, :], part_atoms, shards)
    chosen = (
        lax.broadcasted_iota(jnp.int32, (part_atoms, near.shape[1]), 0) == near
    ).astype(jnp.bfloat16)
    chunks = row_chunks(base_ref.shape[0], LONG)
    gathered = None
    for first in range(0, len(chunks), 2):
        group = chunks[first : first + 2]
        picked = [
            picked_rows(fetch_ref[rows, :], slots_ref[...], mask_ref[rows, :]) for rows in group
        ]
        states = [
            (base_ref[rows, :] + product(each, stack_ref[...]) * root_half).astype(jnp.bfloat16)
            for rows, each in zip(group, picked)
        ]
        for layer in range(residual_ref.shape[0]):
            middles = [
                silu(product(each, residual_ref[layer, 0])).astype(jnp.bfloat16) for each in states
            ]
            branches = [silu(product(each, residual_ref[layer, 1])) for each in middles]
            states = [
                ((each.astype(jnp.float32) + branch) * root_half).astype(jnp.bfloat16)
                for each, branch in zip(states, branches)
            ]
        for rows, each in zip(group, states):
            state_ref[rows, :] = each
            term = product(chosen[:, rows], each)
            gathered = term if gathered is None else gathered + term
    sums_ref[...] = product(gathered.astype(jnp.bfloat16), message_ref[...]).astype(jnp.bfloat16)


def near_atoms(index, part_atoms, shards):
    count = part_atoms // shards
    holder = index // count
    return (holder ^ lax.axis_index("edge")) * count + lax.rem(index, count)


def side_kernel(shards, *refs):
    state_ref, join_ref, index_ref, atoms_ref, weight_ref, out_ref, chosen_ref, fixed_ref, onward_ref = refs
    part_atoms, width = atoms_ref.shape
    for rows in row_chunks(state_ref.shape[0]):
        out_ref[rows, :] = product(state_ref[rows, :], join_ref[2 * width :, :])
    index = near_atoms(index_ref[...], part_atoms, shards)
    for end in range(2):
        column = as_column(index[end : end + 1, :])
        chosen_ref[:, end * part_atoms : (end + 1) * part_atoms] = (
            lax.broadcasted_iota(jnp.int32, (column.shape[0], part_atoms), 1) == column
        ).astype(jnp.bfloat16)
        join = join_ref[end * width : (end + 1) * width, :]
        fixed_ref[end * part_atoms : (end + 1) * part_atoms, :] = product(atoms_ref[...], join)
        onward_ref[end * width : (end + 1) * width, :] = product(weight_ref[1], join).astype(
            jnp.bfloat16
        )


def final_kernel(shards, scale, *refs):
    sums = refs[:shards]
    atoms_ref, weight_ref, state_ref, side_ref, chosen_ref, fixed_ref, onward_ref = refs[
        shards : shards + 7
    ]
    edges_hbm, own_hbm, table_ref, edges_ref, own_ref, sems = refs[shards + 7 :]
    part_atoms = atoms_ref.shape[0]
    count = part_atoms // shards
    total = sums[0][...].astype(jnp.float32)
    for by, part in list(zip(orders(shards)[1], sums))[1:]:
        pieces = [part[(at ^ by) * count : ((at ^ by) + 1) * count, :] for at in range(shards)]
        total = total + jnp.concatenate(pieces, axis=0).astype(jnp.float32)
    scaled = (total * scale).astype(jnp.bfloat16)
    middle = silu(product(scaled, weight_ref[0])).astype(jnp.bfloat16)
    width = middle.shape[1]
    for end in range(2):
        rows = slice(end * part_atoms, (end + 1) * part_atoms)
        onward = product(middle, onward_ref[end * width : (end + 1) * width, :])
        table_ref[rows, :] = (fixed_ref[rows, :] + onward).astype(jnp.bfloat16)
    renewed = atoms_ref[:count, :].astype(jnp.float32) + product(middle[:count, :], weight_ref[1])
    own_ref[...] = renewed.astype(jnp.bfloat16)
    own_copy = pltpu.make_async_copy(own_ref, own_hbm, sems.at[0])
    own_copy.start()
    copies = [own_copy]
    chunks = row_chunks(state_ref.shape[0])
    for first in range(0, len(chunks), 2):
        group = chunks[first : first + 2]
        found = [product(chosen_ref[rows, :], table_ref[...]) + side_ref[rows, :] for rows in group]
        for at, (rows, each) in enumerate(zip(group, found)):
            state = state_ref[rows, :].astype(jnp.float32)
            edges_ref[rows, :] = ((state + silu(each)) * root_half).astype(jnp.bfloat16)
            copies.append(
                pltpu.make_async_copy(
                    edges_ref.at[rows], edges_hbm.at[rows], sems.at[1 + first + at]
                )
            )
            copies[-1].start()
    for copy in copies:
        copy.wait()


def orders(shards):
    if shards == 4:
        return [0, 1, 2, 3], [0, 1, 3, 2]
    return list(range(shards)), list(range(shards))


def from_others(value, order):
    return [value] + [
        lax.ppermute(value, "edge", [(at, at ^ by) for at in range(len(order))])
        for by in order[1:]
    ]


def body(
    edges,
    atoms,
    reverse,
    atom_index,
    tile_source,
    tiles,
    weight_edge,
    weight_down,
    weight_up,
    weight_residual,
    weight_message,
    weight_atom,
    weight_join,
):
    rows, wide = edges.shape
    channels = weight_down.shape[0]
    domains = lax.axis_size("dom")
    shards = lax.axis_size("edge")
    count, atom_wide = atoms.shape
    part_atoms = count * shards
    capacity = rows // domains
    partners = domains - 1
    slots = partners * capacity
    lines = rows // 2
    packed = 2 * channels

    narrow = call(
        narrow_kernel,
        shaped((lines, packed)),
        (edges, weight_edge, weight_down),
        hbm=(0, 1, 2),
        scratch=[
            pltpu.VMEM(edges.shape, jnp.bfloat16),
            pltpu.VMEM(weight_edge.shape, jnp.bfloat16),
            pltpu.VMEM(weight_down.shape, jnp.bfloat16),
            pltpu.SemaphoreType.DMA((2 + 2 * len(row_chunks(lines, LONG)),)),
        ],
        flops=2 * rows * wide * (wide + channels),
        nbytes=2 * (rows * wide + wide * wide),
    )
    atom_parts = from_others(atoms, orders(shards)[0])
    narrow_parts = from_others(narrow, orders(shards)[0])
    later = (
        weight_up, edges, tiles, weight_residual, weight_message, weight_join, weight_atom, atom_index
    )
    each, grouped = rows // GROUPS, GROUPS * channels
    column = domains // 2 * (capacity // 2)
    send, send_mask, fetch, fetch_mask, local, local_mask, up_stack, *later = call(
        functools.partial(index_kernel, domains, shards, channels, len(later)),
        (
            shaped((slots, each)),
            shaped((slots, grouped)),
            shaped((rows, column)),
            shaped((rows, grouped)),
            shaped((rows, each)),
            shaped((rows, grouped)),
            shaped((grouped, wide)),
        )
        + tuple(shaped(each.shape, each.dtype) for each in later),
        (reverse.reshape(1, rows), *later),
        hbm=range(1, 1 + len(later)),
        scratch=[pltpu.SemaphoreType.DMA((len(later) + GROUPS,))],
        flops=40 * rows * rows,
        nbytes=6 * rows * rows,
    )
    weight_up, edges, tiles, weight_residual, weight_message, weight_join, weight_atom, atom_index = later
    trip_out, *outgoing = call(
        functools.partial(mix_kernel, shards),
        (shaped((each, grouped)),) + (shaped((capacity // 2, packed)),) * partners,
        (tile_source, tiles, *narrow_parts, send, send_mask),
        smem=(0,),
        scratch=[pltpu.VMEM((shards * lines, packed), jnp.bfloat16)],
        flops=2 * rows * rows * channels,
        nbytes=2 * rows * rows,
    )
    arrived = [
        lax.ppermute(block, "dom", [(at, at ^ (partners - place)) for at in range(domains)])
        for place, block in enumerate(outgoing)
    ]
    base, all_atoms = call(
        functools.partial(base_kernel, shards),
        (shaped((rows, wide), jnp.float32), shaped((part_atoms, atom_wide))),
        (edges, trip_out, local, local_mask, weight_up, up_stack, *atom_parts),
        flops=2 * rows * channels * (rows + 2 * wide),
        nbytes=2 * rows * rows + 6 * rows * wide,
    )
    state, sums = call(
        functools.partial(state_kernel, partners),
        (shaped((rows, wide)), shaped((part_atoms, atom_wide))),
        (base, fetch, fetch_mask, up_stack, weight_residual, weight_message, atom_index, *arrived),
        scratch=[pltpu.VMEM((column, grouped), jnp.bfloat16)],
        flops=4 * rows * wide * wide,
        nbytes=8 * rows * wide,
    )
    sums_parts = from_others(sums, orders(shards)[1])
    side, chosen, fixed, onward = call(
        functools.partial(side_kernel, shards),
        (
            shaped((rows, wide), jnp.float32),
            shaped((rows, 2 * part_atoms)),
            shaped((2 * part_atoms, wide), jnp.float32),
            shaped((2 * atom_wide, wide)),
        ),
        (state, weight_join, atom_index, all_atoms, weight_atom),
        flops=2 * rows * wide * wide,
        nbytes=8 * rows * wide,
    )
    return call(
        functools.partial(final_kernel, shards, (rows // count) ** -0.5),
        (shaped((rows, wide), space=pltpu.HBM), shaped((count, atom_wide), space=pltpu.HBM)),
        (*sums_parts, all_atoms, weight_atom, state, side, chosen, fixed, onward),
        scratch=[
            pltpu.VMEM((2 * part_atoms, wide), jnp.bfloat16),
            pltpu.VMEM((rows, wide), jnp.bfloat16),
            pltpu.VMEM((count, atom_wide), jnp.bfloat16),
            pltpu.SemaphoreType.DMA((1 + len(row_chunks(rows)),)),
        ],
        flops=4 * rows * part_atoms * wide,
        nbytes=8 * rows * wide,
    )


def solution(mesh):
    split = P(("dom", "edge"))
    placed = (
        P(("dom", "edge"), None),
        P(("dom", "edge"), None),
        split,
        P(None, ("dom", "edge")),
        P(("dom", "edge"), None),
        P(("dom", "edge"), None, None),
    ) + (P(),) * 7
    return jax.shard_map(
        body,
        mesh=mesh,
        in_specs=placed,
        out_specs=(P(("dom", "edge"), None), P(("dom", "edge"), None)),
        check_vma=False,
    )
```

```python
import functools

import jax
import jax.numpy as jnp
from jax import lax
from jax.experimental import pallas as pl
from jax.experimental.pallas import tpu as pltpu
from jax.sharding import PartitionSpec as P

root_half = 0.7071067811865476
MIB = 1 << 20
CHUNK = 256
LONG = 512
GROUPS = 4


def product(operand, weights):
    return jnp.dot(operand, weights, preferred_element_type=jnp.float32)


def silu(value):
    halved = 0.5 * value
    return halved + halved * jnp.tanh(halved)


def narrow_silu(value):
    halved = value.astype(jnp.bfloat16) * jnp.bfloat16(0.5)
    return halved + halved * jnp.tanh(halved)


def as_column(row):
    wide = jnp.broadcast_to(row.astype(jnp.float32), (8, row.shape[1]))
    return jnp.transpose(wide)[:, :1].astype(jnp.int32)


def row_chunks(rows, step=CHUNK):
    step = min(step, rows)
    return [slice(at, at + step) for at in range(0, rows, step)]


def call(kernel, outs, args, *, smem=(), hbm=(), scratch=(), flops=0, nbytes=0, limit=24):
    def space(at):
        return pltpu.SMEM if at in smem else pltpu.HBM if at in hbm else pltpu.VMEM

    args = [
        pltpu.with_memory_space_constraint(arg, pltpu.HBM) if at in hbm else arg
        for at, arg in enumerate(args)
    ]
    return pl.pallas_call(
        kernel,
        out_shape=outs,
        in_specs=[pl.BlockSpec(memory_space=space(at)) for at in range(len(args))],
        out_specs=jax.tree.map(
            lambda out: pl.BlockSpec(
                memory_space=pltpu.HBM if out.memory_space == pltpu.HBM else pltpu.VMEM
            ),
            outs,
        ),
        scratch_shapes=list(scratch),
        compiler_params=pltpu.CompilerParams(vmem_limit_bytes=limit * MIB),
        cost_estimate=pl.CostEstimate(flops=flops, bytes_accessed=nbytes, transcendentals=0),
    )(*args)


def shaped(shape, dtype=jnp.bfloat16, space=pltpu.VMEM):
    return space(tuple(shape), dtype)


def narrow_kernel(edges_hbm, weight_hbm, down_hbm, out_ref, edges_ref, weight_ref, down_ref, sems):
    half = edges_hbm.shape[0] // 2
    cut = weight_hbm.shape[0] // 2
    copies = [pltpu.make_async_copy(down_hbm, down_ref, sems.at[0])]
    for at, rows in enumerate((slice(0, cut), slice(cut, 2 * cut))):
        copies.append(pltpu.make_async_copy(weight_hbm.at[rows], weight_ref.at[rows], sems.at[1 + at]))
    pieces = row_chunks(2 * half)
    for at, rows in enumerate(pieces):
        copies.append(pltpu.make_async_copy(edges_hbm.at[rows], edges_ref.at[rows], sems.at[3 + at]))
    for copy in copies[1:] + copies[:1]:
        copy.start()
    for copy in copies:
        copy.wait()
    hidden = [
        narrow_silu(product(edges_ref[side * half : (side + 1) * half, :], weight_ref[...]))
        for side in range(2)
    ]
    sides = [
        lax.dot_general(
            each, down_ref[...], (((1,), (1,)), ((), ())), preferred_element_type=jnp.float32
        )
        for each in hidden
    ]
    out_ref[...] = silu(jnp.concatenate(sides, axis=1)).astype(jnp.bfloat16)


def one_hot(shape, axis, chosen):
    return (lax.broadcasted_iota(jnp.int32, shape, axis) == chosen).astype(jnp.bfloat16)


def group_mask(group, channels):
    column = lax.broadcasted_iota(jnp.int32, (group.shape[0], GROUPS * channels), 1)
    return (column // channels == group).astype(jnp.bfloat16)


def index_kernel(domains, shards, channels, operands, *refs):
    reverse_ref = refs[0]
    sources = refs[1 : 1 + operands]
    send_ref, send_mask_ref, fetch_ref, fetch_mask_ref, local_ref, local_mask_ref, stack_ref = refs[
        1 + operands : 8 + operands
    ]
    targets = refs[8 + operands : 8 + 2 * operands]
    sems = refs[-1]
    copies = [
        pltpu.make_async_copy(source, target, sems.at[at])
        for at, (source, target) in enumerate(zip(sources, targets))
    ] + [
        pltpu.make_async_copy(
            sources[0].at[1],
            stack_ref.at[at * channels : (at + 1) * channels, :],
            sems.at[operands + at],
        )
        for at in range(GROUPS)
    ]
    for copy in copies:
        copy.start()
    rows = reverse_ref.shape[1]
    each = rows // GROUPS
    capacity = rows // domains
    half = capacity // 2
    slots = (domains - 1) * capacity
    own = lax.axis_index("dom")
    reverse = reverse_ref[...]
    holder = reverse // (rows * shards)
    source_row = lax.rem(reverse, rows)
    partner = holder ^ own
    remote = partner != 0
    block = domains - 1 - partner
    member = one_hot((domains, rows), 0, partner)
    before = (
        lax.broadcasted_iota(jnp.int32, (rows, rows), 0)
        < lax.broadcasted_iota(jnp.int32, (rows, rows), 1)
    ).astype(jnp.bfloat16)
    earlier = (as_column(source_row) < source_row).astype(jnp.bfloat16)

    def rank(matrix):
        counts = product(member, matrix) * member.astype(jnp.float32)
        return jnp.sum(counts, axis=0, keepdims=True).astype(jnp.int32)

    place = rank(before)
    part = (place >= half).astype(jnp.int32)
    send_slot = part * (slots // 2) + block * half + place - part * half
    sent = one_hot((slots, rows), 0, jnp.where(remote, send_slot, -1))
    owner = (
        lax.broadcasted_iota(jnp.int32, (rows, GROUPS * channels), 0) // each
        == lax.broadcasted_iota(jnp.int32, (rows, GROUPS * channels), 1) // channels
    ).astype(jnp.bfloat16)
    send_mask_ref[...] = product(sent, owner).astype(jnp.bfloat16)
    folded = sent[:, :each]
    for at in range(1, GROUPS):
        folded = folded + sent[:, at * each : (at + 1) * each]
    send_ref[...] = folded

    far_place = rank(earlier)
    part = (far_place >= half).astype(jnp.int32)
    side = (block >= domains // 2).astype(jnp.int32)
    fetch_row = (block - side * (domains // 2)) * half + far_place - part * half
    fetch_ref[...] = one_hot(
        fetch_ref.shape, 1, as_column(jnp.where(remote, fetch_row, -1))
    )
    fetch_mask_ref[...] = group_mask(as_column(2 * side + part), channels)
    local_group = source_row // each
    local_row = source_row - local_group * each
    local_ref[...] = one_hot(local_ref.shape, 1, as_column(jnp.where(remote, -1, local_row)))
    local_mask_ref[...] = group_mask(as_column(local_group), channels)
    for copy in copies:
        copy.wait()


def picked_rows(chosen, table, mask):
    return product(chosen, table).astype(jnp.bfloat16) * mask


def mix_kernel(shards, *refs):
    source_ref, tiles_ref = refs[:2]
    parts = refs[2 : 2 + shards]
    send_ref, mask_ref, trip_ref = refs[2 + shards : 5 + shards]
    out_refs = refs[5 + shards : -1]
    held_ref = refs[-1]
    blocks, block_len, width = tiles_ref.shape
    count = width // block_len
    lines = held_ref.shape[0] // shards
    me = lax.axis_index("edge")
    for part, at in zip(parts, orders(shards)[0]):
        held_ref[at * lines : (at + 1) * lines, :] = part[...]
    half_blocks = blocks // 2
    channels = trip_ref.shape[1] // GROUPS
    per = blocks // GROUPS

    def mixed(block):
        picks = []
        for tile in range(count):
            source = source_ref[block, tile]
            shard = source // blocks
            within = source - shard * blocks
            upper = within // half_blocks
            start = (shard ^ me) * lines + (within - upper * half_blocks) * block_len
            rows = held_ref[pl.ds(pl.multiple_of(start, block_len), block_len), :]
            picks.append(jnp.where(upper == 1, rows[:, channels:], rows[:, :channels]))
        return product(tiles_ref[block], jnp.concatenate(picks, axis=0))

    for at in range(per):
        for group in range(0, GROUPS, 2):
            pair = [mixed((group + side) * per + at) for side in range(2)]
            trip_ref[
                at * block_len : (at + 1) * block_len, group * channels : (group + 2) * channels
            ] = jnp.concatenate(pair, axis=1).astype(jnp.bfloat16)
    half_slots = send_ref.shape[0] // 2
    parts = []
    for side in range(2):
        rows = slice(side * half_slots, (side + 1) * half_slots)
        found = product(send_ref[rows, :], trip_ref[...]) * mask_ref[rows, :].astype(jnp.float32)
        both = found[:, : 2 * channels] + found[:, 2 * channels :]
        parts.append(both + pltpu.roll(both, channels, 1))
    lane = lax.broadcasted_iota(jnp.int32, parts[0].shape, 1)
    packed = jnp.where(lane < channels, parts[0], parts[1]).astype(jnp.bfloat16)
    each = half_slots // len(out_refs)
    for at, out_ref in enumerate(out_refs):
        out_ref[...] = packed[at * each : (at + 1) * each, :]


def base_kernel(shards, *refs):
    edges_ref, trip_ref, local_ref, mask_ref, up_ref, stack_ref = refs[:6]
    atoms = refs[6 : 6 + shards]
    out_ref, atoms_ref = refs[6 + shards :]
    count = atoms[0].shape[0]
    for part, at in zip(atoms, orders(shards)[0]):
        atoms_ref[at * count : (at + 1) * count, :] = part[...]
    each = trip_ref.shape[0]
    channels = up_ref.shape[1]
    for group in range(GROUPS):
        rows = slice(group * each, (group + 1) * each)
        picked = picked_rows(local_ref[rows, :], trip_ref[...], mask_ref[rows, :])
        direct = trip_ref[:, group * channels : (group + 1) * channels]
        joined = product(direct, up_ref[0]) + product(picked, stack_ref[...])
        out_ref[rows, :] = edges_ref[rows, :].astype(jnp.float32) + joined * root_half


def state_kernel(partners, *refs):
    base_ref, fetch_ref, mask_ref, stack_ref, residual_ref, message_ref, index_ref = refs[:7]
    arrived = refs[7 : 7 + partners]
    state_ref, sums_ref, slots_ref = refs[7 + partners :]
    each, lanes = arrived[0].shape
    column = (partners + 1) // 2
    for at in range(partners):
        down, right = at % column, at // column
        slots_ref[down * each : (down + 1) * each, right * lanes : (right + 1) * lanes] = arrived[at][...]
    down, right = partners % column, partners // column
    slots_ref[down * each : (down + 1) * each, right * lanes : (right + 1) * lanes] = jnp.zeros(
        (each, lanes), slots_ref.dtype
    )
    part_atoms = sums_ref.shape[0]
    shards = lax.axis_size("edge")
    near = near_atoms(index_ref[1:2, :], part_atoms, shards)
    chosen = (
        lax.broadcasted_iota(jnp.int32, (part_atoms, near.shape[1]), 0) == near
    ).astype(jnp.bfloat16)
    chunks = row_chunks(base_ref.shape[0], LONG)
    gathered = None
    for first in range(0, len(chunks), 2):
        group = chunks[first : first + 2]
        picked = [
            picked_rows(fetch_ref[rows, :], slots_ref[...], mask_ref[rows, :]) for rows in group
        ]
        states = [
            (base_ref[rows, :] + product(each, stack_ref[...]) * root_half).astype(jnp.bfloat16)
            for rows, each in zip(group, picked)
        ]
        for layer in range(residual_ref.shape[0]):
            middles = [narrow_silu(product(each, residual_ref[layer, 0])) for each in states]
            branches = [narrow_silu(product(each, residual_ref[layer, 1])) for each in middles]
            states = [
                (
                    (each.astype(jnp.float32) + branch.astype(jnp.float32)) * root_half
                ).astype(jnp.bfloat16)
                for each, branch in zip(states, branches)
            ]
        for rows, each in zip(group, states):
            state_ref[rows, :] = each
            term = product(chosen[:, rows], each)
            gathered = term if gathered is None else gathered + term
    sums_ref[...] = product(gathered.astype(jnp.bfloat16), message_ref[...]).astype(jnp.bfloat16)


def near_atoms(index, part_atoms, shards):
    count = part_atoms // shards
    holder = index // count
    return (holder ^ lax.axis_index("edge")) * count + lax.rem(index, count)


def side_kernel(shards, *refs):
    state_ref, join_ref, index_ref, atoms_ref, weight_ref, out_ref, chosen_ref, fixed_ref, onward_ref = refs
    part_atoms, width = atoms_ref.shape
    for rows in row_chunks(state_ref.shape[0]):
        out_ref[rows, :] = product(state_ref[rows, :], join_ref[2 * width :, :])
    index = near_atoms(index_ref[...], part_atoms, shards)
    for end in range(2):
        column = as_column(index[end : end + 1, :])
        chosen_ref[:, end * part_atoms : (end + 1) * part_atoms] = (
            lax.broadcasted_iota(jnp.int32, (column.shape[0], part_atoms), 1) == column
        ).astype(jnp.bfloat16)
        join = join_ref[end * width : (end + 1) * width, :]
        fixed_ref[end * part_atoms : (end + 1) * part_atoms, :] = product(atoms_ref[...], join)
        onward_ref[end * width : (end + 1) * width, :] = product(weight_ref[1], join).astype(
            jnp.bfloat16
        )


def final_kernel(shards, scale, *refs):
    sums = refs[:shards]
    atoms_ref, weight_ref, state_ref, side_ref, chosen_ref, fixed_ref, onward_ref = refs[
        shards : shards + 7
    ]
    edges_hbm, own_hbm, table_ref, edges_ref, own_ref, sems = refs[shards + 7 :]
    part_atoms = atoms_ref.shape[0]
    count = part_atoms // shards
    total = sums[0][...].astype(jnp.float32)
    for by, part in list(zip(orders(shards)[1], sums))[1:]:
        pieces = [part[(at ^ by) * count : ((at ^ by) + 1) * count, :] for at in range(shards)]
        total = total + jnp.concatenate(pieces, axis=0).astype(jnp.float32)
    scaled = (total * scale).astype(jnp.bfloat16)
    middle = silu(product(scaled, weight_ref[0])).astype(jnp.bfloat16)
    width = middle.shape[1]
    for end in range(2):
        rows = slice(end * part_atoms, (end + 1) * part_atoms)
        onward = product(middle, onward_ref[end * width : (end + 1) * width, :])
        table_ref[rows, :] = (fixed_ref[rows, :] + onward).astype(jnp.bfloat16)
    renewed = atoms_ref[:count, :].astype(jnp.float32) + product(middle[:count, :], weight_ref[1])
    own_ref[...] = renewed.astype(jnp.bfloat16)
    own_copy = pltpu.make_async_copy(own_ref, own_hbm, sems.at[0])
    own_copy.start()
    copies = [own_copy]
    chunks = row_chunks(state_ref.shape[0])
    for first in range(0, len(chunks), 2):
        group = chunks[first : first + 2]
        found = [product(chosen_ref[rows, :], table_ref[...]) + side_ref[rows, :] for rows in group]
        for at, (rows, each) in enumerate(zip(group, found)):
            state = state_ref[rows, :].astype(jnp.float32)
            update = narrow_silu(each).astype(jnp.float32)
            edges_ref[rows, :] = ((state + update) * root_half).astype(jnp.bfloat16)
            copies.append(
                pltpu.make_async_copy(
                    edges_ref.at[rows], edges_hbm.at[rows], sems.at[1 + first + at]
                )
            )
            copies[-1].start()
    for copy in copies:
        copy.wait()


def orders(shards):
    if shards == 4:
        return [0, 1, 2, 3], [0, 1, 3, 2]
    return list(range(shards)), list(range(shards))


def from_others(value, order):
    return [value] + [
        lax.ppermute(value, "edge", [(at, at ^ by) for at in range(len(order))])
        for by in order[1:]
    ]


def body(
    edges,
    atoms,
    reverse,
    atom_index,
    tile_source,
    tiles,
    weight_edge,
    weight_down,
    weight_up,
    weight_residual,
    weight_message,
    weight_atom,
    weight_join,
):
    rows, wide = edges.shape
    channels = weight_down.shape[0]
    domains = lax.axis_size("dom")
    shards = lax.axis_size("edge")
    count, atom_wide = atoms.shape
    part_atoms = count * shards
    capacity = rows // domains
    partners = domains - 1
    slots = partners * capacity
    lines = rows // 2
    packed = 2 * channels

    narrow = call(
        narrow_kernel,
        shaped((lines, packed)),
        (edges, weight_edge, weight_down),
        hbm=(0, 1, 2),
        scratch=[
            pltpu.VMEM(edges.shape, jnp.bfloat16),
            pltpu.VMEM(weight_edge.shape, jnp.bfloat16),
            pltpu.VMEM(weight_down.shape, jnp.bfloat16),
            pltpu.SemaphoreType.DMA((3 + len(row_chunks(rows)),)),
        ],
        flops=2 * rows * wide * (wide + channels),
        nbytes=2 * (rows * wide + wide * wide),
    )
    atom_parts = from_others(atoms, orders(shards)[0])
    narrow_parts = from_others(narrow, orders(shards)[0])
    later = (
        weight_up, edges, tiles, weight_residual, weight_message, weight_join, weight_atom, atom_index
    )
    each, grouped = rows // GROUPS, GROUPS * channels
    column = domains // 2 * (capacity // 2)
    send, send_mask, fetch, fetch_mask, local, local_mask, up_stack, *later = call(
        functools.partial(index_kernel, domains, shards, channels, len(later)),
        (
            shaped((slots, each)),
            shaped((slots, grouped)),
            shaped((rows, column)),
            shaped((rows, grouped)),
            shaped((rows, each)),
            shaped((rows, grouped)),
            shaped((grouped, wide)),
        )
        + tuple(shaped(each.shape, each.dtype) for each in later),
        (reverse.reshape(1, rows), *later),
        hbm=range(1, 1 + len(later)),
        scratch=[pltpu.SemaphoreType.DMA((len(later) + GROUPS,))],
        flops=40 * rows * rows,
        nbytes=6 * rows * rows,
    )
    weight_up, edges, tiles, weight_residual, weight_message, weight_join, weight_atom, atom_index = later
    trip_out, *outgoing = call(
        functools.partial(mix_kernel, shards),
        (shaped((each, grouped)),) + (shaped((capacity // 2, packed)),) * partners,
        (tile_source, tiles, *narrow_parts, send, send_mask),
        smem=(0,),
        scratch=[pltpu.VMEM((shards * lines, packed), jnp.bfloat16)],
        flops=2 * rows * rows * channels,
        nbytes=2 * rows * rows,
    )
    arrived = [
        lax.ppermute(block, "dom", [(at, at ^ (partners - place)) for at in range(domains)])
        for place, block in enumerate(outgoing)
    ]
    base, all_atoms = call(
        functools.partial(base_kernel, shards),
        (shaped((rows, wide), jnp.float32), shaped((part_atoms, atom_wide))),
        (edges, trip_out, local, local_mask, weight_up, up_stack, *atom_parts),
        flops=2 * rows * channels * (rows + 2 * wide),
        nbytes=2 * rows * rows + 6 * rows * wide,
    )
    state, sums = call(
        functools.partial(state_kernel, partners),
        (shaped((rows, wide)), shaped((part_atoms, atom_wide))),
        (base, fetch, fetch_mask, up_stack, weight_residual, weight_message, atom_index, *arrived),
        scratch=[pltpu.VMEM((column, grouped), jnp.bfloat16)],
        flops=4 * rows * wide * wide,
        nbytes=8 * rows * wide,
    )
    sums_parts = from_others(sums, orders(shards)[1])
    side, chosen, fixed, onward = call(
        functools.partial(side_kernel, shards),
        (
            shaped((rows, wide), jnp.float32),
            shaped((rows, 2 * part_atoms)),
            shaped((2 * part_atoms, wide), jnp.float32),
            shaped((2 * atom_wide, wide)),
        ),
        (state, weight_join, atom_index, all_atoms, weight_atom),
        flops=2 * rows * wide * wide,
        nbytes=8 * rows * wide,
    )
    return call(
        functools.partial(final_kernel, shards, (rows // count) ** -0.5),
        (shaped((rows, wide), space=pltpu.HBM), shaped((count, atom_wide), space=pltpu.HBM)),
        (*sums_parts, all_atoms, weight_atom, state, side, chosen, fixed, onward),
        scratch=[
            pltpu.VMEM((2 * part_atoms, wide), jnp.bfloat16),
            pltpu.VMEM((rows, wide), jnp.bfloat16),
            pltpu.VMEM((count, atom_wide), jnp.bfloat16),
            pltpu.SemaphoreType.DMA((1 + len(row_chunks(rows)),)),
        ],
        flops=4 * rows * part_atoms * wide,
        nbytes=8 * rows * wide,
    )


def solution(mesh):
    split = P(("dom", "edge"))
    placed = (
        P(("dom", "edge"), None),
        P(("dom", "edge"), None),
        split,
        P(None, ("dom", "edge")),
        P(("dom", "edge"), None),
        P(("dom", "edge"), None, None),
    ) + (P(),) * 7
    return jax.shard_map(
        body,
        mesh=mesh,
        in_specs=placed,
        out_specs=(P(("dom", "edge"), None), P(("dom", "edge"), None)),
        check_vma=False,
    )
```

```python
import functools

import jax
import jax.numpy as jnp
from jax import lax
from jax.experimental import pallas as pl
from jax.experimental.pallas import tpu as pltpu
from jax.sharding import PartitionSpec as P

root_half = 0.7071067811865476
MIB = 1 << 20
CHUNK = 256
LONG = 512
GROUPS = 4


def product(operand, weights):
    return jnp.dot(operand, weights, preferred_element_type=jnp.float32)


def silu(value):
    halved = 0.5 * value
    return halved + halved * jnp.tanh(halved)


def narrow_silu(value):
    halved = value.astype(jnp.bfloat16) * jnp.bfloat16(0.5)
    return halved + halved * jnp.tanh(halved)


def as_column(row):
    wide = jnp.broadcast_to(row.astype(jnp.float32), (8, row.shape[1]))
    return jnp.transpose(wide)[:, :1].astype(jnp.int32)


def row_chunks(rows, step=CHUNK):
    step = min(step, rows)
    return [slice(at, at + step) for at in range(0, rows, step)]


def call(kernel, outs, args, *, smem=(), hbm=(), scratch=(), flops=0, nbytes=0, limit=24):
    def space(at):
        return pltpu.SMEM if at in smem else pltpu.HBM if at in hbm else pltpu.VMEM

    args = [
        pltpu.with_memory_space_constraint(arg, pltpu.HBM) if at in hbm else arg
        for at, arg in enumerate(args)
    ]
    return pl.pallas_call(
        kernel,
        out_shape=outs,
        in_specs=[pl.BlockSpec(memory_space=space(at)) for at in range(len(args))],
        out_specs=jax.tree.map(
            lambda out: pl.BlockSpec(
                memory_space=pltpu.HBM if out.memory_space == pltpu.HBM else pltpu.VMEM
            ),
            outs,
        ),
        scratch_shapes=list(scratch),
        compiler_params=pltpu.CompilerParams(vmem_limit_bytes=limit * MIB),
        cost_estimate=pl.CostEstimate(flops=flops, bytes_accessed=nbytes, transcendentals=0),
    )(*args)


def shaped(shape, dtype=jnp.bfloat16, space=pltpu.VMEM):
    return space(tuple(shape), dtype)


def narrow_kernel(edges_hbm, weight_hbm, down_hbm, out_ref, edges_ref, weight_ref, down_ref, sems):
    half = edges_hbm.shape[0] // 2
    cut = weight_hbm.shape[0] // 2
    copies = [pltpu.make_async_copy(down_hbm, down_ref, sems.at[0])]
    for at, rows in enumerate((slice(0, cut), slice(cut, 2 * cut))):
        copies.append(pltpu.make_async_copy(weight_hbm.at[rows], weight_ref.at[rows], sems.at[1 + at]))
    pieces = row_chunks(2 * half)
    for at, rows in enumerate(pieces):
        copies.append(pltpu.make_async_copy(edges_hbm.at[rows], edges_ref.at[rows], sems.at[3 + at]))
    for copy in copies[1:] + copies[:1]:
        copy.start()
    for copy in copies:
        copy.wait()
    hidden = [
        narrow_silu(product(edges_ref[side * half : (side + 1) * half, :], weight_ref[...]))
        for side in range(2)
    ]
    sides = [
        lax.dot_general(
            each, down_ref[...], (((1,), (1,)), ((), ())), preferred_element_type=jnp.float32
        )
        for each in hidden
    ]
    out_ref[...] = silu(jnp.concatenate(sides, axis=1)).astype(jnp.bfloat16)


def one_hot(shape, axis, chosen):
    return (lax.broadcasted_iota(jnp.int32, shape, axis) == chosen).astype(jnp.bfloat16)


def group_mask(group, channels):
    column = lax.broadcasted_iota(jnp.int32, (group.shape[0], GROUPS * channels), 1)
    return (column // channels == group).astype(jnp.bfloat16)


def index_kernel(domains, shards, channels, operands, *refs):
    reverse_ref = refs[0]
    sources = refs[1 : 1 + operands]
    send_ref, send_mask_ref, fetch_ref, fetch_mask_ref, local_ref, local_mask_ref, stack_ref = refs[
        1 + operands : 8 + operands
    ]
    targets = refs[8 + operands : 8 + 2 * operands]
    sems = refs[-1]
    copies = [
        pltpu.make_async_copy(source, target, sems.at[at])
        for at, (source, target) in enumerate(zip(sources, targets))
    ] + [
        pltpu.make_async_copy(
            sources[0].at[1],
            stack_ref.at[at * channels : (at + 1) * channels, :],
            sems.at[operands + at],
        )
        for at in range(GROUPS)
    ]
    for copy in copies:
        copy.start()
    rows = reverse_ref.shape[1]
    each = rows // GROUPS
    capacity = rows // domains
    half = capacity // 2
    slots = (domains - 1) * capacity
    own = lax.axis_index("dom")
    reverse = reverse_ref[...]
    holder = reverse // (rows * shards)
    source_row = lax.rem(reverse, rows)
    partner = holder ^ own
    remote = partner != 0
    block = domains - 1 - partner
    member = one_hot((domains, rows), 0, partner)
    before = (
        lax.broadcasted_iota(jnp.int32, (rows, rows), 0)
        < lax.broadcasted_iota(jnp.int32, (rows, rows), 1)
    ).astype(jnp.bfloat16)
    earlier = (as_column(source_row) < source_row).astype(jnp.bfloat16)

    def rank(matrix):
        counts = product(member, matrix) * member.astype(jnp.float32)
        return jnp.sum(counts, axis=0, keepdims=True).astype(jnp.int32)

    place = rank(before)
    part = (place >= half).astype(jnp.int32)
    send_slot = part * (slots // 2) + block * half + place - part * half
    sent = one_hot((slots, rows), 0, jnp.where(remote, send_slot, -1))
    owner = (
        lax.broadcasted_iota(jnp.int32, (rows, GROUPS * channels), 0) // each
        == lax.broadcasted_iota(jnp.int32, (rows, GROUPS * channels), 1) // channels
    ).astype(jnp.bfloat16)
    send_mask_ref[...] = product(sent, owner).astype(jnp.bfloat16)
    folded = sent[:, :each]
    for at in range(1, GROUPS):
        folded = folded + sent[:, at * each : (at + 1) * each]
    send_ref[...] = folded

    far_place = rank(earlier)
    part = (far_place >= half).astype(jnp.int32)
    side = (block >= domains // 2).astype(jnp.int32)
    fetch_row = (block - side * (domains // 2)) * half + far_place - part * half
    fetch_ref[...] = one_hot(
        fetch_ref.shape, 1, as_column(jnp.where(remote, fetch_row, -1))
    )
    fetch_mask_ref[...] = group_mask(as_column(2 * side + part), channels)
    local_group = source_row // each
    local_row = source_row - local_group * each
    local_ref[...] = one_hot(local_ref.shape, 1, as_column(jnp.where(remote, -1, local_row)))
    local_mask_ref[...] = group_mask(as_column(local_group), channels)
    for copy in copies:
        copy.wait()


def picked_rows(chosen, table, mask):
    return product(chosen, table).astype(jnp.bfloat16) * mask


def mix_kernel(shards, *refs):
    start_ref, upper_ref, tiles_ref = refs[:3]
    parts = refs[3 : 3 + shards]
    send_ref, mask_ref, trip_ref = refs[3 + shards : 6 + shards]
    out_refs = refs[6 + shards : -1]
    held_ref = refs[-1]
    blocks, block_len, width = tiles_ref.shape
    count = width // block_len
    lines = held_ref.shape[0] // shards
    for part, at in zip(parts, orders(shards)[0]):
        held_ref[at * lines : (at + 1) * lines, :] = part[...]
    channels = trip_ref.shape[1] // GROUPS
    per = blocks // GROUPS

    def mixed(block):
        picks = []
        for tile in range(count):
            start = pl.multiple_of(start_ref[block * count + tile], block_len)
            rows = held_ref[pl.ds(start, block_len), :]
            upper = upper_ref[block * count + tile] == 1
            picks.append(jnp.where(upper, rows[:, channels:], rows[:, :channels]))
        return product(tiles_ref[block], jnp.concatenate(picks, axis=0))

    for at in range(per):
        for group in range(0, GROUPS, 2):
            pair = [mixed((group + side) * per + at) for side in range(2)]
            trip_ref[
                at * block_len : (at + 1) * block_len, group * channels : (group + 2) * channels
            ] = jnp.concatenate(pair, axis=1).astype(jnp.bfloat16)
    half_slots = send_ref.shape[0] // 2
    parts = []
    for side in range(2):
        rows = slice(side * half_slots, (side + 1) * half_slots)
        found = product(send_ref[rows, :], trip_ref[...]) * mask_ref[rows, :].astype(jnp.float32)
        both = found[:, : 2 * channels] + found[:, 2 * channels :]
        parts.append(both + pltpu.roll(both, channels, 1))
    lane = lax.broadcasted_iota(jnp.int32, parts[0].shape, 1)
    packed = jnp.where(lane < channels, parts[0], parts[1]).astype(jnp.bfloat16)
    each = half_slots // len(out_refs)
    for at, out_ref in enumerate(out_refs):
        out_ref[...] = packed[at * each : (at + 1) * each, :]


def base_kernel(shards, *refs):
    edges_ref, trip_ref, local_ref, mask_ref, up_ref, stack_ref = refs[:6]
    atoms = refs[6 : 6 + shards]
    out_ref, atoms_ref = refs[6 + shards :]
    count = atoms[0].shape[0]
    for part, at in zip(atoms, orders(shards)[0]):
        atoms_ref[at * count : (at + 1) * count, :] = part[...]
    each = trip_ref.shape[0]
    channels = up_ref.shape[1]
    for group in range(GROUPS):
        rows = slice(group * each, (group + 1) * each)
        picked = picked_rows(local_ref[rows, :], trip_ref[...], mask_ref[rows, :])
        direct = trip_ref[:, group * channels : (group + 1) * channels]
        joined = product(direct, up_ref[0]) + product(picked, stack_ref[...])
        out_ref[rows, :] = edges_ref[rows, :].astype(jnp.float32) + joined * root_half


def state_kernel(partners, *refs):
    base_ref, fetch_ref, mask_ref, stack_ref, residual_ref, message_ref, index_ref = refs[:7]
    arrived = refs[7 : 7 + partners]
    state_ref, sums_ref, slots_ref = refs[7 + partners :]
    each, lanes = arrived[0].shape
    column = (partners + 1) // 2
    for at in range(partners):
        down, right = at % column, at // column
        slots_ref[down * each : (down + 1) * each, right * lanes : (right + 1) * lanes] = arrived[at][...]
    down, right = partners % column, partners // column
    slots_ref[down * each : (down + 1) * each, right * lanes : (right + 1) * lanes] = jnp.zeros(
        (each, lanes), slots_ref.dtype
    )
    part_atoms = sums_ref.shape[0]
    shards = lax.axis_size("edge")
    near = near_atoms(index_ref[1:2, :], part_atoms, shards)
    chosen = (
        lax.broadcasted_iota(jnp.int32, (part_atoms, near.shape[1]), 0) == near
    ).astype(jnp.bfloat16)
    chunks = row_chunks(base_ref.shape[0], LONG)
    gathered = None
    for first in range(0, len(chunks), 2):
        group = chunks[first : first + 2]
        picked = [
            picked_rows(fetch_ref[rows, :], slots_ref[...], mask_ref[rows, :]) for rows in group
        ]
        states = [
            (base_ref[rows, :] + product(each, stack_ref[...]) * root_half).astype(jnp.bfloat16)
            for rows, each in zip(group, picked)
        ]
        for layer in range(residual_ref.shape[0]):
            middles = [narrow_silu(product(each, residual_ref[layer, 0])) for each in states]
            branches = [narrow_silu(product(each, residual_ref[layer, 1])) for each in middles]
            states = [
                (
                    (each.astype(jnp.float32) + branch.astype(jnp.float32)) * root_half
                ).astype(jnp.bfloat16)
                for each, branch in zip(states, branches)
            ]
        for rows, each in zip(group, states):
            state_ref[rows, :] = each
            term = product(chosen[:, rows], each)
            gathered = term if gathered is None else gathered + term
    sums_ref[...] = product(gathered.astype(jnp.bfloat16), message_ref[...]).astype(jnp.bfloat16)


def near_atoms(index, part_atoms, shards):
    count = part_atoms // shards
    holder = index // count
    return (holder ^ lax.axis_index("edge")) * count + lax.rem(index, count)


def side_kernel(shards, *refs):
    state_ref, join_ref, index_ref, atoms_ref, weight_ref, out_ref, chosen_ref, fixed_ref, onward_ref = refs
    part_atoms, width = atoms_ref.shape
    for rows in row_chunks(state_ref.shape[0]):
        out_ref[rows, :] = product(state_ref[rows, :], join_ref[2 * width :, :])
    index = near_atoms(index_ref[...], part_atoms, shards)
    for end in range(2):
        column = as_column(index[end : end + 1, :])
        chosen_ref[:, end * part_atoms : (end + 1) * part_atoms] = (
            lax.broadcasted_iota(jnp.int32, (column.shape[0], part_atoms), 1) == column
        ).astype(jnp.bfloat16)
        join = join_ref[end * width : (end + 1) * width, :]
        fixed_ref[end * part_atoms : (end + 1) * part_atoms, :] = product(atoms_ref[...], join)
        onward_ref[end * width : (end + 1) * width, :] = product(weight_ref[1], join).astype(
            jnp.bfloat16
        )


def final_kernel(shards, scale, *refs):
    sums = refs[:shards]
    atoms_ref, weight_ref, state_ref, side_ref, chosen_ref, fixed_ref, onward_ref = refs[
        shards : shards + 7
    ]
    edges_hbm, own_hbm, table_ref, edges_ref, own_ref, sems = refs[shards + 7 :]
    part_atoms = atoms_ref.shape[0]
    count = part_atoms // shards
    total = sums[0][...].astype(jnp.float32)
    for by, part in list(zip(orders(shards)[1], sums))[1:]:
        pieces = [part[(at ^ by) * count : ((at ^ by) + 1) * count, :] for at in range(shards)]
        total = total + jnp.concatenate(pieces, axis=0).astype(jnp.float32)
    scaled = (total * scale).astype(jnp.bfloat16)
    middle = silu(product(scaled, weight_ref[0])).astype(jnp.bfloat16)
    width = middle.shape[1]
    for end in range(2):
        rows = slice(end * part_atoms, (end + 1) * part_atoms)
        onward = product(middle, onward_ref[end * width : (end + 1) * width, :])
        table_ref[rows, :] = (fixed_ref[rows, :] + onward).astype(jnp.bfloat16)
    renewed = atoms_ref[:count, :].astype(jnp.float32) + product(middle[:count, :], weight_ref[1])
    own_ref[...] = renewed.astype(jnp.bfloat16)
    own_copy = pltpu.make_async_copy(own_ref, own_hbm, sems.at[0])
    own_copy.start()
    copies = [own_copy]
    chunks = row_chunks(state_ref.shape[0])
    for first in range(0, len(chunks), 2):
        group = chunks[first : first + 2]
        found = [product(chosen_ref[rows, :], table_ref[...]) + side_ref[rows, :] for rows in group]
        for at, (rows, each) in enumerate(zip(group, found)):
            state = state_ref[rows, :].astype(jnp.float32)
            update = narrow_silu(each).astype(jnp.float32)
            edges_ref[rows, :] = ((state + update) * root_half).astype(jnp.bfloat16)
            copies.append(
                pltpu.make_async_copy(
                    edges_ref.at[rows], edges_hbm.at[rows], sems.at[1 + first + at]
                )
            )
            copies[-1].start()
    for copy in copies:
        copy.wait()


def orders(shards):
    if shards == 4:
        return [0, 1, 2, 3], [0, 1, 3, 2]
    return list(range(shards)), list(range(shards))


def from_others(value, order):
    return [value] + [
        lax.ppermute(value, "edge", [(at, at ^ by) for at in range(len(order))])
        for by in order[1:]
    ]


def body(
    edges,
    atoms,
    reverse,
    atom_index,
    tile_source,
    tiles,
    weight_edge,
    weight_down,
    weight_up,
    weight_residual,
    weight_message,
    weight_atom,
    weight_join,
):
    rows, wide = edges.shape
    channels = weight_down.shape[0]
    domains = lax.axis_size("dom")
    shards = lax.axis_size("edge")
    count, atom_wide = atoms.shape
    part_atoms = count * shards
    capacity = rows // domains
    partners = domains - 1
    slots = partners * capacity
    lines = rows // 2
    packed = 2 * channels

    narrow = call(
        narrow_kernel,
        shaped((lines, packed)),
        (edges, weight_edge, weight_down),
        hbm=(0, 1, 2),
        scratch=[
            pltpu.VMEM(edges.shape, jnp.bfloat16),
            pltpu.VMEM(weight_edge.shape, jnp.bfloat16),
            pltpu.VMEM(weight_down.shape, jnp.bfloat16),
            pltpu.SemaphoreType.DMA((3 + len(row_chunks(rows)),)),
        ],
        flops=2 * rows * wide * (wide + channels),
        nbytes=2 * (rows * wide + wide * wide),
    )
    atom_parts = from_others(atoms, orders(shards)[0])
    narrow_parts = from_others(narrow, orders(shards)[0])
    later = (
        weight_up, edges, tiles, weight_residual, weight_message, weight_join, weight_atom, atom_index
    )
    each, grouped = rows // GROUPS, GROUPS * channels
    column = domains // 2 * (capacity // 2)
    send, send_mask, fetch, fetch_mask, local, local_mask, up_stack, *later = call(
        functools.partial(index_kernel, domains, shards, channels, len(later)),
        (
            shaped((slots, each)),
            shaped((slots, grouped)),
            shaped((rows, column)),
            shaped((rows, grouped)),
            shaped((rows, each)),
            shaped((rows, grouped)),
            shaped((grouped, wide)),
        )
        + tuple(shaped(each.shape, each.dtype) for each in later),
        (reverse.reshape(1, rows), *later),
        hbm=range(1, 1 + len(later)),
        scratch=[pltpu.SemaphoreType.DMA((len(later) + GROUPS,))],
        flops=40 * rows * rows,
        nbytes=6 * rows * rows,
    )
    weight_up, edges, tiles, weight_residual, weight_message, weight_join, weight_atom, atom_index = later
    blocks, block_len = tiles.shape[:2]
    source = tile_source.reshape(-1)
    within = lax.rem(source, blocks)
    upper = lax.div(within, blocks // 2)
    start = (lax.div(source, blocks) ^ lax.axis_index("edge")) * lines + (
        within - upper * (blocks // 2)
    ) * block_len
    trip_out, *outgoing = call(
        functools.partial(mix_kernel, shards),
        (shaped((each, grouped)),) + (shaped((capacity // 2, packed)),) * partners,
        (start, upper, tiles, *narrow_parts, send, send_mask),
        smem=(0, 1),
        scratch=[pltpu.VMEM((shards * lines, packed), jnp.bfloat16)],
        flops=2 * rows * rows * channels,
        nbytes=2 * rows * rows,
    )
    arrived = [
        lax.ppermute(block, "dom", [(at, at ^ (partners - place)) for at in range(domains)])
        for place, block in enumerate(outgoing)
    ]
    base, all_atoms = call(
        functools.partial(base_kernel, shards),
        (shaped((rows, wide), jnp.float32), shaped((part_atoms, atom_wide))),
        (edges, trip_out, local, local_mask, weight_up, up_stack, *atom_parts),
        flops=2 * rows * channels * (rows + 2 * wide),
        nbytes=2 * rows * rows + 6 * rows * wide,
    )
    state, sums = call(
        functools.partial(state_kernel, partners),
        (shaped((rows, wide)), shaped((part_atoms, atom_wide))),
        (base, fetch, fetch_mask, up_stack, weight_residual, weight_message, atom_index, *arrived),
        scratch=[pltpu.VMEM((column, grouped), jnp.bfloat16)],
        flops=4 * rows * wide * wide,
        nbytes=8 * rows * wide,
    )
    sums_parts = from_others(sums, orders(shards)[1])
    side, chosen, fixed, onward = call(
        functools.partial(side_kernel, shards),
        (
            shaped((rows, wide), jnp.float32),
            shaped((rows, 2 * part_atoms)),
            shaped((2 * part_atoms, wide), jnp.float32),
            shaped((2 * atom_wide, wide)),
        ),
        (state, weight_join, atom_index, all_atoms, weight_atom),
        flops=2 * rows * wide * wide,
        nbytes=8 * rows * wide,
    )
    return call(
        functools.partial(final_kernel, shards, (rows // count) ** -0.5),
        (shaped((rows, wide), space=pltpu.HBM), shaped((count, atom_wide), space=pltpu.HBM)),
        (*sums_parts, all_atoms, weight_atom, state, side, chosen, fixed, onward),
        scratch=[
            pltpu.VMEM((2 * part_atoms, wide), jnp.bfloat16),
            pltpu.VMEM((rows, wide), jnp.bfloat16),
            pltpu.VMEM((count, atom_wide), jnp.bfloat16),
            pltpu.SemaphoreType.DMA((1 + len(row_chunks(rows)),)),
        ],
        flops=4 * rows * part_atoms * wide,
        nbytes=8 * rows * wide,
    )


def solution(mesh):
    split = P(("dom", "edge"))
    placed = (
        P(("dom", "edge"), None),
        P(("dom", "edge"), None),
        split,
        P(None, ("dom", "edge")),
        P(("dom", "edge"), None),
        P(("dom", "edge"), None, None),
    ) + (P(),) * 7
    return jax.shard_map(
        body,
        mesh=mesh,
        in_specs=placed,
        out_specs=(P(("dom", "edge"), None), P(("dom", "edge"), None)),
        check_vma=False,
    )
```

```python
import functools

import jax
import jax.numpy as jnp
from jax import lax
from jax.experimental import pallas as pl
from jax.experimental.pallas import tpu as pltpu
from jax.sharding import PartitionSpec as P

root_half = 0.7071067811865476
MIB = 1 << 20
CHUNK = 256
LONG = 512
GROUPS = 4


def product(operand, weights):
    return jnp.dot(operand, weights, preferred_element_type=jnp.float32)


def silu(value):
    halved = 0.5 * value
    return halved + halved * jnp.tanh(halved)


def narrow_silu(value):
    halved = value.astype(jnp.bfloat16) * jnp.bfloat16(0.5)
    return halved + halved * jnp.tanh(halved)


def as_column(row):
    wide = jnp.broadcast_to(row.astype(jnp.float32), (8, row.shape[1]))
    return jnp.transpose(wide)[:, :1].astype(jnp.int32)


def row_chunks(rows, step=CHUNK):
    step = min(step, rows)
    return [slice(at, at + step) for at in range(0, rows, step)]


def call(kernel, outs, args, *, smem=(), hbm=(), scratch=(), flops=0, nbytes=0, limit=24):
    def space(at):
        return pltpu.SMEM if at in smem else pltpu.HBM if at in hbm else pltpu.VMEM

    args = [
        pltpu.with_memory_space_constraint(arg, pltpu.HBM) if at in hbm else arg
        for at, arg in enumerate(args)
    ]
    return pl.pallas_call(
        kernel,
        out_shape=outs,
        in_specs=[pl.BlockSpec(memory_space=space(at)) for at in range(len(args))],
        out_specs=jax.tree.map(
            lambda out: pl.BlockSpec(
                memory_space=pltpu.HBM if out.memory_space == pltpu.HBM else pltpu.VMEM
            ),
            outs,
        ),
        scratch_shapes=list(scratch),
        compiler_params=pltpu.CompilerParams(vmem_limit_bytes=limit * MIB),
        cost_estimate=pl.CostEstimate(flops=flops, bytes_accessed=nbytes, transcendentals=0),
    )(*args)


def shaped(shape, dtype=jnp.bfloat16, space=pltpu.VMEM):
    return space(tuple(shape), dtype)


def narrow_kernel(edges_hbm, weight_hbm, down_hbm, out_ref, edges_ref, weight_ref, down_ref, sems):
    half = edges_hbm.shape[0] // 2
    cut = weight_hbm.shape[0] // 2
    copies = [pltpu.make_async_copy(down_hbm, down_ref, sems.at[0])]
    for at, rows in enumerate((slice(0, cut), slice(cut, 2 * cut))):
        copies.append(pltpu.make_async_copy(weight_hbm.at[rows], weight_ref.at[rows], sems.at[1 + at]))
    pieces = row_chunks(2 * half)
    for at, rows in enumerate(pieces):
        copies.append(pltpu.make_async_copy(edges_hbm.at[rows], edges_ref.at[rows], sems.at[3 + at]))
    for copy in copies[1:] + copies[:1]:
        copy.start()
    first = 3 + len(pieces) // 2
    for copy in copies[1:first]:
        copy.wait()
    hidden = [narrow_silu(product(edges_ref[:half, :], weight_ref[...]))]
    for copy in copies[first:] + copies[:1]:
        copy.wait()
    hidden.append(narrow_silu(product(edges_ref[half:, :], weight_ref[...])))
    sides = [
        lax.dot_general(
            each, down_ref[...], (((1,), (1,)), ((), ())), preferred_element_type=jnp.float32
        )
        for each in hidden
    ]
    out_ref[...] = silu(jnp.concatenate(sides, axis=1)).astype(jnp.bfloat16)


def one_hot(shape, axis, chosen):
    return (lax.broadcasted_iota(jnp.int32, shape, axis) == chosen).astype(jnp.bfloat16)


def group_mask(group, channels):
    column = lax.broadcasted_iota(jnp.int32, (group.shape[0], GROUPS * channels), 1)
    return (column // channels == group).astype(jnp.bfloat16)


def index_kernel(domains, shards, channels, operands, *refs):
    reverse_ref = refs[0]
    sources = refs[1 : 1 + operands]
    send_ref, send_mask_ref, fetch_ref, fetch_mask_ref, local_ref, local_mask_ref, stack_ref = refs[
        1 + operands : 8 + operands
    ]
    targets = refs[8 + operands : 8 + 2 * operands]
    sems = refs[-1]
    copies = [
        pltpu.make_async_copy(source, target, sems.at[at])
        for at, (source, target) in enumerate(zip(sources, targets))
    ] + [
        pltpu.make_async_copy(
            sources[0].at[1],
            stack_ref.at[at * channels : (at + 1) * channels, :],
            sems.at[operands + at],
        )
        for at in range(GROUPS)
    ]
    for copy in copies:
        copy.start()
    rows = reverse_ref.shape[1]
    each = rows // GROUPS
    capacity = rows // domains
    half = capacity // 2
    slots = (domains - 1) * capacity
    own = lax.axis_index("dom")
    reverse = reverse_ref[...]
    holder = reverse // (rows * shards)
    source_row = lax.rem(reverse, rows)
    partner = holder ^ own
    remote = partner != 0
    block = domains - 1 - partner
    member = one_hot((domains, rows), 0, partner)
    before = (
        lax.broadcasted_iota(jnp.int32, (rows, rows), 0)
        < lax.broadcasted_iota(jnp.int32, (rows, rows), 1)
    ).astype(jnp.bfloat16)
    earlier = (as_column(source_row) < source_row).astype(jnp.bfloat16)

    def rank(matrix):
        counts = product(member, matrix) * member.astype(jnp.float32)
        return jnp.sum(counts, axis=0, keepdims=True).astype(jnp.int32)

    place = rank(before)
    part = (place >= half).astype(jnp.int32)
    send_slot = part * (slots // 2) + block * half + place - part * half
    sent = one_hot((slots, rows), 0, jnp.where(remote, send_slot, -1))
    owner = (
        lax.broadcasted_iota(jnp.int32, (rows, GROUPS * channels), 0) // each
        == lax.broadcasted_iota(jnp.int32, (rows, GROUPS * channels), 1) // channels
    ).astype(jnp.bfloat16)
    send_mask_ref[...] = product(sent, owner).astype(jnp.bfloat16)
    folded = sent[:, :each]
    for at in range(1, GROUPS):
        folded = folded + sent[:, at * each : (at + 1) * each]
    send_ref[...] = folded

    far_place = rank(earlier)
    part = (far_place >= half).astype(jnp.int32)
    side = (block >= domains // 2).astype(jnp.int32)
    fetch_row = (block - side * (domains // 2)) * half + far_place - part * half
    fetch_ref[...] = one_hot(
        fetch_ref.shape, 1, as_column(jnp.where(remote, fetch_row, -1))
    )
    fetch_mask_ref[...] = group_mask(as_column(2 * side + part), channels)
    local_group = source_row // each
    local_row = source_row - local_group * each
    local_ref[...] = one_hot(local_ref.shape, 1, as_column(jnp.where(remote, -1, local_row)))
    local_mask_ref[...] = group_mask(as_column(local_group), channels)
    for copy in copies:
        copy.wait()


def picked_rows(chosen, table, mask):
    return product(chosen, table).astype(jnp.bfloat16) * mask


def mix_kernel(shards, *refs):
    source_ref, tiles_ref = refs[:2]
    parts = refs[2 : 2 + shards]
    send_ref, mask_ref, trip_ref = refs[2 + shards : 5 + shards]
    out_refs = refs[5 + shards : -1]
    held_ref = refs[-1]
    blocks, block_len, width = tiles_ref.shape
    count = width // block_len
    lines = held_ref.shape[0] // shards
    me = lax.axis_index("edge")
    for part, at in zip(parts, orders(shards)[0]):
        held_ref[at * lines : (at + 1) * lines, :] = part[...]
    half_blocks = blocks // 2
    channels = trip_ref.shape[1] // GROUPS
    per = blocks // GROUPS

    def mixed(block):
        picks = []
        for tile in range(count):
            source = source_ref[block, tile]
            shard = lax.div(source, blocks)
            within = source - shard * blocks
            upper = (within >= half_blocks).astype(jnp.int32)
            start = (shard ^ me) * lines + (within - upper * half_blocks) * block_len
            rows = held_ref[pl.ds(pl.multiple_of(start, block_len), block_len), :]
            picks.append(jnp.where(upper == 1, rows[:, channels:], rows[:, :channels]))
        return product(tiles_ref[block], jnp.concatenate(picks, axis=0))

    for at in range(per):
        for group in range(0, GROUPS, 2):
            pair = [mixed((group + side) * per + at) for side in range(2)]
            trip_ref[
                at * block_len : (at + 1) * block_len, group * channels : (group + 2) * channels
            ] = jnp.concatenate(pair, axis=1).astype(jnp.bfloat16)
    half_slots = send_ref.shape[0] // 2
    parts = []
    for side in range(2):
        rows = slice(side * half_slots, (side + 1) * half_slots)
        found = product(send_ref[rows, :], trip_ref[...]) * mask_ref[rows, :].astype(jnp.float32)
        both = found[:, : 2 * channels] + found[:, 2 * channels :]
        parts.append(both + pltpu.roll(both, channels, 1))
    lane = lax.broadcasted_iota(jnp.int32, parts[0].shape, 1)
    packed = jnp.where(lane < channels, parts[0], parts[1]).astype(jnp.bfloat16)
    each = half_slots // len(out_refs)
    for at, out_ref in enumerate(out_refs):
        out_ref[...] = packed[at * each : (at + 1) * each, :]


def base_kernel(shards, *refs):
    edges_ref, trip_ref, local_ref, mask_ref, up_ref, stack_ref = refs[:6]
    atoms = refs[6 : 6 + shards]
    out_ref, atoms_ref = refs[6 + shards :]
    count = atoms[0].shape[0]
    for part, at in zip(atoms, orders(shards)[0]):
        atoms_ref[at * count : (at + 1) * count, :] = part[...]
    each = trip_ref.shape[0]
    channels = up_ref.shape[1]
    for group in range(GROUPS):
        rows = slice(group * each, (group + 1) * each)
        picked = picked_rows(local_ref[rows, :], trip_ref[...], mask_ref[rows, :])
        direct = trip_ref[:, group * channels : (group + 1) * channels]
        joined = product(direct, up_ref[0]) + product(picked, stack_ref[...])
        out_ref[rows, :] = edges_ref[rows, :].astype(jnp.float32) + joined * root_half


def state_kernel(partners, *refs):
    base_ref, fetch_ref, mask_ref, stack_ref, residual_ref, message_ref, index_ref = refs[:7]
    arrived = refs[7 : 7 + partners]
    state_ref, sums_ref, slots_ref = refs[7 + partners :]
    each, lanes = arrived[0].shape
    column = (partners + 1) // 2
    for at in range(partners):
        down, right = at % column, at // column
        slots_ref[down * each : (down + 1) * each, right * lanes : (right + 1) * lanes] = arrived[at][...]
    down, right = partners % column, partners // column
    slots_ref[down * each : (down + 1) * each, right * lanes : (right + 1) * lanes] = jnp.zeros(
        (each, lanes), slots_ref.dtype
    )
    part_atoms = sums_ref.shape[0]
    shards = lax.axis_size("edge")
    near = near_atoms(index_ref[1:2, :], part_atoms, shards)
    chosen = (
        lax.broadcasted_iota(jnp.int32, (part_atoms, near.shape[1]), 0) == near
    ).astype(jnp.bfloat16)
    chunks = row_chunks(base_ref.shape[0], LONG)
    gathered = None
    for first in range(0, len(chunks), 2):
        group = chunks[first : first + 2]
        picked = [
            picked_rows(fetch_ref[rows, :], slots_ref[...], mask_ref[rows, :]) for rows in group
        ]
        states = [
            (base_ref[rows, :] + product(each, stack_ref[...]) * root_half).astype(jnp.bfloat16)
            for rows, each in zip(group, picked)
        ]
        for layer in range(residual_ref.shape[0]):
            middles = [narrow_silu(product(each, residual_ref[layer, 0])) for each in states]
            branches = [narrow_silu(product(each, residual_ref[layer, 1])) for each in middles]
            states = [
                (
                    (each.astype(jnp.float32) + branch.astype(jnp.float32)) * root_half
                ).astype(jnp.bfloat16)
                for each, branch in zip(states, branches)
            ]
        for rows, each in zip(group, states):
            state_ref[rows, :] = each
            term = product(chosen[:, rows], each)
            gathered = term if gathered is None else gathered + term
    sums_ref[...] = product(gathered.astype(jnp.bfloat16), message_ref[...]).astype(jnp.bfloat16)


def near_atoms(index, part_atoms, shards):
    count = part_atoms // shards
    holder = index // count
    return (holder ^ lax.axis_index("edge")) * count + lax.rem(index, count)


def side_kernel(shards, *refs):
    state_ref, join_ref, index_ref, atoms_ref, weight_ref, out_ref, chosen_ref, fixed_ref, onward_ref = refs
    part_atoms, width = atoms_ref.shape
    for rows in row_chunks(state_ref.shape[0]):
        out_ref[rows, :] = product(state_ref[rows, :], join_ref[2 * width :, :])
    index = near_atoms(index_ref[...], part_atoms, shards)
    for end in range(2):
        column = as_column(index[end : end + 1, :])
        chosen_ref[:, end * part_atoms : (end + 1) * part_atoms] = (
            lax.broadcasted_iota(jnp.int32, (column.shape[0], part_atoms), 1) == column
        ).astype(jnp.bfloat16)
        join = join_ref[end * width : (end + 1) * width, :]
        fixed_ref[end * part_atoms : (end + 1) * part_atoms, :] = product(atoms_ref[...], join)
        onward_ref[end * width : (end + 1) * width, :] = product(weight_ref[1], join).astype(
            jnp.bfloat16
        )


def final_kernel(shards, scale, *refs):
    sums = refs[:shards]
    atoms_ref, weight_ref, state_ref, side_ref, chosen_ref, fixed_ref, onward_ref = refs[
        shards : shards + 7
    ]
    edges_hbm, own_hbm, table_ref, edges_ref, own_ref, sems = refs[shards + 7 :]
    part_atoms = atoms_ref.shape[0]
    count = part_atoms // shards
    total = sums[0][...].astype(jnp.float32)
    for by, part in list(zip(orders(shards)[1], sums))[1:]:
        pieces = [part[(at ^ by) * count : ((at ^ by) + 1) * count, :] for at in range(shards)]
        total = total + jnp.concatenate(pieces, axis=0).astype(jnp.float32)
    scaled = (total * scale).astype(jnp.bfloat16)
    middle = silu(product(scaled, weight_ref[0])).astype(jnp.bfloat16)
    width = middle.shape[1]
    for end in range(2):
        rows = slice(end * part_atoms, (end + 1) * part_atoms)
        onward = product(middle, onward_ref[end * width : (end + 1) * width, :])
        table_ref[rows, :] = (fixed_ref[rows, :] + onward).astype(jnp.bfloat16)
    renewed = atoms_ref[:count, :].astype(jnp.float32) + product(middle[:count, :], weight_ref[1])
    own_ref[...] = renewed.astype(jnp.bfloat16)
    own_copy = pltpu.make_async_copy(own_ref, own_hbm, sems.at[0])
    own_copy.start()
    copies = [own_copy]
    chunks = row_chunks(state_ref.shape[0])
    for first in range(0, len(chunks), 2):
        group = chunks[first : first + 2]
        found = [product(chosen_ref[rows, :], table_ref[...]) + side_ref[rows, :] for rows in group]
        for at, (rows, each) in enumerate(zip(group, found)):
            state = state_ref[rows, :].astype(jnp.float32)
            update = narrow_silu(each).astype(jnp.float32)
            edges_ref[rows, :] = ((state + update) * root_half).astype(jnp.bfloat16)
            copies.append(
                pltpu.make_async_copy(
                    edges_ref.at[rows], edges_hbm.at[rows], sems.at[1 + first + at]
                )
            )
            copies[-1].start()
    for copy in copies:
        copy.wait()


def orders(shards):
    if shards == 4:
        return [0, 1, 2, 3], [0, 1, 3, 2]
    return list(range(shards)), list(range(shards))


def from_others(value, order):
    return [value] + [
        lax.ppermute(value, "edge", [(at, at ^ by) for at in range(len(order))])
        for by in order[1:]
    ]


def body(
    edges,
    atoms,
    reverse,
    atom_index,
    tile_source,
    tiles,
    weight_edge,
    weight_down,
    weight_up,
    weight_residual,
    weight_message,
    weight_atom,
    weight_join,
):
    rows, wide = edges.shape
    channels = weight_down.shape[0]
    domains = lax.axis_size("dom")
    shards = lax.axis_size("edge")
    count, atom_wide = atoms.shape
    part_atoms = count * shards
    capacity = rows // domains
    partners = domains - 1
    slots = partners * capacity
    lines = rows // 2
    packed = 2 * channels

    narrow = call(
        narrow_kernel,
        shaped((lines, packed)),
        (edges, weight_edge, weight_down),
        hbm=(0, 1, 2),
        scratch=[
            pltpu.VMEM(edges.shape, jnp.bfloat16),
            pltpu.VMEM(weight_edge.shape, jnp.bfloat16),
            pltpu.VMEM(weight_down.shape, jnp.bfloat16),
            pltpu.SemaphoreType.DMA((3 + len(row_chunks(rows)),)),
        ],
        flops=2 * rows * wide * (wide + channels),
        nbytes=2 * (rows * wide + wide * wide),
    )
    atom_parts = from_others(atoms, orders(shards)[0])
    narrow_parts = from_others(narrow, orders(shards)[0])
    later = (
        weight_up, edges, tiles, weight_residual, weight_message, weight_join, weight_atom, atom_index
    )
    each, grouped = rows // GROUPS, GROUPS * channels
    column = domains // 2 * (capacity // 2)
    send, send_mask, fetch, fetch_mask, local, local_mask, up_stack, *later = call(
        functools.partial(index_kernel, domains, shards, channels, len(later)),
        (
            shaped((slots, each)),
            shaped((slots, grouped)),
            shaped((rows, column)),
            shaped((rows, grouped)),
            shaped((rows, each)),
            shaped((rows, grouped)),
            shaped((grouped, wide)),
        )
        + tuple(shaped(each.shape, each.dtype) for each in later),
        (reverse.reshape(1, rows), *later),
        hbm=range(1, 1 + len(later)),
        scratch=[pltpu.SemaphoreType.DMA((len(later) + GROUPS,))],
        flops=40 * rows * rows,
        nbytes=6 * rows * rows,
    )
    weight_up, edges, tiles, weight_residual, weight_message, weight_join, weight_atom, atom_index = later
    trip_out, *outgoing = call(
        functools.partial(mix_kernel, shards),
        (shaped((each, grouped)),) + (shaped((capacity // 2, packed)),) * partners,
        (tile_source, tiles, *narrow_parts, send, send_mask),
        smem=(0,),
        scratch=[pltpu.VMEM((shards * lines, packed), jnp.bfloat16)],
        flops=2 * rows * rows * channels,
        nbytes=2 * rows * rows,
    )
    arrived = [
        lax.ppermute(block, "dom", [(at, at ^ (partners - place)) for at in range(domains)])
        for place, block in enumerate(outgoing)
    ]
    base, all_atoms = call(
        functools.partial(base_kernel, shards),
        (shaped((rows, wide), jnp.float32), shaped((part_atoms, atom_wide))),
        (edges, trip_out, local, local_mask, weight_up, up_stack, *atom_parts),
        flops=2 * rows * channels * (rows + 2 * wide),
        nbytes=2 * rows * rows + 6 * rows * wide,
    )
    state, sums = call(
        functools.partial(state_kernel, partners),
        (shaped((rows, wide)), shaped((part_atoms, atom_wide))),
        (base, fetch, fetch_mask, up_stack, weight_residual, weight_message, atom_index, *arrived),
        scratch=[pltpu.VMEM((column, grouped), jnp.bfloat16)],
        flops=4 * rows * wide * wide,
        nbytes=8 * rows * wide,
    )
    sums_parts = from_others(sums, orders(shards)[1])
    side, chosen, fixed, onward = call(
        functools.partial(side_kernel, shards),
        (
            shaped((rows, wide), jnp.float32),
            shaped((rows, 2 * part_atoms)),
            shaped((2 * part_atoms, wide), jnp.float32),
            shaped((2 * atom_wide, wide)),
        ),
        (state, weight_join, atom_index, all_atoms, weight_atom),
        flops=2 * rows * wide * wide,
        nbytes=8 * rows * wide,
    )
    return call(
        functools.partial(final_kernel, shards, (rows // count) ** -0.5),
        (shaped((rows, wide), space=pltpu.HBM), shaped((count, atom_wide), space=pltpu.HBM)),
        (*sums_parts, all_atoms, weight_atom, state, side, chosen, fixed, onward),
        scratch=[
            pltpu.VMEM((2 * part_atoms, wide), jnp.bfloat16),
            pltpu.VMEM((rows, wide), jnp.bfloat16),
            pltpu.VMEM((count, atom_wide), jnp.bfloat16),
            pltpu.SemaphoreType.DMA((1 + len(row_chunks(rows)),)),
        ],
        flops=4 * rows * part_atoms * wide,
        nbytes=8 * rows * wide,
    )


def solution(mesh):
    split = P(("dom", "edge"))
    placed = (
        P(("dom", "edge"), None),
        P(("dom", "edge"), None),
        split,
        P(None, ("dom", "edge")),
        P(("dom", "edge"), None),
        P(("dom", "edge"), None, None),
    ) + (P(),) * 7
    return jax.shard_map(
        body,
        mesh=mesh,
        in_specs=placed,
        out_specs=(P(("dom", "edge"), None), P(("dom", "edge"), None)),
        check_vma=False,
    )
```

```python
import functools

import jax
import jax.numpy as jnp
from jax import lax
from jax.experimental import pallas as pl
from jax.experimental.pallas import tpu as pltpu
from jax.sharding import PartitionSpec as P

root_half = 0.7071067811865476
MIB = 1 << 20
CHUNK = 256
LONG = 512
GROUPS = 4


def product(operand, weights):
    return jnp.dot(operand, weights, preferred_element_type=jnp.float32)


def silu(value):
    halved = 0.5 * value
    return halved + halved * jnp.tanh(halved)


def narrow_silu(value):
    halved = value.astype(jnp.bfloat16) * jnp.bfloat16(0.5)
    return halved + halved * jnp.tanh(halved)


def as_column(row):
    wide = jnp.broadcast_to(row.astype(jnp.float32), (8, row.shape[1]))
    return jnp.transpose(wide)[:, :1].astype(jnp.int32)


def row_chunks(rows, step=CHUNK):
    step = min(step, rows)
    return [slice(at, at + step) for at in range(0, rows, step)]


def call(kernel, outs, args, *, smem=(), hbm=(), scratch=(), flops=0, nbytes=0, limit=24):
    def space(at):
        return pltpu.SMEM if at in smem else pltpu.HBM if at in hbm else pltpu.VMEM

    args = [
        pltpu.with_memory_space_constraint(arg, pltpu.HBM) if at in hbm else arg
        for at, arg in enumerate(args)
    ]
    return pl.pallas_call(
        kernel,
        out_shape=outs,
        in_specs=[pl.BlockSpec(memory_space=space(at)) for at in range(len(args))],
        out_specs=jax.tree.map(
            lambda out: pl.BlockSpec(
                memory_space=pltpu.HBM if out.memory_space == pltpu.HBM else pltpu.VMEM
            ),
            outs,
        ),
        scratch_shapes=list(scratch),
        compiler_params=pltpu.CompilerParams(vmem_limit_bytes=limit * MIB),
        cost_estimate=pl.CostEstimate(flops=flops, bytes_accessed=nbytes, transcendentals=0),
    )(*args)


def shaped(shape, dtype=jnp.bfloat16, space=pltpu.VMEM):
    return space(tuple(shape), dtype)


def narrow_kernel(edges_hbm, weight_hbm, down_hbm, out_ref, edges_ref, weight_ref, down_ref, sems):
    half = edges_hbm.shape[0] // 2
    cut = weight_hbm.shape[0] // 2
    copies = [pltpu.make_async_copy(down_hbm, down_ref, sems.at[0])]
    for at, rows in enumerate((slice(0, cut), slice(cut, 2 * cut))):
        copies.append(pltpu.make_async_copy(weight_hbm.at[rows], weight_ref.at[rows], sems.at[1 + at]))
    pieces = row_chunks(2 * half)
    for at, rows in enumerate(pieces):
        copies.append(pltpu.make_async_copy(edges_hbm.at[rows], edges_ref.at[rows], sems.at[3 + at]))
    for copy in copies[1:] + copies[:1]:
        copy.start()
    for copy in copies:
        copy.wait()
    hidden = [
        narrow_silu(product(edges_ref[side * half : (side + 1) * half, :], weight_ref[...]))
        for side in range(2)
    ]
    sides = [
        lax.dot_general(
            each, down_ref[...], (((1,), (1,)), ((), ())), preferred_element_type=jnp.float32
        )
        for each in hidden
    ]
    out_ref[...] = silu(jnp.concatenate(sides, axis=1)).astype(jnp.bfloat16)


def one_hot(shape, axis, chosen):
    return (lax.broadcasted_iota(jnp.int32, shape, axis) == chosen).astype(jnp.bfloat16)


def group_mask(group, channels):
    column = lax.broadcasted_iota(jnp.int32, (group.shape[0], GROUPS * channels), 1)
    return (column // channels == group).astype(jnp.bfloat16)


def index_kernel(domains, shards, channels, operands, *refs):
    reverse_ref = refs[0]
    sources = refs[1 : 1 + operands]
    send_ref, send_mask_ref, fetch_ref, fetch_mask_ref, local_ref, local_mask_ref, stack_ref = refs[
        1 + operands : 8 + operands
    ]
    targets = refs[8 + operands : 8 + 2 * operands]
    sems = refs[-1]
    copies = [
        pltpu.make_async_copy(source, target, sems.at[at])
        for at, (source, target) in enumerate(zip(sources, targets))
    ] + [
        pltpu.make_async_copy(
            sources[0].at[1],
            stack_ref.at[at * channels : (at + 1) * channels, :],
            sems.at[operands + at],
        )
        for at in range(GROUPS)
    ]
    for copy in copies:
        copy.start()
    rows = reverse_ref.shape[1]
    each = rows // GROUPS
    capacity = rows // domains
    half = capacity // 2
    slots = (domains - 1) * capacity
    own = lax.axis_index("dom")
    reverse = reverse_ref[...]
    holder = reverse // (rows * shards)
    source_row = lax.rem(reverse, rows)
    partner = holder ^ own
    remote = partner != 0
    block = domains - 1 - partner
    member = one_hot((domains, rows), 0, partner)
    before = (
        lax.broadcasted_iota(jnp.int32, (rows, rows), 0)
        < lax.broadcasted_iota(jnp.int32, (rows, rows), 1)
    ).astype(jnp.bfloat16)
    earlier = (as_column(source_row) < source_row).astype(jnp.bfloat16)

    def rank(matrix):
        counts = product(member, matrix) * member.astype(jnp.float32)
        return jnp.sum(counts, axis=0, keepdims=True).astype(jnp.int32)

    place = rank(before)
    part = (place >= half).astype(jnp.int32)
    send_slot = part * (slots // 2) + block * half + place - part * half
    sent = one_hot((slots, rows), 0, jnp.where(remote, send_slot, -1))
    owner = (
        lax.broadcasted_iota(jnp.int32, (rows, GROUPS * channels), 0) // each
        == lax.broadcasted_iota(jnp.int32, (rows, GROUPS * channels), 1) // channels
    ).astype(jnp.bfloat16)
    send_mask_ref[...] = product(sent, owner).astype(jnp.bfloat16)
    folded = sent[:, :each]
    for at in range(1, GROUPS):
        folded = folded + sent[:, at * each : (at + 1) * each]
    send_ref[...] = folded

    far_place = rank(earlier)
    part = (far_place >= half).astype(jnp.int32)
    side = (block >= domains // 2).astype(jnp.int32)
    fetch_row = (block - side * (domains // 2)) * half + far_place - part * half
    fetch_ref[...] = one_hot(
        fetch_ref.shape, 1, as_column(jnp.where(remote, fetch_row, -1))
    )
    fetch_mask_ref[...] = group_mask(as_column(2 * side + part), channels)
    local_group = source_row // each
    local_row = source_row - local_group * each
    local_ref[...] = one_hot(local_ref.shape, 1, as_column(jnp.where(remote, -1, local_row)))
    local_mask_ref[...] = group_mask(as_column(local_group), channels)
    for copy in copies:
        copy.wait()


def picked_rows(chosen, table, mask):
    return product(chosen, table).astype(jnp.bfloat16) * mask


def mix_kernel(shards, *refs):
    source_ref, tiles_ref = refs[:2]
    parts = refs[2 : 2 + shards]
    send_ref, mask_ref, trip_ref = refs[2 + shards : 5 + shards]
    out_refs = refs[5 + shards : -1]
    held_ref = refs[-1]
    blocks, block_len, width = tiles_ref.shape
    count = width // block_len
    lines = held_ref.shape[0] // shards
    me = lax.axis_index("edge")
    for part, at in zip(parts, orders(shards)[0]):
        held_ref[at * lines : (at + 1) * lines, :] = part[...]
    half_blocks = blocks // 2
    channels = trip_ref.shape[1] // GROUPS
    per = blocks // GROUPS

    def mixed(block):
        picks = []
        for tile in range(count):
            source = source_ref[block, tile]
            shard = lax.div(source, blocks)
            within = source - shard * blocks
            upper = (within >= half_blocks).astype(jnp.int32)
            start = (shard ^ me) * lines + (within - upper * half_blocks) * block_len
            rows = held_ref[pl.ds(pl.multiple_of(start, block_len), block_len), :]
            picks.append(jnp.where(upper == 1, rows[:, channels:], rows[:, :channels]))
        return product(tiles_ref[block], jnp.concatenate(picks, axis=0))

    for at in range(per):
        for group in range(0, GROUPS, 2):
            pair = [mixed((group + side) * per + at) for side in range(2)]
            trip_ref[
                at * block_len : (at + 1) * block_len, group * channels : (group + 2) * channels
            ] = jnp.concatenate(pair, axis=1).astype(jnp.bfloat16)
    half_slots = send_ref.shape[0] // 2
    parts = []
    for side in range(2):
        rows = slice(side * half_slots, (side + 1) * half_slots)
        found = product(send_ref[rows, :], trip_ref[...]) * mask_ref[rows, :].astype(jnp.float32)
        both = found[:, : 2 * channels] + found[:, 2 * channels :]
        parts.append(both + pltpu.roll(both, channels, 1))
    lane = lax.broadcasted_iota(jnp.int32, parts[0].shape, 1)
    packed = jnp.where(lane < channels, parts[0], parts[1]).astype(jnp.bfloat16)
    each = half_slots // len(out_refs)
    for at, out_ref in enumerate(out_refs):
        out_ref[...] = packed[at * each : (at + 1) * each, :]


def base_kernel(shards, *refs):
    edges_ref, trip_ref, local_ref, mask_ref, up_ref, stack_ref = refs[:6]
    atoms = refs[6 : 6 + shards]
    out_ref, atoms_ref = refs[6 + shards :]
    count = atoms[0].shape[0]
    for part, at in zip(atoms, orders(shards)[0]):
        atoms_ref[at * count : (at + 1) * count, :] = part[...]
    each = trip_ref.shape[0]
    channels = up_ref.shape[1]
    for group in range(GROUPS):
        rows = slice(group * each, (group + 1) * each)
        picked = picked_rows(local_ref[rows, :], trip_ref[...], mask_ref[rows, :])
        direct = trip_ref[:, group * channels : (group + 1) * channels]
        joined = product(direct, up_ref[0]) + product(picked, stack_ref[...])
        out_ref[rows, :] = edges_ref[rows, :].astype(jnp.float32) + joined * root_half


def state_kernel(partners, *refs):
    base_ref, fetch_ref, mask_ref, stack_ref, residual_ref, message_ref, index_ref = refs[:7]
    arrived = refs[7 : 7 + partners]
    state_ref, sums_ref, slots_ref = refs[7 + partners :]
    each, lanes = arrived[0].shape
    column = (partners + 1) // 2
    for at in range(partners):
        down, right = at % column, at // column
        slots_ref[down * each : (down + 1) * each, right * lanes : (right + 1) * lanes] = arrived[at][...]
    down, right = partners % column, partners // column
    slots_ref[down * each : (down + 1) * each, right * lanes : (right + 1) * lanes] = jnp.zeros(
        (each, lanes), slots_ref.dtype
    )
    part_atoms = sums_ref.shape[0]
    shards = lax.axis_size("edge")
    near = near_atoms(index_ref[1:2, :], part_atoms, shards)
    chosen = (
        lax.broadcasted_iota(jnp.int32, (part_atoms, near.shape[1]), 0) == near
    ).astype(jnp.bfloat16)
    chunks = row_chunks(base_ref.shape[0], LONG)
    gathered = None
    for first in range(0, len(chunks), 2):
        group = chunks[first : first + 2]
        picked = [
            picked_rows(fetch_ref[rows, :], slots_ref[...], mask_ref[rows, :]) for rows in group
        ]
        states = [
            (base_ref[rows, :] + product(each, stack_ref[...]) * root_half).astype(jnp.bfloat16)
            for rows, each in zip(group, picked)
        ]
        for layer in range(residual_ref.shape[0]):
            middles = [narrow_silu(product(each, residual_ref[layer, 0])) for each in states]
            branches = [narrow_silu(product(each, residual_ref[layer, 1])) for each in middles]
            states = [
                (
                    (each.astype(jnp.float32) + branch.astype(jnp.float32)) * root_half
                ).astype(jnp.bfloat16)
                for each, branch in zip(states, branches)
            ]
        for rows, each in zip(group, states):
            state_ref[rows, :] = each
            term = product(chosen[:, rows], each)
            gathered = term if gathered is None else gathered + term
    sums_ref[...] = product(gathered.astype(jnp.bfloat16), message_ref[...]).astype(jnp.bfloat16)


def near_atoms(index, part_atoms, shards):
    count = part_atoms // shards
    holder = index // count
    return (holder ^ lax.axis_index("edge")) * count + lax.rem(index, count)


def side_kernel(shards, *refs):
    state_ref, join_ref, index_ref, atoms_ref, weight_ref, out_ref, chosen_ref, fixed_ref, onward_ref = refs
    part_atoms, width = atoms_ref.shape
    for rows in row_chunks(state_ref.shape[0]):
        out_ref[rows, :] = product(state_ref[rows, :], join_ref[2 * width :, :])
    index = near_atoms(index_ref[...], part_atoms, shards)
    for end in range(2):
        column = as_column(index[end : end + 1, :])
        chosen_ref[:, end * part_atoms : (end + 1) * part_atoms] = (
            lax.broadcasted_iota(jnp.int32, (column.shape[0], part_atoms), 1) == column
        ).astype(jnp.bfloat16)
        join = join_ref[end * width : (end + 1) * width, :]
        fixed_ref[end * part_atoms : (end + 1) * part_atoms, :] = product(atoms_ref[...], join)
        onward_ref[end * width : (end + 1) * width, :] = product(weight_ref[1], join).astype(
            jnp.bfloat16
        )


def final_kernel(shards, scale, *refs):
    sums = refs[:shards]
    atoms_ref, weight_ref, state_ref, side_ref, chosen_ref, fixed_ref, onward_ref = refs[
        shards : shards + 7
    ]
    edges_hbm, own_hbm, table_ref, edges_ref, own_ref, sems = refs[shards + 7 :]
    part_atoms = atoms_ref.shape[0]
    count = part_atoms // shards
    total = sums[0][...].astype(jnp.float32)
    for by, part in list(zip(orders(shards)[1], sums))[1:]:
        pieces = [part[(at ^ by) * count : ((at ^ by) + 1) * count, :] for at in range(shards)]
        total = total + jnp.concatenate(pieces, axis=0).astype(jnp.float32)
    scaled = (total * scale).astype(jnp.bfloat16)
    middle = silu(product(scaled, weight_ref[0])).astype(jnp.bfloat16)
    width = middle.shape[1]
    for end in range(2):
        rows = slice(end * part_atoms, (end + 1) * part_atoms)
        onward = product(middle, onward_ref[end * width : (end + 1) * width, :])
        table_ref[rows, :] = (fixed_ref[rows, :] + onward).astype(jnp.bfloat16)
    renewed = atoms_ref[:count, :].astype(jnp.float32) + product(middle[:count, :], weight_ref[1])
    own_ref[...] = renewed.astype(jnp.bfloat16)
    own_copy = pltpu.make_async_copy(own_ref, own_hbm, sems.at[0])
    own_copy.start()
    copies = [own_copy]
    chunks = row_chunks(state_ref.shape[0])
    for first in range(0, len(chunks), 2):
        group = chunks[first : first + 2]
        found = [product(chosen_ref[rows, :], table_ref[...]) + side_ref[rows, :] for rows in group]
        for at, (rows, each) in enumerate(zip(group, found)):
            state = state_ref[rows, :].astype(jnp.float32)
            update = narrow_silu(each).astype(jnp.float32)
            edges_ref[rows, :] = ((state + update) * root_half).astype(jnp.bfloat16)
            copies.append(
                pltpu.make_async_copy(
                    edges_ref.at[rows], edges_hbm.at[rows], sems.at[1 + first + at]
                )
            )
            copies[-1].start()
    for copy in copies:
        copy.wait()


def orders(shards):
    if shards == 4:
        return [0, 1, 3, 2], [0, 1, 3, 2]
    return list(range(shards)), list(range(shards))


def from_others(value, order):
    return [value] + [
        lax.ppermute(value, "edge", [(at, at ^ by) for at in range(len(order))])
        for by in order[1:]
    ]


def body(
    edges,
    atoms,
    reverse,
    atom_index,
    tile_source,
    tiles,
    weight_edge,
    weight_down,
    weight_up,
    weight_residual,
    weight_message,
    weight_atom,
    weight_join,
):
    rows, wide = edges.shape
    channels = weight_down.shape[0]
    domains = lax.axis_size("dom")
    shards = lax.axis_size("edge")
    count, atom_wide = atoms.shape
    part_atoms = count * shards
    capacity = rows // domains
    partners = domains - 1
    slots = partners * capacity
    lines = rows // 2
    packed = 2 * channels

    narrow = call(
        narrow_kernel,
        shaped((lines, packed)),
        (edges, weight_edge, weight_down),
        hbm=(0, 1, 2),
        scratch=[
            pltpu.VMEM(edges.shape, jnp.bfloat16),
            pltpu.VMEM(weight_edge.shape, jnp.bfloat16),
            pltpu.VMEM(weight_down.shape, jnp.bfloat16),
            pltpu.SemaphoreType.DMA((3 + len(row_chunks(rows)),)),
        ],
        flops=2 * rows * wide * (wide + channels),
        nbytes=2 * (rows * wide + wide * wide),
    )
    atom_parts = from_others(atoms, orders(shards)[0])
    narrow_parts = from_others(narrow, orders(shards)[0])
    later = (
        weight_up, edges, tiles, weight_residual, weight_message, weight_join, weight_atom, atom_index
    )
    each, grouped = rows // GROUPS, GROUPS * channels
    column = domains // 2 * (capacity // 2)
    send, send_mask, fetch, fetch_mask, local, local_mask, up_stack, *later = call(
        functools.partial(index_kernel, domains, shards, channels, len(later)),
        (
            shaped((slots, each)),
            shaped((slots, grouped)),
            shaped((rows, column)),
            shaped((rows, grouped)),
            shaped((rows, each)),
            shaped((rows, grouped)),
            shaped((grouped, wide)),
        )
        + tuple(shaped(each.shape, each.dtype) for each in later),
        (reverse.reshape(1, rows), *later),
        hbm=range(1, 1 + len(later)),
        scratch=[pltpu.SemaphoreType.DMA((len(later) + GROUPS,))],
        flops=40 * rows * rows,
        nbytes=6 * rows * rows,
    )
    weight_up, edges, tiles, weight_residual, weight_message, weight_join, weight_atom, atom_index = later
    trip_out, *outgoing = call(
        functools.partial(mix_kernel, shards),
        (shaped((each, grouped)),) + (shaped((capacity // 2, packed)),) * partners,
        (tile_source, tiles, *narrow_parts, send, send_mask),
        smem=(0,),
        scratch=[pltpu.VMEM((shards * lines, packed), jnp.bfloat16)],
        flops=2 * rows * rows * channels,
        nbytes=2 * rows * rows,
    )
    arrived = [
        lax.ppermute(block, "dom", [(at, at ^ (partners - place)) for at in range(domains)])
        for place, block in enumerate(outgoing)
    ]
    base, all_atoms = call(
        functools.partial(base_kernel, shards),
        (shaped((rows, wide), jnp.float32), shaped((part_atoms, atom_wide))),
        (edges, trip_out, local, local_mask, weight_up, up_stack, *atom_parts),
        flops=2 * rows * channels * (rows + 2 * wide),
        nbytes=2 * rows * rows + 6 * rows * wide,
    )
    state, sums = call(
        functools.partial(state_kernel, partners),
        (shaped((rows, wide)), shaped((part_atoms, atom_wide))),
        (base, fetch, fetch_mask, up_stack, weight_residual, weight_message, atom_index, *arrived),
        scratch=[pltpu.VMEM((column, grouped), jnp.bfloat16)],
        flops=4 * rows * wide * wide,
        nbytes=8 * rows * wide,
    )
    sums_parts = from_others(sums, orders(shards)[1])
    side, chosen, fixed, onward = call(
        functools.partial(side_kernel, shards),
        (
            shaped((rows, wide), jnp.float32),
            shaped((rows, 2 * part_atoms)),
            shaped((2 * part_atoms, wide), jnp.float32),
            shaped((2 * atom_wide, wide)),
        ),
        (state, weight_join, atom_index, all_atoms, weight_atom),
        flops=2 * rows * wide * wide,
        nbytes=8 * rows * wide,
    )
    return call(
        functools.partial(final_kernel, shards, (rows // count) ** -0.5),
        (shaped((rows, wide), space=pltpu.HBM), shaped((count, atom_wide), space=pltpu.HBM)),
        (*sums_parts, all_atoms, weight_atom, state, side, chosen, fixed, onward),
        scratch=[
            pltpu.VMEM((2 * part_atoms, wide), jnp.bfloat16),
            pltpu.VMEM((rows, wide), jnp.bfloat16),
            pltpu.VMEM((count, atom_wide), jnp.bfloat16),
            pltpu.SemaphoreType.DMA((1 + len(row_chunks(rows)),)),
        ],
        flops=4 * rows * part_atoms * wide,
        nbytes=8 * rows * wide,
    )


def solution(mesh):
    split = P(("dom", "edge"))
    placed = (
        P(("dom", "edge"), None),
        P(("dom", "edge"), None),
        split,
        P(None, ("dom", "edge")),
        P(("dom", "edge"), None),
        P(("dom", "edge"), None, None),
    ) + (P(),) * 7
    return jax.shard_map(
        body,
        mesh=mesh,
        in_specs=placed,
        out_specs=(P(("dom", "edge"), None), P(("dom", "edge"), None)),
        check_vma=False,
    )
```

```python
import functools

import jax
import jax.numpy as jnp
from jax import lax
from jax.experimental import pallas as pl
from jax.experimental.pallas import tpu as pltpu
from jax.sharding import PartitionSpec as P

root_half = 0.7071067811865476
MIB = 1 << 20
CHUNK = 256
LONG = 512
GROUPS = 4


def product(operand, weights):
    return jnp.dot(operand, weights, preferred_element_type=jnp.float32)


def silu(value):
    halved = 0.5 * value
    return halved + halved * jnp.tanh(halved)


def narrow_silu(value):
    halved = value.astype(jnp.bfloat16) * jnp.bfloat16(0.5)
    return halved + halved * jnp.tanh(halved)


def as_column(row):
    wide = jnp.broadcast_to(row.astype(jnp.float32), (8, row.shape[1]))
    return jnp.transpose(wide)[:, :1].astype(jnp.int32)


def row_chunks(rows, step=CHUNK):
    step = min(step, rows)
    return [slice(at, at + step) for at in range(0, rows, step)]


def call(kernel, outs, args, *, smem=(), hbm=(), scratch=(), flops=0, nbytes=0, limit=24):
    def space(at):
        return pltpu.SMEM if at in smem else pltpu.HBM if at in hbm else pltpu.VMEM

    args = [
        pltpu.with_memory_space_constraint(arg, pltpu.HBM) if at in hbm else arg
        for at, arg in enumerate(args)
    ]
    return pl.pallas_call(
        kernel,
        out_shape=outs,
        in_specs=[pl.BlockSpec(memory_space=space(at)) for at in range(len(args))],
        out_specs=jax.tree.map(
            lambda out: pl.BlockSpec(
                memory_space=pltpu.HBM if out.memory_space == pltpu.HBM else pltpu.VMEM
            ),
            outs,
        ),
        scratch_shapes=list(scratch),
        compiler_params=pltpu.CompilerParams(vmem_limit_bytes=limit * MIB),
        cost_estimate=pl.CostEstimate(flops=flops, bytes_accessed=nbytes, transcendentals=0),
    )(*args)


def shaped(shape, dtype=jnp.bfloat16, space=pltpu.VMEM):
    return space(tuple(shape), dtype)


def narrow_kernel(edges_hbm, weight_hbm, down_hbm, out_ref, edges_ref, weight_ref, down_ref, sems):
    half = edges_hbm.shape[0] // 2
    cut = weight_hbm.shape[0] // 2
    copies = [pltpu.make_async_copy(down_hbm, down_ref, sems.at[0])]
    for at, rows in enumerate((slice(0, cut), slice(cut, 2 * cut))):
        copies.append(pltpu.make_async_copy(weight_hbm.at[rows], weight_ref.at[rows], sems.at[1 + at]))
    pieces = row_chunks(2 * half)
    for at, rows in enumerate(pieces):
        copies.append(pltpu.make_async_copy(edges_hbm.at[rows], edges_ref.at[rows], sems.at[3 + at]))
    for copy in copies[1:] + copies[:1]:
        copy.start()
    for copy in copies:
        copy.wait()
    hidden = [
        narrow_silu(product(edges_ref[side * half : (side + 1) * half, :], weight_ref[...]))
        for side in range(2)
    ]
    sides = [
        lax.dot_general(
            each, down_ref[...], (((1,), (1,)), ((), ())), preferred_element_type=jnp.float32
        )
        for each in hidden
    ]
    out_ref[...] = silu(jnp.concatenate(sides, axis=1)).astype(jnp.bfloat16)


def one_hot(shape, axis, chosen):
    return (lax.broadcasted_iota(jnp.int32, shape, axis) == chosen).astype(jnp.bfloat16)


def group_mask(group, channels):
    column = lax.broadcasted_iota(jnp.int32, (group.shape[0], GROUPS * channels), 1)
    return (column // channels == group).astype(jnp.bfloat16)


def index_kernel(domains, shards, channels, operands, *refs):
    reverse_ref = refs[0]
    sources = refs[1 : 1 + operands]
    send_ref, send_mask_ref, fetch_ref, fetch_mask_ref, local_ref, local_mask_ref, stack_ref = refs[
        1 + operands : 8 + operands
    ]
    targets = refs[8 + operands : 8 + 2 * operands]
    sems = refs[-1]
    copies = [
        pltpu.make_async_copy(source, target, sems.at[at])
        for at, (source, target) in enumerate(zip(sources, targets))
    ] + [
        pltpu.make_async_copy(
            sources[0].at[1],
            stack_ref.at[at * channels : (at + 1) * channels, :],
            sems.at[operands + at],
        )
        for at in range(GROUPS)
    ]
    for copy in copies:
        copy.start()
    rows = reverse_ref.shape[1]
    each = rows // GROUPS
    capacity = rows // domains
    half = capacity // 2
    slots = (domains - 1) * capacity
    own = lax.axis_index("dom")
    reverse = reverse_ref[...]
    holder = reverse // (rows * shards)
    source_row = lax.rem(reverse, rows)
    partner = holder ^ own
    remote = partner != 0
    block = domains - 1 - partner
    member = one_hot((domains, rows), 0, partner)
    before = (
        lax.broadcasted_iota(jnp.int32, (rows, rows), 0)
        < lax.broadcasted_iota(jnp.int32, (rows, rows), 1)
    ).astype(jnp.bfloat16)
    earlier = (as_column(source_row) < source_row).astype(jnp.bfloat16)

    def rank(matrix):
        counts = product(member, matrix) * member.astype(jnp.float32)
        return jnp.sum(counts, axis=0, keepdims=True).astype(jnp.int32)

    place = rank(before)
    part = (place >= half).astype(jnp.int32)
    send_slot = part * (slots // 2) + block * half + place - part * half
    sent = one_hot((slots, rows), 0, jnp.where(remote, send_slot, -1))
    owner = (
        lax.broadcasted_iota(jnp.int32, (rows, GROUPS * channels), 0) // each
        == lax.broadcasted_iota(jnp.int32, (rows, GROUPS * channels), 1) // channels
    ).astype(jnp.bfloat16)
    send_mask_ref[...] = product(sent, owner).astype(jnp.bfloat16)
    folded = sent[:, :each]
    for at in range(1, GROUPS):
        folded = folded + sent[:, at * each : (at + 1) * each]
    send_ref[...] = folded

    far_place = rank(earlier)
    part = (far_place >= half).astype(jnp.int32)
    side = (block >= domains // 2).astype(jnp.int32)
    fetch_row = (block - side * (domains // 2)) * half + far_place - part * half
    fetch_ref[...] = one_hot(
        fetch_ref.shape, 1, as_column(jnp.where(remote, fetch_row, -1))
    )
    fetch_mask_ref[...] = group_mask(as_column(2 * side + part), channels)
    local_group = source_row // each
    local_row = source_row - local_group * each
    local_ref[...] = one_hot(local_ref.shape, 1, as_column(jnp.where(remote, -1, local_row)))
    local_mask_ref[...] = group_mask(as_column(local_group), channels)
    for copy in copies:
        copy.wait()


def picked_rows(chosen, table, mask):
    return product(chosen, table).astype(jnp.bfloat16) * mask


def mix_kernel(shards, *refs):
    source_ref, tiles_ref = refs[:2]
    parts = refs[2 : 2 + shards]
    send_ref, mask_ref, trip_ref = refs[2 + shards : 5 + shards]
    out_refs = refs[5 + shards : -1]
    held_ref = refs[-1]
    blocks, block_len, width = tiles_ref.shape
    count = width // block_len
    lines = held_ref.shape[0] // shards
    me = lax.axis_index("edge")
    for part, at in zip(parts, orders(shards)[0]):
        held_ref[at * lines : (at + 1) * lines, :] = part[...]
    half_blocks = blocks // 2
    channels = trip_ref.shape[1] // GROUPS
    per = blocks // GROUPS

    def mixed(block):
        picks = []
        for tile in range(count):
            source = source_ref[block, tile]
            shard = lax.div(source, blocks)
            within = source - shard * blocks
            upper = (within >= half_blocks).astype(jnp.int32)
            start = (shard ^ me) * lines + (within - upper * half_blocks) * block_len
            rows = held_ref[pl.ds(pl.multiple_of(start, block_len), block_len), :]
            picks.append(jnp.where(upper == 1, rows[:, channels:], rows[:, :channels]))
        return product(tiles_ref[block], jnp.concatenate(picks, axis=0))

    for at in range(per):
        for group in range(0, GROUPS, 2):
            pair = [mixed((group + side) * per + at) for side in range(2)]
            trip_ref[
                at * block_len : (at + 1) * block_len, group * channels : (group + 2) * channels
            ] = jnp.concatenate(pair, axis=1).astype(jnp.bfloat16)
    half_slots = send_ref.shape[0] // 2
    parts = []
    for side in range(2):
        rows = slice(side * half_slots, (side + 1) * half_slots)
        found = product(send_ref[rows, :], trip_ref[...]) * mask_ref[rows, :].astype(jnp.float32)
        both = found[:, : 2 * channels] + found[:, 2 * channels :]
        parts.append(both + pltpu.roll(both, channels, 1))
    lane = lax.broadcasted_iota(jnp.int32, parts[0].shape, 1)
    packed = jnp.where(lane < channels, parts[0], parts[1]).astype(jnp.bfloat16)
    each = half_slots // len(out_refs)
    for at, out_ref in enumerate(out_refs):
        out_ref[...] = packed[at * each : (at + 1) * each, :]


def base_kernel(shards, *refs):
    edges_ref, trip_ref, local_ref, mask_ref, up_ref, stack_ref = refs[:6]
    atoms = refs[6 : 6 + shards]
    out_ref, atoms_ref = refs[6 + shards :]
    count = atoms[0].shape[0]
    for part, at in zip(atoms, orders(shards)[0]):
        atoms_ref[at * count : (at + 1) * count, :] = part[...]
    each = trip_ref.shape[0]
    channels = up_ref.shape[1]
    for group in range(GROUPS):
        rows = slice(group * each, (group + 1) * each)
        picked = picked_rows(local_ref[rows, :], trip_ref[...], mask_ref[rows, :])
        direct = trip_ref[:, group * channels : (group + 1) * channels]
        joined = product(direct, up_ref[0]) + product(picked, stack_ref[...])
        out_ref[rows, :] = edges_ref[rows, :].astype(jnp.float32) + joined * root_half


def state_kernel(partners, *refs):
    base_ref, fetch_ref, mask_ref, stack_ref, residual_ref, message_ref, index_ref = refs[:7]
    arrived = refs[7 : 7 + partners]
    state_ref, sums_ref, slots_ref = refs[7 + partners :]
    each, lanes = arrived[0].shape
    column = (partners + 1) // 2
    for at in range(partners):
        down, right = at % column, at // column
        slots_ref[down * each : (down + 1) * each, right * lanes : (right + 1) * lanes] = arrived[at][...]
    down, right = partners % column, partners // column
    slots_ref[down * each : (down + 1) * each, right * lanes : (right + 1) * lanes] = jnp.zeros(
        (each, lanes), slots_ref.dtype
    )
    part_atoms = sums_ref.shape[0]
    shards = lax.axis_size("edge")
    near = near_atoms(index_ref[1:2, :], part_atoms, shards)
    chosen = (
        lax.broadcasted_iota(jnp.int32, (part_atoms, near.shape[1]), 0) == near
    ).astype(jnp.bfloat16)
    chunks = row_chunks(base_ref.shape[0])
    gathered = None
    for first in range(0, len(chunks), 4):
        group = chunks[first : first + 4]
        picked = [
            picked_rows(fetch_ref[rows, :], slots_ref[...], mask_ref[rows, :]) for rows in group
        ]
        states = [
            (base_ref[rows, :] + product(each, stack_ref[...]) * root_half).astype(jnp.bfloat16)
            for rows, each in zip(group, picked)
        ]
        for layer in range(residual_ref.shape[0]):
            middles = [narrow_silu(product(each, residual_ref[layer, 0])) for each in states]
            branches = [narrow_silu(product(each, residual_ref[layer, 1])) for each in middles]
            states = [
                (
                    (each.astype(jnp.float32) + branch.astype(jnp.float32)) * root_half
                ).astype(jnp.bfloat16)
                for each, branch in zip(states, branches)
            ]
        for rows, each in zip(group, states):
            state_ref[rows, :] = each
            term = product(chosen[:, rows], each)
            gathered = term if gathered is None else gathered + term
    sums_ref[...] = product(gathered.astype(jnp.bfloat16), message_ref[...]).astype(jnp.bfloat16)


def near_atoms(index, part_atoms, shards):
    count = part_atoms // shards
    holder = index // count
    return (holder ^ lax.axis_index("edge")) * count + lax.rem(index, count)


def side_kernel(shards, *refs):
    state_ref, join_ref, index_ref, atoms_ref, weight_ref, out_ref, chosen_ref, fixed_ref, onward_ref = refs
    part_atoms, width = atoms_ref.shape
    for rows in row_chunks(state_ref.shape[0]):
        out_ref[rows, :] = product(state_ref[rows, :], join_ref[2 * width :, :])
    index = near_atoms(index_ref[...], part_atoms, shards)
    for end in range(2):
        column = as_column(index[end : end + 1, :])
        chosen_ref[:, end * part_atoms : (end + 1) * part_atoms] = (
            lax.broadcasted_iota(jnp.int32, (column.shape[0], part_atoms), 1) == column
        ).astype(jnp.bfloat16)
        join = join_ref[end * width : (end + 1) * width, :]
        fixed_ref[end * part_atoms : (end + 1) * part_atoms, :] = product(atoms_ref[...], join)
        onward_ref[end * width : (end + 1) * width, :] = product(weight_ref[1], join).astype(
            jnp.bfloat16
        )


def final_chunks(rows):
    *chunks, last = row_chunks(rows)
    middle = (last.start + last.stop) // 2
    return chunks + [slice(last.start, middle), slice(middle, last.stop)]


def final_kernel(shards, scale, *refs):
    sums = refs[:shards]
    atoms_ref, weight_ref, state_ref, side_ref, chosen_ref, fixed_ref, onward_ref = refs[
        shards : shards + 7
    ]
    edges_hbm, own_hbm, table_ref, edges_ref, own_ref, sems = refs[shards + 7 :]
    part_atoms = atoms_ref.shape[0]
    count = part_atoms // shards
    total = sums[0][...].astype(jnp.float32)
    for by, part in list(zip(orders(shards)[1], sums))[1:]:
        pieces = [part[(at ^ by) * count : ((at ^ by) + 1) * count, :] for at in range(shards)]
        total = total + jnp.concatenate(pieces, axis=0).astype(jnp.float32)
    scaled = (total * scale).astype(jnp.bfloat16)
    middle = silu(product(scaled, weight_ref[0])).astype(jnp.bfloat16)
    width = middle.shape[1]
    for end in range(2):
        rows = slice(end * part_atoms, (end + 1) * part_atoms)
        onward = product(middle, onward_ref[end * width : (end + 1) * width, :])
        table_ref[rows, :] = (fixed_ref[rows, :] + onward).astype(jnp.bfloat16)
    renewed = atoms_ref[:count, :].astype(jnp.float32) + product(middle[:count, :], weight_ref[1])
    own_ref[...] = renewed.astype(jnp.bfloat16)
    own_copy = pltpu.make_async_copy(own_ref, own_hbm, sems.at[0])
    own_copy.start()
    copies = [own_copy]
    chunks = final_chunks(state_ref.shape[0])
    for first in range(0, len(chunks), 2):
        group = chunks[first : first + 2]
        found = [product(chosen_ref[rows, :], table_ref[...]) + side_ref[rows, :] for rows in group]
        for at, (rows, each) in enumerate(zip(group, found)):
            state = state_ref[rows, :].astype(jnp.float32)
            update = narrow_silu(each).astype(jnp.float32)
            edges_ref[rows, :] = ((state + update) * root_half).astype(jnp.bfloat16)
            copies.append(
                pltpu.make_async_copy(
                    edges_ref.at[rows], edges_hbm.at[rows], sems.at[1 + first + at]
                )
            )
            copies[-1].start()
    for copy in copies:
        copy.wait()


def orders(shards):
    if shards == 4:
        return [0, 1, 3, 2], [0, 1, 3, 2]
    return list(range(shards)), list(range(shards))


def from_others(value, order):
    return [value] + [
        lax.ppermute(value, "edge", [(at, at ^ by) for at in range(len(order))])
        for by in order[1:]
    ]


def body(
    edges,
    atoms,
    reverse,
    atom_index,
    tile_source,
    tiles,
    weight_edge,
    weight_down,
    weight_up,
    weight_residual,
    weight_message,
    weight_atom,
    weight_join,
):
    rows, wide = edges.shape
    channels = weight_down.shape[0]
    domains = lax.axis_size("dom")
    shards = lax.axis_size("edge")
    count, atom_wide = atoms.shape
    part_atoms = count * shards
    capacity = rows // domains
    partners = domains - 1
    slots = partners * capacity
    lines = rows // 2
    packed = 2 * channels

    narrow = call(
        narrow_kernel,
        shaped((lines, packed)),
        (edges, weight_edge, weight_down),
        hbm=(0, 1, 2),
        scratch=[
            pltpu.VMEM(edges.shape, jnp.bfloat16),
            pltpu.VMEM(weight_edge.shape, jnp.bfloat16),
            pltpu.VMEM(weight_down.shape, jnp.bfloat16),
            pltpu.SemaphoreType.DMA((3 + len(row_chunks(rows)),)),
        ],
        flops=2 * rows * wide * (wide + channels),
        nbytes=2 * (rows * wide + wide * wide),
    )
    atom_parts = from_others(atoms, orders(shards)[0])
    narrow_parts = from_others(narrow, orders(shards)[0])
    later = (
        weight_up, edges, tiles, weight_residual, weight_message, weight_join, weight_atom, atom_index
    )
    each, grouped = rows // GROUPS, GROUPS * channels
    column = domains // 2 * (capacity // 2)
    send, send_mask, fetch, fetch_mask, local, local_mask, up_stack, *later = call(
        functools.partial(index_kernel, domains, shards, channels, len(later)),
        (
            shaped((slots, each)),
            shaped((slots, grouped)),
            shaped((rows, column)),
            shaped((rows, grouped)),
            shaped((rows, each)),
            shaped((rows, grouped)),
            shaped((grouped, wide)),
        )
        + tuple(shaped(each.shape, each.dtype) for each in later),
        (reverse.reshape(1, rows), *later),
        hbm=range(1, 1 + len(later)),
        scratch=[pltpu.SemaphoreType.DMA((len(later) + GROUPS,))],
        flops=40 * rows * rows,
        nbytes=6 * rows * rows,
    )
    weight_up, edges, tiles, weight_residual, weight_message, weight_join, weight_atom, atom_index = later
    trip_out, *outgoing = call(
        functools.partial(mix_kernel, shards),
        (shaped((each, grouped)),) + (shaped((capacity // 2, packed)),) * partners,
        (tile_source, tiles, *narrow_parts, send, send_mask),
        smem=(0,),
        scratch=[pltpu.VMEM((shards * lines, packed), jnp.bfloat16)],
        flops=2 * rows * rows * channels,
        nbytes=2 * rows * rows,
    )
    arrived = [
        lax.ppermute(block, "dom", [(at, at ^ (partners - place)) for at in range(domains)])
        for place, block in enumerate(outgoing)
    ]
    base, all_atoms = call(
        functools.partial(base_kernel, shards),
        (shaped((rows, wide), jnp.float32), shaped((part_atoms, atom_wide))),
        (edges, trip_out, local, local_mask, weight_up, up_stack, *atom_parts),
        flops=2 * rows * channels * (rows + 2 * wide),
        nbytes=2 * rows * rows + 6 * rows * wide,
    )
    state, sums = call(
        functools.partial(state_kernel, partners),
        (shaped((rows, wide)), shaped((part_atoms, atom_wide))),
        (base, fetch, fetch_mask, up_stack, weight_residual, weight_message, atom_index, *arrived),
        scratch=[pltpu.VMEM((column, grouped), jnp.bfloat16)],
        flops=4 * rows * wide * wide,
        nbytes=8 * rows * wide,
    )
    sums_parts = from_others(sums, orders(shards)[1])
    side, chosen, fixed, onward = call(
        functools.partial(side_kernel, shards),
        (
            shaped((rows, wide), jnp.float32),
            shaped((rows, 2 * part_atoms)),
            shaped((2 * part_atoms, wide), jnp.float32),
            shaped((2 * atom_wide, wide)),
        ),
        (state, weight_join, atom_index, all_atoms, weight_atom),
        flops=2 * rows * wide * wide,
        nbytes=8 * rows * wide,
    )
    return call(
        functools.partial(final_kernel, shards, (rows // count) ** -0.5),
        (shaped((rows, wide), space=pltpu.HBM), shaped((count, atom_wide), space=pltpu.HBM)),
        (*sums_parts, all_atoms, weight_atom, state, side, chosen, fixed, onward),
        scratch=[
            pltpu.VMEM((2 * part_atoms, wide), jnp.bfloat16),
            pltpu.VMEM((rows, wide), jnp.bfloat16),
            pltpu.VMEM((count, atom_wide), jnp.bfloat16),
            pltpu.SemaphoreType.DMA((1 + len(final_chunks(rows)),)),
        ],
        flops=4 * rows * part_atoms * wide,
        nbytes=8 * rows * wide,
    )


def solution(mesh):
    split = P(("dom", "edge"))
    placed = (
        P(("dom", "edge"), None),
        P(("dom", "edge"), None),
        split,
        P(None, ("dom", "edge")),
        P(("dom", "edge"), None),
        P(("dom", "edge"), None, None),
    ) + (P(),) * 7
    return jax.shard_map(
        body,
        mesh=mesh,
        in_specs=placed,
        out_specs=(P(("dom", "edge"), None), P(("dom", "edge"), None)),
        check_vma=False,
    )
```

```python
import functools

import jax
import jax.numpy as jnp
from jax import lax
from jax.experimental import pallas as pl
from jax.experimental.pallas import tpu as pltpu
from jax.sharding import PartitionSpec as P

root_half = 0.7071067811865476
MIB = 1 << 20
CHUNK = 256
LONG = 512
GROUPS = 4


def product(operand, weights):
    return jnp.dot(operand, weights, preferred_element_type=jnp.float32)


def silu(value):
    halved = 0.5 * value
    return halved + halved * jnp.tanh(halved)


def narrow_silu(value):
    halved = value.astype(jnp.bfloat16) * jnp.bfloat16(0.5)
    return halved + halved * jnp.tanh(halved)


def as_column(row):
    wide = jnp.broadcast_to(row.astype(jnp.float32), (8, row.shape[1]))
    return jnp.transpose(wide)[:, :1].astype(jnp.int32)


def row_chunks(rows, step=CHUNK):
    step = min(step, rows)
    return [slice(at, at + step) for at in range(0, rows, step)]


def call(kernel, outs, args, *, smem=(), hbm=(), scratch=(), flops=0, nbytes=0, limit=24):
    def space(at):
        return pltpu.SMEM if at in smem else pltpu.HBM if at in hbm else pltpu.VMEM

    args = [
        pltpu.with_memory_space_constraint(arg, pltpu.HBM) if at in hbm else arg
        for at, arg in enumerate(args)
    ]
    return pl.pallas_call(
        kernel,
        out_shape=outs,
        in_specs=[pl.BlockSpec(memory_space=space(at)) for at in range(len(args))],
        out_specs=jax.tree.map(
            lambda out: pl.BlockSpec(
                memory_space=out.memory_space
                if out.memory_space in (pltpu.HBM, pltpu.SMEM)
                else pltpu.VMEM
            ),
            outs,
        ),
        scratch_shapes=list(scratch),
        compiler_params=pltpu.CompilerParams(vmem_limit_bytes=limit * MIB),
        cost_estimate=pl.CostEstimate(flops=flops, bytes_accessed=nbytes, transcendentals=0),
    )(*args)


def shaped(shape, dtype=jnp.bfloat16, space=pltpu.VMEM):
    return space(tuple(shape), dtype)


def narrow_kernel(edges_hbm, weight_hbm, down_hbm, out_ref, edges_ref, weight_ref, down_ref, sems):
    half = edges_hbm.shape[0] // 2
    cut = weight_hbm.shape[0] // 2
    copies = [pltpu.make_async_copy(down_hbm, down_ref, sems.at[0])]
    for at, rows in enumerate((slice(0, cut), slice(cut, 2 * cut))):
        copies.append(pltpu.make_async_copy(weight_hbm.at[rows], weight_ref.at[rows], sems.at[1 + at]))
    pieces = row_chunks(2 * half)
    for at, rows in enumerate(pieces):
        copies.append(pltpu.make_async_copy(edges_hbm.at[rows], edges_ref.at[rows], sems.at[3 + at]))
    for copy in copies[1:] + copies[:1]:
        copy.start()
    for copy in copies:
        copy.wait()
    hidden = [
        narrow_silu(product(edges_ref[side * half : (side + 1) * half, :], weight_ref[...]))
        for side in range(2)
    ]
    sides = [
        lax.dot_general(
            each, down_ref[...], (((1,), (1,)), ((), ())), preferred_element_type=jnp.float32
        )
        for each in hidden
    ]
    out_ref[...] = silu(jnp.concatenate(sides, axis=1)).astype(jnp.bfloat16)


def one_hot(shape, axis, chosen):
    return (lax.broadcasted_iota(jnp.int32, shape, axis) == chosen).astype(jnp.bfloat16)


def group_mask(group, channels):
    column = lax.broadcasted_iota(jnp.int32, (group.shape[0], GROUPS * channels), 1)
    return (column // channels == group).astype(jnp.bfloat16)


def index_kernel(domains, shards, channels, operands, *refs):
    reverse_ref, source_ref = refs[:2]
    place_ref = refs[-2]
    refs = refs[1:]
    blocks, tile_count = source_ref.shape
    lines, block_len = reverse_ref.shape[1] // 2, reverse_ref.shape[1] // blocks
    for at in range(blocks):
        for tile in range(tile_count):
            source = source_ref[at, tile]
            shard = lax.div(source, blocks)
            within = source - shard * blocks
            upper = (within >= blocks // 2).astype(jnp.int32)
            start = (shard ^ lax.axis_index("edge")) * lines
            start = start + (within - upper * (blocks // 2)) * block_len
            place_ref[at, tile] = 2 * start + upper
    sources = refs[1 : 1 + operands]
    send_ref, send_mask_ref, fetch_ref, fetch_mask_ref, local_ref, local_mask_ref, stack_ref = refs[
        1 + operands : 8 + operands
    ]
    targets = refs[8 + operands : 8 + 2 * operands]
    sems = refs[-1]
    copies = [
        pltpu.make_async_copy(source, target, sems.at[at])
        for at, (source, target) in enumerate(zip(sources, targets))
    ] + [
        pltpu.make_async_copy(
            sources[0].at[1],
            stack_ref.at[at * channels : (at + 1) * channels, :],
            sems.at[operands + at],
        )
        for at in range(GROUPS)
    ]
    for copy in copies:
        copy.start()
    rows = reverse_ref.shape[1]
    each = rows // GROUPS
    capacity = rows // domains
    half = capacity // 2
    slots = (domains - 1) * capacity
    own = lax.axis_index("dom")
    reverse = reverse_ref[...]
    holder = reverse // (rows * shards)
    source_row = lax.rem(reverse, rows)
    partner = holder ^ own
    remote = partner != 0
    block = domains - 1 - partner
    member = one_hot((domains, rows), 0, partner)
    before = (
        lax.broadcasted_iota(jnp.int32, (rows, rows), 0)
        < lax.broadcasted_iota(jnp.int32, (rows, rows), 1)
    ).astype(jnp.bfloat16)
    earlier = (as_column(source_row) < source_row).astype(jnp.bfloat16)

    def rank(matrix):
        counts = product(member, matrix) * member.astype(jnp.float32)
        return jnp.sum(counts, axis=0, keepdims=True).astype(jnp.int32)

    place = rank(before)
    part = (place >= half).astype(jnp.int32)
    send_slot = part * (slots // 2) + block * half + place - part * half
    sent = one_hot((slots, rows), 0, jnp.where(remote, send_slot, -1))
    owner = (
        lax.broadcasted_iota(jnp.int32, (rows, GROUPS * channels), 0) // each
        == lax.broadcasted_iota(jnp.int32, (rows, GROUPS * channels), 1) // channels
    ).astype(jnp.bfloat16)
    send_mask_ref[...] = product(sent, owner).astype(jnp.bfloat16)
    folded = sent[:, :each]
    for at in range(1, GROUPS):
        folded = folded + sent[:, at * each : (at + 1) * each]
    send_ref[...] = folded

    far_place = rank(earlier)
    part = (far_place >= half).astype(jnp.int32)
    side = (block >= domains // 2).astype(jnp.int32)
    fetch_row = (block - side * (domains // 2)) * half + far_place - part * half
    fetch_ref[...] = one_hot(
        fetch_ref.shape, 1, as_column(jnp.where(remote, fetch_row, -1))
    )
    fetch_mask_ref[...] = group_mask(as_column(2 * side + part), channels)
    local_group = source_row // each
    local_row = source_row - local_group * each
    local_ref[...] = one_hot(local_ref.shape, 1, as_column(jnp.where(remote, -1, local_row)))
    local_mask_ref[...] = group_mask(as_column(local_group), channels)
    for copy in copies:
        copy.wait()


def picked_rows(chosen, table, mask):
    return product(chosen, table).astype(jnp.bfloat16) * mask


def mix_kernel(shards, *refs):
    source_ref, tiles_ref = refs[:2]
    parts = refs[2 : 2 + shards]
    send_ref, mask_ref, trip_ref = refs[2 + shards : 5 + shards]
    out_refs = refs[5 + shards : -1]
    held_ref = refs[-1]
    blocks, block_len, width = tiles_ref.shape
    count = width // block_len
    lines = held_ref.shape[0] // shards
    me = lax.axis_index("edge")
    for part, at in zip(parts, orders(shards)[0]):
        held_ref[at * lines : (at + 1) * lines, :] = part[...]
    channels = trip_ref.shape[1] // GROUPS
    per = blocks // GROUPS

    def mixed(block):
        picks = []
        for tile in range(count):
            place = source_ref[block, tile]
            start = lax.shift_right_logical(place, 1)
            upper = lax.bitwise_and(place, 1)
            rows = held_ref[pl.ds(pl.multiple_of(start, block_len), block_len), :]
            picks.append(jnp.where(upper == 1, rows[:, channels:], rows[:, :channels]))
        return product(tiles_ref[block], jnp.concatenate(picks, axis=0))

    for at in range(per):
        for group in range(0, GROUPS, 2):
            pair = [mixed((group + side) * per + at) for side in range(2)]
            trip_ref[
                at * block_len : (at + 1) * block_len, group * channels : (group + 2) * channels
            ] = jnp.concatenate(pair, axis=1).astype(jnp.bfloat16)
    half_slots = send_ref.shape[0] // 2
    parts = []
    for side in range(2):
        rows = slice(side * half_slots, (side + 1) * half_slots)
        found = product(send_ref[rows, :], trip_ref[...]) * mask_ref[rows, :].astype(jnp.float32)
        both = found[:, : 2 * channels] + found[:, 2 * channels :]
        parts.append(both + pltpu.roll(both, channels, 1))
    lane = lax.broadcasted_iota(jnp.int32, parts[0].shape, 1)
    packed = jnp.where(lane < channels, parts[0], parts[1]).astype(jnp.bfloat16)
    each = half_slots // len(out_refs)
    for at, out_ref in enumerate(out_refs):
        out_ref[...] = packed[at * each : (at + 1) * each, :]


def base_kernel(shards, *refs):
    edges_ref, trip_ref, local_ref, mask_ref, up_ref, stack_ref = refs[:6]
    atoms = refs[6 : 6 + shards]
    out_ref, atoms_ref = refs[6 + shards :]
    count = atoms[0].shape[0]
    for part, at in zip(atoms, orders(shards)[0]):
        atoms_ref[at * count : (at + 1) * count, :] = part[...]
    each = trip_ref.shape[0]
    channels = up_ref.shape[1]
    for group in range(GROUPS):
        rows = slice(group * each, (group + 1) * each)
        picked = picked_rows(local_ref[rows, :], trip_ref[...], mask_ref[rows, :])
        direct = trip_ref[:, group * channels : (group + 1) * channels]
        joined = product(direct, up_ref[0]) + product(picked, stack_ref[...])
        out_ref[rows, :] = edges_ref[rows, :].astype(jnp.float32) + joined * root_half


def state_kernel(partners, *refs):
    base_ref, fetch_ref, mask_ref, stack_ref, residual_ref, message_ref, index_ref = refs[:7]
    arrived = refs[7 : 7 + partners]
    state_ref, sums_ref, slots_ref = refs[7 + partners :]
    each, lanes = arrived[0].shape
    column = (partners + 1) // 2
    for at in range(partners):
        down, right = at % column, at // column
        slots_ref[down * each : (down + 1) * each, right * lanes : (right + 1) * lanes] = arrived[at][...]
    down, right = partners % column, partners // column
    slots_ref[down * each : (down + 1) * each, right * lanes : (right + 1) * lanes] = jnp.zeros(
        (each, lanes), slots_ref.dtype
    )
    part_atoms = sums_ref.shape[0]
    shards = lax.axis_size("edge")
    near = near_atoms(index_ref[1:2, :], part_atoms, shards)
    chosen = (
        lax.broadcasted_iota(jnp.int32, (part_atoms, near.shape[1]), 0) == near
    ).astype(jnp.bfloat16)
    chunks = row_chunks(base_ref.shape[0], LONG)
    gathered = None
    for first in range(0, len(chunks), 2):
        group = chunks[first : first + 2]
        picked = [
            picked_rows(fetch_ref[rows, :], slots_ref[...], mask_ref[rows, :]) for rows in group
        ]
        states = [
            (base_ref[rows, :] + product(each, stack_ref[...]) * root_half).astype(jnp.bfloat16)
            for rows, each in zip(group, picked)
        ]
        for layer in range(residual_ref.shape[0]):
            middles = [narrow_silu(product(each, residual_ref[layer, 0])) for each in states]
            branches = [narrow_silu(product(each, residual_ref[layer, 1])) for each in middles]
            states = [
                (
                    (each.astype(jnp.float32) + branch.astype(jnp.float32)) * root_half
                ).astype(jnp.bfloat16)
                for each, branch in zip(states, branches)
            ]
        for rows, each in zip(group, states):
            state_ref[rows, :] = each
            term = product(chosen[:, rows], each)
            gathered = term if gathered is None else gathered + term
    sums_ref[...] = product(gathered.astype(jnp.bfloat16), message_ref[...]).astype(jnp.bfloat16)


def near_atoms(index, part_atoms, shards):
    count = part_atoms // shards
    holder = index // count
    return (holder ^ lax.axis_index("edge")) * count + lax.rem(index, count)


def side_kernel(shards, *refs):
    state_ref, join_ref, index_ref, atoms_ref, weight_ref, out_ref, chosen_ref, fixed_ref, onward_ref = refs
    part_atoms, width = atoms_ref.shape
    for rows in row_chunks(state_ref.shape[0]):
        out_ref[rows, :] = product(state_ref[rows, :], join_ref[2 * width :, :])
    index = near_atoms(index_ref[...], part_atoms, shards)
    for end in range(2):
        column = as_column(index[end : end + 1, :])
        chosen_ref[:, end * part_atoms : (end + 1) * part_atoms] = (
            lax.broadcasted_iota(jnp.int32, (column.shape[0], part_atoms), 1) == column
        ).astype(jnp.bfloat16)
        join = join_ref[end * width : (end + 1) * width, :]
        fixed_ref[end * part_atoms : (end + 1) * part_atoms, :] = product(atoms_ref[...], join)
        onward_ref[end * width : (end + 1) * width, :] = product(weight_ref[1], join).astype(
            jnp.bfloat16
        )


def final_kernel(shards, scale, *refs):
    sums = refs[:shards]
    atoms_ref, weight_ref, state_ref, side_ref, chosen_ref, fixed_ref, onward_ref = refs[
        shards : shards + 7
    ]
    edges_hbm, own_hbm, table_ref, edges_ref, own_ref, sems = refs[shards + 7 :]
    part_atoms = atoms_ref.shape[0]
    count = part_atoms // shards
    total = sums[0][...].astype(jnp.float32)
    for by, part in list(zip(orders(shards)[1], sums))[1:]:
        pieces = [part[(at ^ by) * count : ((at ^ by) + 1) * count, :] for at in range(shards)]
        total = total + jnp.concatenate(pieces, axis=0).astype(jnp.float32)
    scaled = (total * scale).astype(jnp.bfloat16)
    middle = silu(product(scaled, weight_ref[0])).astype(jnp.bfloat16)
    width = middle.shape[1]
    for end in range(2):
        rows = slice(end * part_atoms, (end + 1) * part_atoms)
        onward = product(middle, onward_ref[end * width : (end + 1) * width, :])
        table_ref[rows, :] = (fixed_ref[rows, :] + onward).astype(jnp.bfloat16)
    renewed = atoms_ref[:count, :].astype(jnp.float32) + product(middle[:count, :], weight_ref[1])
    own_ref[...] = renewed.astype(jnp.bfloat16)
    own_copy = pltpu.make_async_copy(own_ref, own_hbm, sems.at[0])
    own_copy.start()
    copies = [own_copy]
    chunks = row_chunks(state_ref.shape[0])
    for first in range(0, len(chunks), 2):
        group = chunks[first : first + 2]
        found = [product(chosen_ref[rows, :], table_ref[...]) + side_ref[rows, :] for rows in group]
        for at, (rows, each) in enumerate(zip(group, found)):
            state = state_ref[rows, :].astype(jnp.float32)
            update = narrow_silu(each).astype(jnp.float32)
            edges_ref[rows, :] = ((state + update) * root_half).astype(jnp.bfloat16)
            copies.append(
                pltpu.make_async_copy(
                    edges_ref.at[rows], edges_hbm.at[rows], sems.at[1 + first + at]
                )
            )
            copies[-1].start()
    for copy in copies:
        copy.wait()


def orders(shards):
    if shards == 4:
        return [0, 1, 3, 2], [0, 1, 3, 2]
    return list(range(shards)), list(range(shards))


def from_others(value, order):
    return [value] + [
        lax.ppermute(value, "edge", [(at, at ^ by) for at in range(len(order))])
        for by in order[1:]
    ]


def body(
    edges,
    atoms,
    reverse,
    atom_index,
    tile_source,
    tiles,
    weight_edge,
    weight_down,
    weight_up,
    weight_residual,
    weight_message,
    weight_atom,
    weight_join,
):
    rows, wide = edges.shape
    channels = weight_down.shape[0]
    domains = lax.axis_size("dom")
    shards = lax.axis_size("edge")
    count, atom_wide = atoms.shape
    part_atoms = count * shards
    capacity = rows // domains
    partners = domains - 1
    slots = partners * capacity
    lines = rows // 2
    packed = 2 * channels

    narrow = call(
        narrow_kernel,
        shaped((lines, packed)),
        (edges, weight_edge, weight_down),
        hbm=(0, 1, 2),
        scratch=[
            pltpu.VMEM(edges.shape, jnp.bfloat16),
            pltpu.VMEM(weight_edge.shape, jnp.bfloat16),
            pltpu.VMEM(weight_down.shape, jnp.bfloat16),
            pltpu.SemaphoreType.DMA((3 + len(row_chunks(rows)),)),
        ],
        flops=2 * rows * wide * (wide + channels),
        nbytes=2 * (rows * wide + wide * wide),
    )
    atom_parts = from_others(atoms, orders(shards)[0])
    narrow_parts = from_others(narrow, orders(shards)[0])
    later = (
        weight_up, edges, tiles, weight_residual, weight_message, weight_join, weight_atom, atom_index
    )
    each, grouped = rows // GROUPS, GROUPS * channels
    column = domains // 2 * (capacity // 2)
    send, send_mask, fetch, fetch_mask, local, local_mask, up_stack, *later, places = call(
        functools.partial(index_kernel, domains, shards, channels, len(later)),
        (
            shaped((slots, each)),
            shaped((slots, grouped)),
            shaped((rows, column)),
            shaped((rows, grouped)),
            shaped((rows, each)),
            shaped((rows, grouped)),
            shaped((grouped, wide)),
        )
        + tuple(shaped(each.shape, each.dtype) for each in later)
        + (shaped(tile_source.shape, jnp.int32, pltpu.SMEM),),
        (reverse.reshape(1, rows), tile_source, *later),
        smem=(1,),
        hbm=range(2, 2 + len(later)),
        scratch=[pltpu.SemaphoreType.DMA((len(later) + GROUPS,))],
        flops=40 * rows * rows,
        nbytes=6 * rows * rows,
    )
    weight_up, edges, tiles, weight_residual, weight_message, weight_join, weight_atom, atom_index = later
    trip_out, *outgoing = call(
        functools.partial(mix_kernel, shards),
        (shaped((each, grouped)),) + (shaped((capacity // 2, packed)),) * partners,
        (places, tiles, *narrow_parts, send, send_mask),
        smem=(0,),
        scratch=[pltpu.VMEM((shards * lines, packed), jnp.bfloat16)],
        flops=2 * rows * rows * channels,
        nbytes=2 * rows * rows,
    )
    arrived = [
        lax.ppermute(block, "dom", [(at, at ^ (partners - place)) for at in range(domains)])
        for place, block in enumerate(outgoing)
    ]
    base, all_atoms = call(
        functools.partial(base_kernel, shards),
        (shaped((rows, wide), jnp.float32), shaped((part_atoms, atom_wide))),
        (edges, trip_out, local, local_mask, weight_up, up_stack, *atom_parts),
        flops=2 * rows * channels * (rows + 2 * wide),
        nbytes=2 * rows * rows + 6 * rows * wide,
    )
    state, sums = call(
        functools.partial(state_kernel, partners),
        (shaped((rows, wide)), shaped((part_atoms, atom_wide))),
        (base, fetch, fetch_mask, up_stack, weight_residual, weight_message, atom_index, *arrived),
        scratch=[pltpu.VMEM((column, grouped), jnp.bfloat16)],
        flops=4 * rows * wide * wide,
        nbytes=8 * rows * wide,
    )
    sums_parts = from_others(sums, orders(shards)[1])
    side, chosen, fixed, onward = call(
        functools.partial(side_kernel, shards),
        (
            shaped((rows, wide), jnp.float32),
            shaped((rows, 2 * part_atoms)),
            shaped((2 * part_atoms, wide), jnp.float32),
            shaped((2 * atom_wide, wide)),
        ),
        (state, weight_join, atom_index, all_atoms, weight_atom),
        flops=2 * rows * wide * wide,
        nbytes=8 * rows * wide,
    )
    return call(
        functools.partial(final_kernel, shards, (rows // count) ** -0.5),
        (shaped((rows, wide), space=pltpu.HBM), shaped((count, atom_wide), space=pltpu.HBM)),
        (*sums_parts, all_atoms, weight_atom, state, side, chosen, fixed, onward),
        scratch=[
            pltpu.VMEM((2 * part_atoms, wide), jnp.bfloat16),
            pltpu.VMEM((rows, wide), jnp.bfloat16),
            pltpu.VMEM((count, atom_wide), jnp.bfloat16),
            pltpu.SemaphoreType.DMA((1 + len(row_chunks(rows)),)),
        ],
        flops=4 * rows * part_atoms * wide,
        nbytes=8 * rows * wide,
    )


def solution(mesh):
    split = P(("dom", "edge"))
    placed = (
        P(("dom", "edge"), None),
        P(("dom", "edge"), None),
        split,
        P(None, ("dom", "edge")),
        P(("dom", "edge"), None),
        P(("dom", "edge"), None, None),
    ) + (P(),) * 7
    return jax.shard_map(
        body,
        mesh=mesh,
        in_specs=placed,
        out_specs=(P(("dom", "edge"), None), P(("dom", "edge"), None)),
        check_vma=False,
    )
```
